256 devices in a mesh: gx: 16 (over z, x_hi), gy: 8 (over y, x_lo), gz: 2 (over core).
Axes of the slice: x: 4 (x_hi: 2, x_lo: 2; x = x_hi * 2 + x_lo), y: 4, z: 8, core: 2. Of those that a mesh axis runs over, the one named last changes fastest.
Arguments:
- state: float32 [16, 32, 32, 8, 128], P(None, 'gx', 'gy', 'gz'), may hold values from -3 to 3.98, as said below
- bin_count: int32 [32, 32, 8], P('gx', 'gy', 'gz'), may hold values from 0 to 128
- departing: float32 [16, 16, 8, 2, 6, 4, 128], P(None, 'gx', 'gy', 'gz'), may hold values from -3 to 3.98, as said below
- depart_count: int32 [16, 8, 2, 6, 4], P('gx', 'gy', 'gz'), may hold values from 0 to 128, as said below
- depart_block: int32 [16, 8, 2, 6, 4], P('gx', 'gy', 'gz'), may hold values from 0 to 31, as said below
- cut_cell: int32 [16, 8, 2, 512], P('gx', 'gy', 'gz'), may hold values from 0 to 2047
- quad_count: int32 [16, 8, 2, 512], P('gx', 'gy', 'gz'), may hold values from 0 to 8
- wall_id: int32 [16, 8, 2, 512], P('gx', 'gy', 'gz'), may hold values from 0 to 3
- cut_level: float32 [16, 8, 2, 512], P('gx', 'gy', 'gz'), may hold values from -1.5 to 1.5
- wall_normal: float32 [4, 3], replicated, may hold values from -2 to 2
- wall_friction: float32 [4], replicated, may hold values from 0.2 to 1
Outputs:
- moved: float32 [16, 32, 32, 8, 128], P(None, 'gx', 'gy', 'gz')
- arrived: float32 [16, 16, 8, 2, 6, 4, 128], P(None, 'gx', 'gy', 'gz')
The draws below stay inside these ranges and needn't reach their ends.
Inputs may be any that keep to these rules, and one draw needn't show every extreme that they name: `state`: rows 0 to 2 lie in [0.02, 3.98], row 15 in [0.85, 1.1]. `departing`: rows 0 to 2 lie in [0.02, 3.98], row 15 in [0.85, 1.1]. `depart_count`: zero for bins whose direction leaves the domain across a y or z face. `depart_block`: flat index (x * 4 + y) * 4 + z of a block of the receiving brick on the face the bin enters: x = 0 for +x, x = 1 for -x, likewise y for +y and -y and z for +z and -z. `cut_cell`: flat owned cell index (x * 4 * 4 + y) * 4 * 4 + z of the brick; cells may repeat.
All inputs are finite; a program needn't handle non-finite values.
Results may differ from the reference program's by a relative error of at most 0.0003.
Values sent between devices are 32-bit elements; how exact they have to be, the bound alone decides.
No kernel may reach another device: no remote copies, remote signals or barrier semaphores. Data moves between devices by JAX's collectives and lax.ppermute only.
A program may use at most 128 MiB of HBM per device.

```python
import jax
import jax.numpy as jnp
import numpy as np
from jax import lax

KX = 2
KY = 4
KZ = 4
MB = 4
CUT = 512
SLOTS = 128
CH = 16
DIRS = 6
QMAX = 8
NWALL = 4
NBX = 32
NBY = 32
NBZ = 8
N_GX = 16
N_GY = 8
N_GZ = 2


def particle_rows(key, shape):
    keys = jax.random.split(key, 4)
    tail = shape[1:]
    position = jax.random.uniform(keys[0], (3,) + tail, jnp.float32, 0.02, 3.98)
    bell = jnp.clip(jax.random.normal(keys[2], (12,) + tail, jnp.float32), -3.0, 3.0)
    mixed = bell
    velocity = mixed[0:3]
    affine = 0.3 * mixed[3:12]
    ratio = jax.random.uniform(keys[3], (1,) + tail, jnp.float32, 0.85, 1.1)
    return jnp.concatenate([position, velocity, affine, ratio], axis=0)


def draw_state(key, part):
    key = jax.random.fold_in(key, 11)
    shape = (CH, NBX, NBY, NBZ, SLOTS)
    return particle_rows(key, shape)


def draw_departing(key, part):
    key = jax.random.fold_in(key, 12)
    shape = (CH, N_GX, N_GY, N_GZ, DIRS, MB, SLOTS)
    return particle_rows(key, shape)


def draw_depart_count(key, part):
    key = jax.random.fold_in(key, 13)
    shape = (N_GX, N_GY, N_GZ, DIRS, MB)
    counts = jax.random.randint(key, shape, 1, SLOTS + 1)
    second = lax.broadcasted_iota(jnp.int32, shape, 1)
    third = lax.broadcasted_iota(jnp.int32, shape, 2)
    direction = lax.broadcasted_iota(jnp.int32, shape, 3)
    member = lax.broadcasted_iota(jnp.int32, shape, 4)
    counts = jnp.where((direction == 0) & (member == 0), SLOTS, counts)
    leaving = (direction == 2) & (second == N_GY - 1) | (direction == 3) & (second == 0)
    leaving = leaving | (direction == 4) & (third == N_GZ - 1) | (direction == 5) & (third == 0)
    return jnp.where(leaving, 0, counts).astype(jnp.int32)


def draw_depart_block(key, part):
    key = jax.random.fold_in(key, 14)
    shape = (N_GX, N_GY, N_GZ, DIRS, MB)
    keys = jax.random.split(key, 3)
    place_first = jax.random.randint(keys[0], shape, 0, KX)
    place_second = jax.random.randint(keys[1], shape, 0, KY)
    place_third = jax.random.randint(keys[2], shape, 0, KZ)
    direction = lax.broadcasted_iota(jnp.int32, shape, 3)
    member = lax.broadcasted_iota(jnp.int32, shape, 4)
    place_second = jnp.where((direction == 0) & (member == 0), 0, place_second)
    place_third = jnp.where((direction == 0) & (member == 0), 0, place_third)
    place_second = jnp.where((direction == 1) & (member == 0), KY - 1, place_second)
    place_third = jnp.where((direction == 1) & (member == 0), KZ - 1, place_third)
    place_first = jnp.where(direction == 0, 0, jnp.where(direction == 1, KX - 1, place_first))
    place_second = jnp.where(direction == 2, 0, jnp.where(direction == 3, KY - 1, place_second))
    place_third = jnp.where(direction == 4, 0, jnp.where(direction == 5, KZ - 1, place_third))
    return ((place_first * KY + place_second) * KZ + place_third).astype(jnp.int32)


def with_ends(drawn, own_key, least, top_value):
    longest = drawn.shape.index(max(drawn.shape))
    spots = []
    for shift in (0, 1):
        where = [jax.random.randint(jax.random.fold_in(own_key, axis), (), 0, length) for axis, length in enumerate(drawn.shape)]
        where[longest] = (where[longest] + shift) % drawn.shape[longest]
        spots.append(tuple(where))
    return drawn.at[spots[0]].set(least).at[spots[1]].set(top_value)


def level_of(rng, dims, shards, low, top_value):
    def one(dim, blocks):
        steps = jax.random.uniform(jax.random.fold_in(jax.random.fold_in(rng, 6), dim), (blocks,), jnp.float32, low / len(shards), top_value / len(shards))
        return jnp.repeat(jnp.exp(steps), dims[dim] // blocks).reshape((-1,) + (1,) * (len(dims) - dim - 1))

    level = one(*shards[0])
    for cut in shards[1:]:
        level = level * one(*cut)
    return level


def bell_draw(own_key, dims, scale, limit, kind=jnp.bfloat16):
    drawn = jax.random.normal(own_key, dims, jnp.float32) * scale
    return jnp.minimum(jnp.maximum(drawn, -limit), limit).astype(kind)


def setup_inputs(seed: int = 0) -> dict:
    key_list = jax.random.split(jax.random.key(seed), 12)
    return {
        "state": draw_state(jax.random.fold_in(key_list[11], 71), 0),
        "bin_count": with_ends(jax.random.randint(key_list[1], (NBX, NBY, NBZ), 0, SLOTS + 1), jax.random.fold_in(key_list[1], 1), 0, SLOTS).astype(jnp.int32),
        "departing": draw_departing(jax.random.fold_in(key_list[11], 71), 0),
        "depart_count": draw_depart_count(jax.random.fold_in(key_list[11], 71), 0),
        "depart_block": draw_depart_block(jax.random.fold_in(key_list[11], 71), 0),
        "cut_cell": with_ends(jax.random.randint(key_list[5], (N_GX, N_GY, N_GZ, CUT), 0, 64 * KX * KY * KZ), jax.random.fold_in(key_list[5], 1), 0, (64 * KX * KY * KZ) - 1).astype(jnp.int32),
        "quad_count": with_ends(jax.random.randint(key_list[6], (N_GX, N_GY, N_GZ, CUT), 0, QMAX + 1), jax.random.fold_in(key_list[6], 1), 0, QMAX).astype(jnp.int32),
        "wall_id": with_ends(jax.random.randint(key_list[7], (N_GX, N_GY, N_GZ, CUT), 0, NWALL), jax.random.fold_in(key_list[7], 1), 0, NWALL - 1).astype(jnp.int32),
        "cut_level": jnp.clip(jax.random.uniform(key_list[8], (N_GX, N_GY, N_GZ, CUT), jnp.float32, -1.5, 1.5) * level_of(key_list[8], (N_GX, N_GY, N_GZ, CUT), ((0, 16), (1, 8), (2, 2)), -0.4, 0.0), -1.5, 1.5),
        "wall_normal": bell_draw(key_list[9], (NWALL, 3), 0.6, 2.0, jnp.float32),
        "wall_friction": jnp.clip(jax.random.uniform(key_list[10], (NWALL,), jnp.float32, 0.2, 1.0), 0.2, 1.0),
    }


time_step = 0.1
stiffness = 4.0
volume = 1.0
particle_mass = 1.0
gravity = 2.0
flip_ratio = 0.95
mass_floor = 0.25
highest = lax.Precision.HIGHEST
quad_points = np.array([[0.5, 0.5, 0.5], [0.2, 0.7, 0.35], [0.8, 0.3, 0.65], [0.35, 0.15, 0.85], [0.65, 0.85, 0.15], [0.1, 0.45, 0.55], [0.9, 0.55, 0.45], [0.45, 0.9, 0.75]], dtype=np.float32)
corner_bits = np.array([[first, second, third] for first in (0, 1) for second in (0, 1) for third in (0, 1)], dtype=np.int32)


def spline(coord):
    offsets = jnp.arange(8, dtype=jnp.float32) - 2.0
    distance = jnp.abs(coord[:, None, :] - offsets[None, :, None])
    inner = 0.75 - distance * distance
    outer = 0.5 * jnp.square(jnp.maximum(1.5 - distance, 0.0))
    return jnp.where(distance < 0.5, inner, outer)


def deposit(state, valid):
    blocks = state.shape[1]
    slots = state.shape[2]
    position = state[0:3]
    velocity = state[3:6]
    affine = state[6:15]
    ratio = state[15]
    pressure = time_step * 4.0 * stiffness * volume * jnp.maximum(1.0 - ratio, 0.0)
    spread = []
    for row in range(3):
        for column in range(3):
            entry = particle_mass * affine[3 * row + column]
            if row == column:
                entry = entry + pressure
            spread.append(entry)
    linear = []
    for row in range(3):
        linear.append(particle_mass * velocity[row] - spread[3 * row] * position[0] - spread[3 * row + 1] * position[1] - spread[3 * row + 2] * position[2])
    rows = jnp.stack([jnp.full_like(ratio, particle_mass)] + linear + spread) * valid[None]
    weight_first = spline(position[0])
    weight_second = spline(position[1])
    weight_third = spline(position[2])
    plane = (weight_first[:, :, None, :] * weight_second[:, None, :, :]).reshape(blocks, 64, slots)
    lifted = rows[:, :, None, :] * weight_third[None]
    moments = jnp.einsum("cbks,bas->bcak", lifted, plane, precision=highest)
    offsets = jnp.arange(8, dtype=jnp.float32) - 2.0
    node_first = jnp.repeat(offsets, 8)[:, None]
    node_second = jnp.tile(offsets, 8)[:, None]
    node_third = offsets[None, :]
    momentum = []
    for row in range(3):
        momentum.append(moments[:, 1 + row] + moments[:, 4 + 3 * row] * node_first + moments[:, 5 + 3 * row] * node_second + moments[:, 6 + 3 * row] * node_third)
    return jnp.stack([moments[:, 0]] + momentum, axis=1).reshape(blocks, 4, 512)


def collect(foot, state, valid):
    blocks = state.shape[1]
    slots = state.shape[2]
    position = state[0:3]
    velocity = state[3:6]
    ratio = state[15]
    offsets = jnp.arange(8, dtype=jnp.float32) - 2.0
    weight_first = spline(position[0])
    weight_second = spline(position[1])
    weight_third = spline(position[2])
    lever_first = weight_first * (offsets[None, :, None] - position[0][:, None, :])
    lever_second = weight_second * (offsets[None, :, None] - position[1][:, None, :])
    lever_third = weight_third * (offsets[None, :, None] - position[2][:, None, :])
    grid = foot.reshape(blocks, 6, 64, 8)
    plane = (weight_first[:, :, None, :] * weight_second[:, None, :, :]).reshape(blocks, 64, slots)
    plane_first = (lever_first[:, :, None, :] * weight_second[:, None, :, :]).reshape(blocks, 64, slots)
    plane_second = (weight_first[:, :, None, :] * lever_second[:, None, :, :]).reshape(blocks, 64, slots)
    base = jnp.einsum("bcak,bas->bcks", grid, plane, precision=highest)
    along_first = jnp.einsum("bcak,bas->bcks", grid[:, 0:3], plane_first, precision=highest)
    along_second = jnp.einsum("bcak,bas->bcks", grid[:, 0:3], plane_second, precision=highest)
    picked = jnp.sum(base * weight_third[:, None], axis=2)
    moment_first = jnp.moveaxis(jnp.sum(along_first * weight_third[:, None], axis=2), 1, 0)
    moment_second = jnp.moveaxis(jnp.sum(along_second * weight_third[:, None], axis=2), 1, 0)
    moment_third = jnp.moveaxis(jnp.sum(base[:, 0:3] * lever_third[:, None], axis=2), 1, 0)
    gathered = [moment_first, moment_second, moment_third]
    transfer = jnp.moveaxis(picked[:, 0:3], 1, 0)
    earlier = jnp.moveaxis(picked[:, 3:6], 1, 0)
    affine = []
    for row in range(3):
        for column in range(3):
            affine.append(4.0 * gathered[column][row])
    new_position = position + time_step * transfer
    new_velocity = flip_ratio * (velocity + transfer - earlier) + (1.0 - flip_ratio) * transfer
    new_ratio = ratio * (1.0 + time_step * (affine[0] + affine[4] + affine[8]))
    result = jnp.concatenate([new_position, new_velocity, jnp.stack(affine), new_ratio[None]], axis=0)
    return result * valid[None]


def advance(sums):
    mass = sums[0]
    previous = sums[1:4] / jnp.maximum(mass, mass_floor)[None]
    velocity = jnp.stack([previous[0], previous[1], previous[2] - time_step * gravity])
    normal = sums[4:7]
    scale = 1.0 + jnp.sum(normal * normal, axis=0)
    inward = jnp.minimum(jnp.sum(velocity * normal, axis=0), 0.0)
    velocity = velocity - (inward / scale)[None] * normal
    along = jnp.sum(velocity * normal, axis=0) / scale
    tangent = velocity - along[None] * normal
    velocity = velocity - (1.0 - jnp.exp(-sums[7]))[None] * tangent
    return jnp.concatenate([velocity, previous], axis=0)


def fold(grid, axis):
    shape = grid.shape
    split = grid.reshape(shape[:axis] + (shape[axis], 2, 4) + shape[axis + 2:])
    lower = lax.index_in_dim(split, 0, axis + 1, keepdims=False)
    upper = lax.index_in_dim(split, 1, axis + 1, keepdims=False)
    widths_lower = [(0, 0)] * lower.ndim
    widths_upper = [(0, 0)] * lower.ndim
    widths_lower[axis] = (0, 1)
    widths_upper[axis] = (1, 0)
    total = jnp.pad(lower, widths_lower) + jnp.pad(upper, widths_upper)
    return total.reshape(shape[:axis] + ((shape[axis] + 1) * 4,) + shape[axis + 2:])


def unfold(grid, axis, count):
    shape = grid.shape
    inner = shape[:axis] + (count, 4) + shape[axis + 1:]
    lower = lax.slice_in_dim(grid, 0, 4 * count, axis=axis).reshape(inner)
    upper = lax.slice_in_dim(grid, 4, 4 * count + 4, axis=axis).reshape(inner)
    return jnp.concatenate([lower, upper], axis=axis + 1)


def assemble(foot):
    count_first, count_second, count_third, channels = foot.shape[:4]
    grid = foot.reshape(count_first, count_second, count_third, channels, 8, 8, 8).transpose(3, 0, 4, 1, 5, 2, 6)
    grid = fold(grid, 1)
    grid = fold(grid, 2)
    return fold(grid, 3)


def spread_out(grid, count_first, count_second, count_third):
    channels = grid.shape[0]
    grid = unfold(grid, 1, count_first)
    grid = unfold(grid, 3, count_second)
    grid = unfold(grid, 5, count_third)
    return grid.transpose(1, 3, 5, 0, 2, 4, 6).reshape(count_first * count_second * count_third, channels, 512)


def wall_terms(counts, walls, level, wall_normal, wall_friction):
    table = jnp.asarray(quad_points, dtype=jnp.float32)
    select = (walls[:, None] == jnp.arange(wall_normal.shape[0], dtype=jnp.int32)[None, :]).astype(jnp.float32)
    normal = jnp.sum(select[:, :, None] * wall_normal[None], axis=1)
    friction = jnp.sum(select * wall_friction[None], axis=1)
    level_set = level[:, None] + jnp.sum(normal[:, None, :] * table[None], axis=2)
    cover = jnp.clip(0.5 - level_set, 0.0, 1.0)
    live = (jnp.arange(table.shape[0], dtype=jnp.int32)[None, :] < counts[:, None]).astype(jnp.float32)
    share = cover * live / jnp.maximum(counts, 1).astype(jnp.float32)[:, None]
    bits = jnp.asarray(corner_bits) == 1
    corner = jnp.prod(jnp.where(bits[None], table[:, None, :], 1.0 - table[:, None, :]), axis=2)
    weights = jnp.sum(share[:, :, None] * corner[None], axis=1)
    normal_part = weights[None] * jnp.transpose(normal)[:, :, None]
    return jnp.concatenate([normal_part, (weights * friction[:, None])[None]], axis=0)


def corner_index(first, second, third, span_second, span_third):
    bits = jnp.asarray(corner_bits)
    node_first = first[:, None] + bits[None, :, 0] + 2
    node_second = second[:, None] + bits[None, :, 1] + 2
    node_third = third[:, None] + bits[None, :, 2] + 2
    return (node_first * span_second + node_second) * span_third + node_third


def arrive(values, lead):
    pieces = []
    for direction in range(6):
        axis = lead + direction // 2
        step = 1 if direction % 2 == 0 else -1
        piece = jnp.take(values, direction, axis=lead + 3)
        shifted = jnp.roll(piece, step, axis=axis)
        if direction >= 2:
            place = lax.broadcasted_iota(jnp.int32, shifted.shape, axis)
            edge = 0 if step == 1 else shifted.shape[axis] - 1
            shifted = jnp.where(place == edge, jnp.zeros_like(shifted), shifted)
        pieces.append(shifted)
    return jnp.stack(pieces, axis=lead + 3)


def reference(state, bin_count, departing, depart_count, depart_block, cut_cell, quad_count, wall_id, cut_level, wall_normal, wall_friction):
    channels, count_first, count_second, count_third, slots = state.shape
    total_blocks = count_first * count_second * count_third
    slot_place = lax.broadcasted_iota(jnp.int32, (count_first, count_second, count_third, slots), 3)
    valid = (slot_place < bin_count[..., None]).astype(jnp.float32)

    def deposit_slab(pieces):
        slab_state, slab_valid = pieces
        return deposit(slab_state.reshape(channels, count_second * count_third, slots), slab_valid.reshape(count_second * count_third, slots))

    footprint = lax.map(deposit_slab, (jnp.moveaxis(state, 1, 0), valid)).reshape(total_blocks, 4, 512)
    incoming = arrive(departing, 1)
    incoming_count = arrive(depart_count, 0)
    incoming_block = arrive(depart_block, 0)
    brick_shape = incoming_block.shape
    brick_first = lax.broadcasted_iota(jnp.int32, brick_shape, 0)
    brick_second = lax.broadcasted_iota(jnp.int32, brick_shape, 1)
    brick_third = lax.broadcasted_iota(jnp.int32, brick_shape, 2)
    local_first = incoming_block // (KY * KZ)
    local_second = incoming_block // KZ % KY
    local_third = incoming_block % KZ
    target = ((brick_first * KX + local_first) * count_second + brick_second * KY + local_second) * count_third + brick_third * KZ + local_third
    arrival_place = lax.broadcasted_iota(jnp.int32, brick_shape + (slots,), 5)
    arrival_valid = (arrival_place < incoming_count[..., None]).astype(jnp.float32)

    def deposit_bricks(pieces):
        brick_state, brick_valid = pieces
        return deposit(brick_state.reshape(channels, -1, slots), brick_valid.reshape(-1, slots))

    landed = lax.map(deposit_bricks, (jnp.moveaxis(incoming, 1, 0), arrival_valid))
    footprint = footprint.at[target.reshape(-1)].add(landed.reshape(-1, 4, 512))
    grid = assemble(footprint.reshape(count_first, count_second, count_third, 4, 512))
    span_first, span_second, span_third = grid.shape[1:]
    cells_second = 4 * KY
    cells_third = 4 * KZ
    cut_first = lax.broadcasted_iota(jnp.int32, cut_cell.shape, 0)
    cut_second = lax.broadcasted_iota(jnp.int32, cut_cell.shape, 1)
    cut_third = lax.broadcasted_iota(jnp.int32, cut_cell.shape, 2)
    cell_first = cut_first * 4 * KX + cut_cell // (cells_second * cells_third)
    cell_second = cut_second * cells_second + cut_cell // cells_third % cells_second
    cell_third = cut_third * cells_third + cut_cell % cells_third
    values = wall_terms(quad_count.reshape(-1), wall_id.reshape(-1), cut_level.reshape(-1), wall_normal, wall_friction)
    index = corner_index(cell_first.reshape(-1), cell_second.reshape(-1), cell_third.reshape(-1), span_second, span_third)
    touch = jnp.zeros((4, span_first * span_second * span_third), jnp.float32).at[:, index.reshape(-1)].add(values.reshape(4, -1))
    sums = jnp.concatenate([grid, touch.reshape(4, span_first, span_second, span_third)], axis=0)
    inner = sums[:, 2:-2]
    inner = inner.at[:, 0:2].add(sums[:, -2:])
    inner = inner.at[:, -2:].add(sums[:, 0:2])
    owned = inner[:, :, 2:-2, 2:-2]
    velocity = advance(owned)
    velocity = jnp.pad(velocity, ((0, 0), (2, 2), (0, 0), (0, 0)), mode="wrap")
    velocity = jnp.pad(velocity, ((0, 0), (0, 0), (2, 2), (2, 2)))
    footprints = spread_out(velocity, count_first, count_second, count_third)

    def collect_slab(pieces):
        slab_foot, slab_state, slab_valid = pieces
        return collect(slab_foot, slab_state.reshape(channels, count_second * count_third, slots), slab_valid.reshape(count_second * count_third, slots))

    moved = lax.map(collect_slab, (footprints.reshape(count_first, count_second * count_third, 6, 512), jnp.moveaxis(state, 1, 0), valid))
    moved = jnp.moveaxis(moved.reshape(count_first, channels, count_second, count_third, slots), 0, 1)

    def collect_bricks(pieces):
        target_slab, brick_state, brick_valid = pieces
        return collect(footprints[target_slab.reshape(-1)], brick_state.reshape(channels, -1, slots), brick_valid.reshape(-1, slots))

    arrived = lax.map(collect_bricks, (target, jnp.moveaxis(incoming, 1, 0), arrival_valid))
    arrived = jnp.moveaxis(arrived.reshape((brick_shape[0], channels) + incoming.shape[2:]), 0, 1)
    return moved, arrived
```

```python
import jax
import jax.numpy as jnp
import numpy as np
from jax import lax
from jax.experimental import pallas as pl
from jax.experimental.pallas import tpu as pltpu
from jax.sharding import PartitionSpec as P

time_step = 0.1
stiffness = 4.0
gravity = 2.0
flip_ratio = 0.95
mass_floor = 0.25
center = 1.5
quad_points = [
    [0.5, 0.5, 0.5],
    [0.2, 0.7, 0.35],
    [0.8, 0.3, 0.65],
    [0.35, 0.15, 0.85],
    [0.65, 0.85, 0.15],
    [0.1, 0.45, 0.55],
    [0.9, 0.55, 0.45],
    [0.45, 0.9, 0.75],
]
f32 = jnp.float32
bf16 = jnp.bfloat16

ZR = 24
LN = 256
BINROWS = 72
XROWS = 192 + 96 + BINROWS
YROWS = 192 + BINROWS
ZROWS = 128


def lane_iota(shape):
    return lax.broadcasted_iota(jnp.int32, shape, len(shape) - 1)


def sub_iota(shape):
    return lax.broadcasted_iota(jnp.int32, shape, len(shape) - 2)


def spline(coord, nodes):
    distance = jnp.abs(coord - nodes)
    inner = 0.75 - distance * distance
    reach = jnp.maximum(1.5 - distance, 0.0)
    return jnp.where(distance < 0.5, inner, 0.5 * reach * reach)


def parts(value):
    high = value.astype(bf16)
    low = (value - high.astype(f32)).astype(bf16)
    return high, low


def plane_of(wx, wy):
    return jnp.concatenate([wy[y : y + 1] * wx for y in range(8)], axis=0)


def roll_lanes(value, shift):
    return pltpu.roll(value, shift % 128, 1)


def contact_terms(cell_ref, quad_ref, wall_ref, level_ref, normal_ref, friction_ref):
    cells = cell_ref[...]
    counts = quad_ref[...]
    walls = wall_ref[...]
    level = level_ref[...]
    normal = []
    for axis in range(3):
        part = jnp.zeros_like(level)
        for wall in range(4):
            part = jnp.where(walls == wall, normal_ref[wall, axis], part)
        normal.append(part)
    friction = jnp.zeros_like(level)
    for wall in range(4):
        friction = jnp.where(walls == wall, friction_ref[wall], friction)
    inverse = 1.0 / jnp.maximum(counts, 1).astype(f32)
    weights = [None] * 8
    for q, point in enumerate(quad_points):
        level_set = level + (normal[0] * point[0] + normal[1] * point[1] + normal[2] * point[2])
        cover = jnp.clip(0.5 - level_set, 0.0, 1.0)
        share = jnp.where(counts > q, cover * inverse, 0.0)
        for corner in range(8):
            factor = 1.0
            for axis in range(3):
                bit = (corner >> (2 - axis)) & 1
                factor *= point[axis] if bit else 1.0 - point[axis]
            term = share * factor
            weights[corner] = term if weights[corner] is None else weights[corner] + term
    return cells, weights, normal + [friction]


def contact_windows(cell_ref, quad_ref, wall_ref, level_ref, normal_ref, friction_ref):
    cells, weights, factors = contact_terms(
        cell_ref, quad_ref, wall_ref, level_ref, normal_ref, friction_ref
    )
    place_third = cells % 16 + 2
    column = (cells // 16) % 16 * 8 + cells // 256
    rows = sub_iota((ZR, 128))
    bit_rows = sub_iota((128, 128))
    lefts_high = []
    lefts_low = []
    rights = []
    for tile in range(4):
        third = place_third[tile : tile + 1]
        first_row = rows == third
        second_row = rows == third + 1
        pieces_high = []
        pieces_low = []
        for pair in range(4):
            lower = weights[2 * pair][tile : tile + 1]
            upper = weights[2 * pair + 1][tile : tile + 1]
            for channel in range(4):
                factor = factors[channel][tile : tile + 1]
                value = jnp.where(
                    first_row, lower * factor, jnp.where(second_row, upper * factor, 0.0)
                )
                high, low = parts(value)
                pieces_high.append(high.astype(f32))
                pieces_low.append(low.astype(f32))
        lefts_high.append(jnp.concatenate(pieces_high, axis=0).astype(bf16))
        lefts_low.append(jnp.concatenate(pieces_low, axis=0).astype(bf16))
        rights.append(
            jnp.where(bit_rows == column[tile : tile + 1], 1.0, 0.0).astype(bf16)
        )
    left = jnp.concatenate(lefts_high + lefts_low, axis=1)
    right = jnp.concatenate(rights + rights, axis=1)
    touched = lax.dot_general(
        left, right, (((1,), (1,)), ((), ())), preferred_element_type=f32
    )
    lanes = lane_iota((4 * ZR, 128))
    first = lanes % 8
    result = [[None, None], [None, None]]
    for pair in range(4):
        dx, dy = pair >> 1, pair & 1
        block = touched[pair * 4 * ZR : (pair + 1) * 4 * ZR]
        near = jnp.where(first <= 5 - dx, block, 0.0)
        far = jnp.where(first >= 6 - dx, block, 0.0)
        for window, (value, shift) in enumerate(
            ((near, 50 + 8 * dy + dx), (far, 46 + 8 * dy + dx))
        ):
            turned = roll_lanes(value, shift)
            for half, piece in enumerate(
                (jnp.where(lanes >= shift, turned, 0.0), jnp.where(lanes < shift, turned, 0.0))
            ):
                known = result[window][half]
                result[window][half] = piece if known is None else known + piece
    return result


def deposit_kernel(
    state_ref,
    bin_count_ref,
    depart_ref,
    depart_count_ref,
    depart_block_ref,
    zbins_ref,
    cell_ref,
    quad_ref,
    wall_ref,
    level_ref,
    normal_ref,
    friction_ref,
    window_ref,
    plus_ref,
    minus_ref,
    data,
    total,
):
    groups = [(state_ref, 8 * g, 8, 8 * g) for g in range(4)]
    groups += [(depart_ref, 8 * g, 8, 32 + 8 * g) for g in range(2)]
    groups += [(zbins_ref, 0, 4, 48)]
    for ref, begin, size, place in groups:
        if ref is zbins_ref:
            channel = [ref[4 * c : 4 * c + 4, :] for c in range(16)]
        else:
            channel = [ref[c, begin : begin + size, :] for c in range(16)]
        pressure = time_step * 4.0 * stiffness * jnp.maximum(1.0 - channel[15], 0.0)
        spread = [channel[6 + e] + (pressure if e % 4 == 0 else 0.0) for e in range(9)]
        offset = [channel[axis] - center for axis in range(3)]
        for axis in range(3):
            data[axis, place : place + size, :] = channel[axis]
            data[3 + axis, place : place + size, :] = (
                channel[3 + axis]
                - spread[3 * axis] * offset[0]
                - spread[3 * axis + 1] * offset[1]
                - spread[3 * axis + 2] * offset[2]
            )
        for entry in range(9):
            data[6 + entry, place : place + size, :] = spread[entry]

    total[...] = jnp.zeros_like(total)
    nodes = sub_iota((8, 128)).astype(f32) - 2.0
    slots = lane_iota((8, 128))
    lanes = lane_iota((32, 128))
    local = lane_iota((8, 128)) % 64
    node_first = (local % 8).astype(f32) - 2.0 - center
    node_second = (local // 8).astype(f32) - 2.0 - center
    node_third = nodes - center
    blank = jnp.zeros((64, 3 * 128), bf16)

    def one_bin(index, window, begin, third, count):
        def row(channel):
            return data[channel, pl.ds(index, 1), :]

        wx = spline(row(0), nodes)
        wy = spline(row(1), nodes)
        wz = jnp.where(slots < count, spline(row(2), nodes), 0.0)
        lifted = jnp.concatenate([wz] + [row(3 + c) * wz for c in range(12)], axis=0)
        lift_high, lift_low = parts(lifted)
        plane_high, plane_low = parts(plane_of(wx, wy))
        left = jnp.concatenate([lift_high, lift_high, lift_low], axis=1)
        right = jnp.concatenate([plane_high, plane_low, plane_high], axis=1)
        right = jnp.concatenate([right, blank], axis=0)
        moments = lax.dot_general(
            left, right, (((1,), (1,)), ((), ())), preferred_element_type=f32
        )
        sums = [moments[0:8]]
        for axis in range(3):
            at = 32 + 24 * axis
            sums.append(
                moments[8 + 8 * axis : 16 + 8 * axis]
                + moments[at : at + 8] * node_first
                + moments[at + 8 : at + 16] * node_second
                + moments[at + 16 : at + 24] * node_third
            )
        turned = pltpu.roll(jnp.concatenate(sums, axis=0), begin % 128, 1)
        inside = (lanes >= begin) & (lanes < begin + 64)
        beyond = (lanes >= begin - 128) & (lanes < begin - 64)
        total[window, third, :, 0:128] += jnp.where(inside, turned, 0.0)
        total[window, third, :, 128:256] += jnp.where(beyond, turned, 0.0)

    def residents(step, carry):
        first = step // 4
        second = step % 4
        for third in range(4):
            one_bin(
                step * 4 + third,
                first + 1,
                32 * (second + 1),
                third,
                bin_count_ref[first, second, third],
            )
        return carry

    lax.fori_loop(0, 8, residents, 0)

    def over_x(member, carry):
        for direction in range(2):
            block = depart_block_ref[0, 0, 0, direction, member]
            one_bin(
                32 + direction * 4 + member,
                3 if direction == 0 else 0,
                32 * (block // 4 % 4 + 1),
                block % 4,
                depart_count_ref[0, 0, 0, direction, member],
            )
        return carry

    lax.fori_loop(0, 4, over_x, 0)

    def over_y(member, carry):
        for direction in range(2, 4):
            block = depart_block_ref[0, 0, 0, direction, member]
            one_bin(
                32 + direction * 4 + member,
                block // 16 + 1,
                160 if direction == 2 else 0,
                block % 4,
                depart_count_ref[0, 0, 0, direction, member],
            )
        return carry

    lax.fori_loop(0, 4, over_y, 0)

    for member in range(4):
        count = zbins_ref[64 + member : 65 + member, :].astype(jnp.int32)[0, 0]
        block = zbins_ref[68 + member : 69 + member, :].astype(jnp.int32)[0, 0]
        one_bin(48 + member, block // 16 + 1, 32 * (block // 4 % 4 + 1), block % 4, count)

    contact = contact_windows(
        cell_ref, quad_ref, wall_ref, level_ref, normal_ref, friction_ref
    )
    lower_rows = sub_iota((8, 128)) < 4
    lower_lanes = lane_iota((8, 128)) % 8 < 4
    lower_tall = lane_iota((ZR, 128)) % 8 < 4
    for half in range(2):
        columns = slice(128 * half, 128 * half + 128)
        for c in range(4):
            folded = []
            for window in range(4):
                piece = [total[window, third, 8 * c : 8 * c + 8, columns] for third in range(4)]
                one = pltpu.roll(piece[1], 4, 0)
                three = pltpu.roll(piece[3], 4, 0)
                folded.append(
                    jnp.concatenate(
                        [
                            piece[0] + jnp.where(lower_rows, 0.0, one),
                            piece[2] + jnp.where(lower_rows, one, three),
                            jnp.where(lower_rows, three, 0.0),
                        ],
                        axis=0,
                    )
                )
            window_ref[0, c, :, columns] = folded[1] + jnp.where(
                lower_tall, roll_lanes(folded[0], -4), 0.0
            )
            window_ref[1, c, :, columns] = folded[2] + jnp.where(
                lower_tall, 0.0, roll_lanes(folded[3], 4)
            )
            at = (2 * c + half) * ZR
            plus_ref[at : at + ZR, :] = folded[3] + jnp.where(
                lower_tall, roll_lanes(folded[2], -4), 0.0
            )
            minus_ref[at : at + ZR, :] = folded[0] + jnp.where(
                lower_tall, 0.0, roll_lanes(folded[1], 4)
            )
            near = contact[0][half][ZR * c : ZR * c + ZR]
            far = contact[1][half][ZR * c : ZR * c + ZR]
            window_ref[0, 4 + c, :, columns] = near
            window_ref[1, 4 + c, :, columns] = far
        for pair in range(2):
            at = 192 + (2 * pair + half) * ZR
            even = ZR * 2 * pair
            odd = even + ZR
            near, far = contact[0][half], contact[1][half]
            plus_ref[at : at + ZR, :] = jnp.where(
                lower_tall, roll_lanes(far[even : even + ZR], -4), far[odd : odd + ZR]
            )
            minus_ref[at : at + ZR, :] = jnp.where(
                lower_tall, near[even : even + ZR], roll_lanes(near[odd : odd + ZR], 4)
            )
    put_bins(plus_ref, 288, depart_ref, depart_count_ref, depart_block_ref, 0)
    put_bins(minus_ref, 288, depart_ref, depart_count_ref, depart_block_ref, 1)


def put_bins(out_ref, at, depart_ref, depart_count_ref, depart_block_ref, direction):
    for c in range(16):
        out_ref[at + 4 * c : at + 4 * c + 4, :] = depart_ref[
            c, 4 * direction : 4 * direction + 4, :
        ]
    for member in range(4):
        count = depart_count_ref[0, 0, 0, direction, member]
        block = depart_block_ref[0, 0, 0, direction, member]
        out_ref[at + 64 + member : at + 65 + member, :] = jnp.full((1, 128), count).astype(f32)
        out_ref[at + 68 + member : at + 69 + member, :] = jnp.full((1, 128), block).astype(f32)


def second_kernel(
    window_in,
    from_minus,
    from_plus,
    depart_ref,
    depart_count_ref,
    depart_block_ref,
    window_ref,
    plus_ref,
    minus_ref,
):
    lower = lane_iota((ZR, 128)) % 8 < 4
    left = lane_iota((ZR, 128)) < 64
    for c in range(8):
        new = [[None, None], [None, None]]
        for half in range(2):
            columns = slice(128 * half, 128 * half + 128)
            if c < 4:
                at = (2 * c + half) * ZR
                near = from_minus[at : at + ZR, :]
                far = from_plus[at : at + ZR, :]
            else:
                at = 192 + (2 * ((c - 4) // 2) + half) * ZR
                near = from_minus[at : at + ZR, :]
                far = from_plus[at : at + ZR, :]
                if c % 2 == 0:
                    near = jnp.where(lower, near, 0.0)
                    far = jnp.where(lower, 0.0, roll_lanes(far, 4))
                else:
                    near = jnp.where(lower, roll_lanes(near, -4), 0.0)
                    far = jnp.where(lower, 0.0, far)
            new[0][half] = window_in[0, c, :, columns] + near
            new[1][half] = window_in[1, c, :, columns] + far
            window_ref[0, c, :, columns] = new[0][half]
            window_ref[1, c, :, columns] = new[1][half]
        at = c * ZR
        plus_ref[at : at + ZR, :] = jnp.where(
            left, roll_lanes(new[0][1], -32), roll_lanes(new[1][1], 32)
        )
        minus_ref[at : at + ZR, :] = jnp.where(left, new[0][0], roll_lanes(new[1][0], 64))
    put_bins(plus_ref, 192, depart_ref, depart_count_ref, depart_block_ref, 2)
    put_bins(minus_ref, 192, depart_ref, depart_count_ref, depart_block_ref, 3)


def third_kernel(window_in, from_minus, from_plus, window_ref, message_ref):
    core = lax.axis_index("gz")
    lanes = lane_iota((ZR, 128))
    lower_rows = sub_iota((8, 128)) < 4
    for window in range(2):
        edges = []
        for c in range(8):
            at = c * ZR
            near = from_minus[at : at + ZR, :]
            far = from_plus[at : at + ZR, :]
            low = window_in[window, c, :, 0:128] + jnp.where(
                (lanes >= 32) & (lanes < 96), roll_lanes(near, 32 if window == 0 else -32), 0.0
            )
            high = window_in[window, c, :, 128:256] + jnp.where(
                lanes < 64, far if window == 0 else roll_lanes(far, 64), 0.0
            )
            window_ref[window, c, :, 0:128] = low
            window_ref[window, c, :, 128:256] = high
            edges.append([jnp.where(core == 0, v[16:24], v[0:8]) for v in (low, high)])
        for pair in range(4):
            for half in range(2):
                at = ((window * 4 + pair) * 2 + half) * 8
                message_ref[at : at + 8, :] = jnp.where(
                    lower_rows, edges[2 * pair][half], pltpu.roll(edges[2 * pair + 1][half], 4, 0)
                )


def advance(sums):
    mass = jnp.maximum(sums[0], mass_floor)
    previous = [sums[1 + axis] / mass for axis in range(3)]
    velocity = [previous[0], previous[1], previous[2] - time_step * gravity]
    normal = sums[4:7]
    scale = 1.0 + (normal[0] * normal[0] + normal[1] * normal[1] + normal[2] * normal[2])
    dot = velocity[0] * normal[0] + velocity[1] * normal[1] + velocity[2] * normal[2]
    inward = jnp.minimum(dot, 0.0) / scale
    velocity = [velocity[axis] - inward * normal[axis] for axis in range(3)]
    dot = velocity[0] * normal[0] + velocity[1] * normal[1] + velocity[2] * normal[2]
    along = dot / scale
    damp = 1.0 - jnp.exp(-sums[7])
    velocity = [
        velocity[axis] - damp * (velocity[axis] - along * normal[axis]) for axis in range(3)
    ]
    return velocity + previous


def collect_kernel(
    window_in,
    from_z,
    from_west,
    from_east,
    from_south,
    from_north,
    zbins_ref,
    state_ref,
    bin_count_ref,
    moved_ref,
    arrived_ref,
    data,
    fields,
    turned,
    table,
    picked,
    live,
    target,
):
    core = lax.axis_index("gz")
    row = lax.axis_index("gy")
    lanes = lane_iota((8, 128))
    subs = sub_iota((8, 128))
    lower_rows = subs < 4
    lower_lanes = lanes % 8 < 4

    for g in range(4):
        for c in range(16):
            data[c, 8 * g : 8 * g + 8, :] = state_ref[c, 8 * g : 8 * g + 8, :]
    arrivals = ((from_west, 288), (from_east, 288), (from_south, 192), (from_north, 192))
    arrivals += ((zbins_ref, 0),)
    for g, (ref, at) in enumerate(arrivals):
        for c in range(16):
            data[c, 32 + 4 * g : 36 + 4 * g, :] = ref[at + 4 * c : at + 4 * c + 4, :]
        slot = lane_iota((4, 128)).astype(f32)
        live[32 + 4 * g : 36 + 4 * g, :] = jnp.where(
            slot < ref[at + 64 : at + 68, :], 1.0, 0.0
        )
        for member in range(4):
            block = ref[at + 68 + member : at + 69 + member, :].astype(jnp.int32)[0, 0]
            target[4 * g + member] = block

    for third in range(3):
        rows = slice(8 * third, 8 * third + 8)
        for half in range(2):
            columns = slice(128 * half, 128 * half + 128)
            sums = [[], []]
            for c in range(8):
                values = [window_in[b, c, rows, columns] for b in range(2)]
                if third != 1:
                    for b in range(2):
                        at = ((b * 4 + c // 2) * 2 + half) * 8
                        edge = from_z[at : at + 8, :]
                        if c % 2 == 1:
                            edge = pltpu.roll(edge, 4, 0)
                        here = core == (1 if third == 0 else 0)
                        values[b] = values[b] + jnp.where(lower_rows & here, edge, 0.0)
                sums[0].append(
                    values[0] + jnp.where(lower_lanes, 0.0, roll_lanes(values[1], 4))
                )
                sums[1].append(
                    values[1] + jnp.where(lower_lanes, roll_lanes(values[0], -4), 0.0)
                )
            node_second = row * 16 + (lanes + 128 * half) // 8 - 6
            node_third = core * 16 + subs + 8 * third - 2
            inside = (
                (node_second >= 0) & (node_second < 128) & (node_third >= 0) & (node_third < 32)
            )
            for b in range(2):
                for c, value in enumerate(advance(sums[b])):
                    fields[b, c, rows, columns] = jnp.where(inside, value, 0.0)

    wide = lane_iota((ZR, 128))
    local = wide % 64
    node_first = (local % 8).astype(f32) - 2.0 - center
    node_second = (local // 8).astype(f32) - 2.0 - center
    for b in range(2):
        for c in range(6):
            low = fields[b, c, :, 0:128]
            high = fields[b, c, :, 128:256]
            shown = [
                jnp.where(wide < 64, roll_lanes(low, -32), roll_lanes(low, 32)),
                jnp.where(wide < 64, roll_lanes(low, 64), low),
                jnp.where(
                    wide < 64,
                    jnp.where(wide < 32, roll_lanes(low, 32), roll_lanes(high, 32)),
                    jnp.where(wide < 96, roll_lanes(low, -32), roll_lanes(high, 96)),
                ),
                jnp.where(wide < 64, high, roll_lanes(high, 64)),
            ]
            for second in range(4):
                turned[second, :, c, :] = shown[second]
                if c < 3:
                    turned[second, :, 6 + c, :] = shown[second] * node_first
                    turned[second, :, 9 + c, :] = shown[second] * node_second
        for second in range(4):
            value = turned[second].reshape(ZR * 16, 128)
            high, low = parts(value)
            table[4 * b + second, :, 0:128] = high
            table[4 * b + second, :, 128:256] = low

    nodes = subs.astype(f32) - 2.0

    def one_bin(index, column, third):
        def row_of(channel):
            return data[channel, pl.ds(index, 1), :]

        place = row_of(2)
        wx = spline(row_of(0), nodes)
        wy = spline(row_of(1), nodes)
        wz = spline(place, nodes)
        lever = wz * (nodes - place)
        high, low = parts(plane_of(wx, wy))
        right = jnp.concatenate([high, low, high, low], axis=0)
        left = table[column, pl.ds(64 * third, 128), :]
        values = jnp.dot(left, right, preferred_element_type=f32)
        first = values[0:8] * wz[0:1]
        second = values[8:16] * wz[0:1]
        moment = values[0:8] * lever[0:1]
        for k in range(1, 8):
            first = first + values[16 * k : 16 * k + 8] * wz[k : k + 1]
            second = second + values[16 * k + 8 : 16 * k + 16] * wz[k : k + 1]
            moment = moment + values[16 * k : 16 * k + 8] * lever[k : k + 1]
        picked[0:8, index, :] = first
        picked[8:16, index, :] = second
        picked[16:24, index, :] = moment

    def residents(step, carry):
        first = step // 4
        second = step % 4
        for third in range(4):
            index = step * 4 + third
            one_bin(index, step, third)
            count = bin_count_ref[first, second, third]
            live[pl.ds(index, 1), :] = jnp.where(lane_iota((1, 128)) < count, 1.0, 0.0)
        return carry

    lax.fori_loop(0, 8, residents, 0)

    def movers(step, carry):
        for member in range(2):
            block = target[2 * step + member]
            one_bin(32 + 2 * step + member, block // 4, block % 4)
        return carry

    lax.fori_loop(0, 10, movers, 0)

    def finish(begin, size):
        rows = slice(begin, begin + size)
        valid = live[rows, :]
        old = [data[c, rows, :] for c in range(16)]
        got = [picked[c, rows, :] for c in range(19)]
        result = []
        for axis in range(3):
            result.append(old[axis] + time_step * got[axis])
        for axis in range(3):
            result.append(
                flip_ratio * (old[3 + axis] + got[axis] - got[3 + axis])
                + (1.0 - flip_ratio) * got[axis]
            )
        affine = []
        for axis in range(3):
            affine.append(4.0 * (got[6 + axis] - (old[0] - center) * got[axis]))
            affine.append(4.0 * (got[9 + axis] - (old[1] - center) * got[axis]))
            affine.append(4.0 * got[16 + axis])
        result += affine
        result.append(old[15] * (1.0 + time_step * (affine[0] + affine[4] + affine[8])))
        return [value * valid for value in result]

    for g in range(4):
        for c, value in enumerate(finish(8 * g, 8)):
            moved_ref[c, 8 * g : 8 * g + 8, :] = value
    for g in range(2):
        for c, value in enumerate(finish(32 + 8 * g, 8)):
            arrived_ref[c, 8 * g : 8 * g + 8, :] = value
    for c, value in enumerate(finish(48, 4)):
        arrived_ref[c, 16:20, :] = jnp.where(core == 1, value, 0.0)
        arrived_ref[c, 20:24, :] = jnp.where(core == 0, value, 0.0)


def ring(axis, step, closed):
    count = lax.axis_size(axis)
    route = [(i, i + step) for i in range(count)]
    if closed:
        return [(i, j % count) for i, j in route]
    return [(i, j) for i, j in route if 0 <= j < count]


vmem = pl.BlockSpec(memory_space=pltpu.VMEM)
smem = pl.BlockSpec(memory_space=pltpu.SMEM)
limits = pltpu.CompilerParams(vmem_limit_bytes=48 * 1024 * 1024)


def shape_of(*dims):
    return jax.ShapeDtypeStruct(dims, f32)


def body(
    state,
    bin_count,
    departing,
    depart_count,
    depart_block,
    cut_cell,
    quad_count,
    wall_id,
    cut_level,
    wall_normal,
    wall_friction,
):
    core = lax.axis_index("gz")
    state_rows = state.reshape(16, 32, 128)
    leaving = departing.reshape(16, 24, 128)
    cut = [value.reshape(4, 128) for value in (cut_cell, quad_count, wall_id, cut_level)]

    def spread(value):
        picked = jnp.where(core == 0, value[0, 0, 0, 4], value[0, 0, 0, 5]).astype(f32)
        return jnp.broadcast_to(picked[:, None], (4, 128))

    upward = jnp.where(core == 0, departing[:, 0, 0, 0, 4], departing[:, 0, 0, 0, 5])
    zbins = jnp.concatenate(
        [upward.reshape(64, 128), spread(depart_count), spread(depart_block)], axis=0
    )
    zbins = lax.ppermute(zbins, "gz", [(0, 1), (1, 0)])

    window, plus, minus = pl.pallas_call(
        deposit_kernel,
        out_shape=[shape_of(2, 8, ZR, LN), shape_of(XROWS, 128), shape_of(XROWS, 128)],
        in_specs=[vmem, smem, vmem, smem, smem, vmem, vmem, vmem, vmem, vmem, smem, smem],
        out_specs=[vmem] * 3,
        scratch_shapes=[pltpu.VMEM((16, 56, 128), f32), pltpu.VMEM((4, 4, 32, LN), f32)],
        compiler_params=limits,
        name="deposit",
    )(
        state_rows,
        bin_count,
        leaving,
        depart_count,
        depart_block,
        zbins,
        *cut,
        wall_normal,
        wall_friction,
    )
    from_west = lax.ppermute(plus, "gx", ring("gx", 1, True))
    from_east = lax.ppermute(minus, "gx", ring("gx", -1, True))
    window, plus, minus = pl.pallas_call(
        second_kernel,
        out_shape=[shape_of(2, 8, ZR, LN), shape_of(YROWS, 128), shape_of(YROWS, 128)],
        in_specs=[vmem, vmem, vmem, vmem, smem, smem],
        out_specs=[vmem] * 3,
        compiler_params=limits,
        name="take_x",
    )(window, from_west, from_east, leaving, depart_count, depart_block)
    from_south = lax.ppermute(plus, "gy", ring("gy", 1, False))
    from_north = lax.ppermute(minus, "gy", ring("gy", -1, False))
    window, message = pl.pallas_call(
        third_kernel,
        out_shape=[shape_of(2, 8, ZR, LN), shape_of(ZROWS, 128)],
        in_specs=[vmem] * 3,
        out_specs=[vmem] * 2,
        compiler_params=limits,
        name="take_y",
    )(window, from_south, from_north)
    from_z = lax.ppermute(message, "gz", [(0, 1), (1, 0)])
    moved, arrived = pl.pallas_call(
        collect_kernel,
        out_shape=[shape_of(16, 32, 128), shape_of(16, 24, 128)],
        in_specs=[vmem] * 8 + [smem],
        out_specs=[vmem] * 2,
        scratch_shapes=[
            pltpu.VMEM((16, 56, 128), f32),
            pltpu.VMEM((2, 6, ZR, LN), f32),
            pltpu.VMEM((4, ZR, 16, 128), f32),
            pltpu.VMEM((8, ZR * 16, 256), bf16),
            pltpu.VMEM((24, 56, 128), f32),
            pltpu.VMEM((56, 128), f32),
            pltpu.SMEM((20,), jnp.int32),
        ],
        compiler_params=limits,
        name="collect",
    )(
        window,
        from_z,
        from_west,
        from_east,
        from_south,
        from_north,
        zbins,
        state_rows,
        bin_count,
    )
    return moved.reshape(state.shape), arrived.reshape(departing.shape)


def solution(mesh):
    placed = (
        P(None, "gx", "gy", "gz", None),
        P("gx", "gy", "gz"),
        P(None, "gx", "gy", "gz", None, None, None),
        P("gx", "gy", "gz", None, None),
        P("gx", "gy", "gz", None, None),
        P("gx", "gy", "gz", None),
        P("gx", "gy", "gz", None),
        P("gx", "gy", "gz", None),
        P("gx", "gy", "gz", None),
        P(),
        P(),
    )
    return jax.shard_map(
        body,
        mesh=mesh,
        in_specs=placed,
        out_specs=(P(None, "gx", "gy", "gz", None), P(None, "gx", "gy", "gz", None, None, None)),
        check_vma=False,
    )
```

```python
import jax
import jax.numpy as jnp
import numpy as np
from jax import lax
from jax.experimental import pallas as pl
from jax.experimental.pallas import tpu as pltpu
from jax.sharding import PartitionSpec as P

time_step = 0.1
stiffness = 4.0
gravity = 2.0
flip_ratio = 0.95
mass_floor = 0.25
center = 1.5
quad_points = [
    [0.5, 0.5, 0.5],
    [0.2, 0.7, 0.35],
    [0.8, 0.3, 0.65],
    [0.35, 0.15, 0.85],
    [0.65, 0.85, 0.15],
    [0.1, 0.45, 0.55],
    [0.9, 0.55, 0.45],
    [0.45, 0.9, 0.75],
]
f32 = jnp.float32
bf16 = jnp.bfloat16

ZR = 24
LN = 256
BINROWS = 72
XROWS = 192 + 48 + BINROWS
YROWS = 96 + 48 + BINROWS
ZROWS = 256 + BINROWS


def lane_iota(shape):
    return lax.broadcasted_iota(jnp.int32, shape, len(shape) - 1)


def sub_iota(shape):
    return lax.broadcasted_iota(jnp.int32, shape, len(shape) - 2)


def spline(coord, nodes):
    distance = jnp.abs(coord - nodes)
    inner = 0.75 - distance * distance
    reach = jnp.maximum(1.5 - distance, 0.0)
    return jnp.where(distance < 0.5, inner, 0.5 * reach * reach)


def parts(value):
    high = value.astype(bf16)
    low = (value - high.astype(f32)).astype(bf16)
    return high, low


def plane_of(wx, wy):
    return jnp.concatenate([wy[y : y + 1] * wx for y in range(8)], axis=0)


def roll_lanes(value, shift):
    return pltpu.roll(value, shift % 128, 1)


def contact_terms(cell_ref, quad_ref, wall_ref, level_ref, normal_ref, friction_ref):
    cells = cell_ref[...]
    counts = quad_ref[...]
    walls = wall_ref[...]
    level = level_ref[...]
    normal = []
    for axis in range(3):
        part = jnp.zeros_like(level)
        for wall in range(4):
            part = jnp.where(walls == wall, normal_ref[wall, axis], part)
        normal.append(part)
    friction = jnp.zeros_like(level)
    for wall in range(4):
        friction = jnp.where(walls == wall, friction_ref[wall], friction)
    inverse = 1.0 / jnp.maximum(counts, 1).astype(f32)
    weights = [None] * 8
    for q, point in enumerate(quad_points):
        level_set = level + (normal[0] * point[0] + normal[1] * point[1] + normal[2] * point[2])
        cover = jnp.clip(0.5 - level_set, 0.0, 1.0)
        share = jnp.where(counts > q, cover * inverse, 0.0)
        for corner in range(8):
            factor = 1.0
            for axis in range(3):
                bit = (corner >> (2 - axis)) & 1
                factor *= point[axis] if bit else 1.0 - point[axis]
            term = share * factor
            weights[corner] = term if weights[corner] is None else weights[corner] + term
    return cells, weights, normal + [friction]


def contact_windows(cell_ref, quad_ref, wall_ref, level_ref, normal_ref, friction_ref):
    cells, weights, factors = contact_terms(
        cell_ref, quad_ref, wall_ref, level_ref, normal_ref, friction_ref
    )
    place_third = cells % 16 + 2 + 4 * lax.axis_index("gz")
    column = (cells // 16) % 16 * 8 + cells // 256
    rows = sub_iota((ZR, 128))
    bit_rows = sub_iota((128, 128))
    lefts_high = []
    lefts_low = []
    rights = []
    for tile in range(4):
        third = place_third[tile : tile + 1]
        first_row = rows == third
        second_row = rows == third + 1
        pieces_high = []
        pieces_low = []
        for pair in range(4):
            lower = weights[2 * pair][tile : tile + 1]
            upper = weights[2 * pair + 1][tile : tile + 1]
            for channel in range(4):
                factor = factors[channel][tile : tile + 1]
                value = jnp.where(
                    first_row, lower * factor, jnp.where(second_row, upper * factor, 0.0)
                )
                high, low = parts(value)
                pieces_high.append(high.astype(f32))
                pieces_low.append(low.astype(f32))
        lefts_high.append(jnp.concatenate(pieces_high, axis=0).astype(bf16))
        lefts_low.append(jnp.concatenate(pieces_low, axis=0).astype(bf16))
        rights.append(
            jnp.where(bit_rows == column[tile : tile + 1], 1.0, 0.0).astype(bf16)
        )
    left = jnp.concatenate(lefts_high + lefts_low, axis=1)
    right = jnp.concatenate(rights + rights, axis=1)
    touched = lax.dot_general(
        left, right, (((1,), (1,)), ((), ())), preferred_element_type=f32
    )
    lanes = lane_iota((4 * ZR, 128))
    first = lanes % 8
    result = [[None, None], [None, None]]
    for pair in range(4):
        dx, dy = pair >> 1, pair & 1
        block = touched[pair * 4 * ZR : (pair + 1) * 4 * ZR]
        near = jnp.where(first <= 5 - dx, block, 0.0)
        far = jnp.where(first >= 6 - dx, block, 0.0)
        for window, (value, shift) in enumerate(
            ((near, 50 + 8 * dy + dx), (far, 46 + 8 * dy + dx))
        ):
            turned = roll_lanes(value, shift)
            for half, piece in enumerate(
                (jnp.where(lanes >= shift, turned, 0.0), jnp.where(lanes < shift, turned, 0.0))
            ):
                known = result[window][half]
                result[window][half] = piece if known is None else known + piece
    return result


def deposit_kernel(*refs):
    inputs, (window_ref, one_ref, two_ref, bins_ref) = refs[:11], refs[11:15]
    even = lax.axis_index("gx") % 2 == 0
    copies, (data, total, semaphores) = refs[15:26], refs[26:]
    started = []
    for place in (5, 6, 7, 8, 9, 10, 0, 2, 1, 3, 4):
        started.append(
            pltpu.make_async_copy(inputs[place], copies[place], semaphores.at[place])
        )
        started[-1].start()
    state_ref, bin_count_ref, depart_ref, depart_count_ref, depart_block_ref = copies[:5]
    total[...] = jnp.zeros_like(total)
    for copy in started[:6]:
        copy.wait()
    contact = contact_windows(*copies[5:])
    for copy in started[6:]:
        copy.wait()

    core = lax.axis_index("gz")
    size = 8
    groups = [(state_ref, 8 * g, 8 * g) for g in range(4)]
    groups += [(depart_ref, 8 * g, 32 + 8 * g) for g in range(3)]
    for ref, begin, place in groups:
        channel = [ref[c, begin : begin + size, :] for c in range(16)]
        pressure = time_step * 4.0 * stiffness * jnp.maximum(1.0 - channel[15], 0.0)
        spread = [channel[6 + e] + (pressure if e % 4 == 0 else 0.0) for e in range(9)]
        offset = [channel[axis] - center for axis in range(3)]
        for axis in range(3):
            data[axis, place : place + size, :] = channel[axis]
            data[3 + axis, place : place + size, :] = (
                channel[3 + axis]
                - spread[3 * axis] * offset[0]
                - spread[3 * axis + 1] * offset[1]
                - spread[3 * axis + 2] * offset[2]
            )
        for entry in range(9):
            data[6 + entry, place : place + size, :] = spread[entry]

    nodes = sub_iota((8, 128)).astype(f32) - 2.0
    slots = lane_iota((8, 128))
    lanes = lane_iota((32, 128))
    local = lane_iota((8, 128)) % 64
    node_first = (local % 8).astype(f32) - 2.0 - center
    node_second = (local // 8).astype(f32) - 2.0 - center
    node_third = nodes - center
    blank = jnp.zeros((64, 3 * 128), bf16)

    def one_bin(index, window, begin, third, count):
        def row(channel):
            return data[channel, pl.ds(index, 1), :]

        wx = spline(row(0), nodes)
        wy = spline(row(1), nodes)
        wz = jnp.where(slots < count, spline(row(2), nodes), 0.0)
        lifted = jnp.concatenate([wz] + [row(3 + c) * wz for c in range(12)], axis=0)
        lift_high, lift_low = parts(lifted)
        plane_high, plane_low = parts(plane_of(wx, wy))
        left = jnp.concatenate([lift_high, lift_high, lift_low], axis=1)
        right = jnp.concatenate([plane_high, plane_low, plane_high], axis=1)
        right = jnp.concatenate([right, blank], axis=0)
        moments = lax.dot_general(
            left, right, (((1,), (1,)), ((), ())), preferred_element_type=f32
        )
        sums = [moments[0:8]]
        for axis in range(3):
            at = 32 + 24 * axis
            sums.append(
                moments[8 + 8 * axis : 16 + 8 * axis]
                + moments[at : at + 8] * node_first
                + moments[at + 8 : at + 16] * node_second
                + moments[at + 16 : at + 24] * node_third
            )
        turned = pltpu.roll(jnp.concatenate(sums, axis=0), begin % 128, 1)
        inside = (lanes >= begin) & (lanes < begin + 64)
        beyond = (lanes >= begin - 128) & (lanes < begin - 64)
        total[window, third, :, 0:128] += jnp.where(inside, turned, 0.0)
        total[window, third, :, 128:256] += jnp.where(beyond, turned, 0.0)

    def residents(step, carry):
        first = step // 4
        second = step % 4
        for third in range(4):
            one_bin(
                step * 4 + third,
                first + 1,
                32 * (second + 1),
                third + core,
                bin_count_ref[first, second, third],
            )
        return carry

    lax.fori_loop(0, 8, residents, 0)

    def over_x(member, carry):
        for direction in range(2):
            block = depart_block_ref[0, 0, 0, member, direction]
            one_bin(
                32 + direction * 4 + member,
                3 if direction == 0 else 0,
                32 * (block // 4 % 4 + 1),
                block % 4 + core,
                depart_count_ref[0, 0, 0, member, direction],
            )
        return carry

    lax.fori_loop(0, 4, over_x, 0)

    def over_y(member, carry):
        for direction in range(2, 4):
            block = depart_block_ref[0, 0, 0, member, direction]
            one_bin(
                32 + direction * 4 + member,
                block // 16 + 1,
                160 if direction == 2 else 0,
                block % 4 + core,
                depart_count_ref[0, 0, 0, member, direction],
            )
        return carry

    lax.fori_loop(0, 4, over_y, 0)

    for member in range(4):
        block = depart_block_ref[0, 0, 0, member, 4 + core]
        one_bin(
            48 + 4 * core + member,
            block // 16 + 1,
            32 * (block // 4 % 4 + 1),
            4 - 4 * core,
            depart_count_ref[0, 0, 0, member, 4 + core],
        )

    lower_rows = sub_iota((8, 128)) < 4
    lower_lanes = lane_iota((8, 128)) % 8 < 4
    lower_tall = lane_iota((ZR, 128)) % 8 < 4
    pieces = {}
    for half in range(2):
        columns = slice(128 * half, 128 * half + 128)
        for c in range(4):
            folded = []
            for window in range(4):
                piece = [total[window, third, 8 * c : 8 * c + 8, columns] for third in range(5)]
                one = pltpu.roll(piece[1], 4, 0)
                three = pltpu.roll(piece[3], 4, 0)
                folded.append(
                    jnp.concatenate(
                        [
                            piece[0] + jnp.where(lower_rows, 0.0, one),
                            piece[2] + jnp.where(lower_rows, one, three),
                            piece[4] + jnp.where(lower_rows, three, 0.0),
                        ],
                        axis=0,
                    )
                )
            window_ref[0, c, :, columns] = folded[1] + jnp.where(
                lower_tall, roll_lanes(folded[0], -4), 0.0
            )
            window_ref[1, c, :, columns] = folded[2] + jnp.where(
                lower_tall, 0.0, roll_lanes(folded[3], 4)
            )
            at = (2 * c + half) * ZR
            pieces[at] = [
                folded[3] + jnp.where(lower_tall, roll_lanes(folded[2], -4), 0.0),
                folded[0] + jnp.where(lower_tall, 0.0, roll_lanes(folded[1], 4)),
            ]
            near = contact[0][half][ZR * c : ZR * c + ZR]
            far = contact[1][half][ZR * c : ZR * c + ZR]
            window_ref[0, 4 + c, :, columns] = near
            window_ref[1, 4 + c, :, columns] = far
    tall = lane_iota((ZR, 128))
    for pair in range(2):
        first_c = slice(2 * pair * ZR, (2 * pair + 1) * ZR)
        second_c = slice((2 * pair + 1) * ZR, (2 * pair + 2) * ZR)
        near = [
            jnp.where(lower_tall, contact[0][half][first_c], roll_lanes(contact[0][half][second_c], 4))
            for half in range(2)
        ]
        far = [
            jnp.where(lower_tall, roll_lanes(contact[1][half][first_c], -4), contact[1][half][second_c])
            for half in range(2)
        ]
        main = 192 + pair * ZR
        rest = (2 * pair + 1) * ZR
        pieces[main] = []
        for side, packed in enumerate((far, near)):
            pieces[main].append(jnp.where(tall >= 48, packed[0], packed[1]))
            pieces[rest][side] = jnp.where(
                (tall >= 96) & (tall < 104), roll_lanes(packed[1], 48), pieces[rest][side]
            )
    for at, (plus, minus) in pieces.items():
        put_pair(one_ref, two_ref, slice(at, at + ZR), even, plus, minus)
    plus = bins_of(depart_ref, depart_count_ref, depart_block_ref, 0)
    minus = bins_of(depart_ref, depart_count_ref, depart_block_ref, 1)
    for part in range(18):
        at = 240 + 4 * part
        put_pair(one_ref, two_ref, slice(at, at + 4), even, plus[part], minus[part])
    south = bins_of(depart_ref, depart_count_ref, depart_block_ref, 2)
    north = bins_of(depart_ref, depart_count_ref, depart_block_ref, 3)
    up = bins_of(depart_ref, depart_count_ref, depart_block_ref, 4)
    down = bins_of(depart_ref, depart_count_ref, depart_block_ref, 5)
    for part in range(18):
        bins_ref[4 * part : 4 * part + 4, :] = south[part]
        bins_ref[72 + 4 * part : 76 + 4 * part, :] = north[part]
        bins_ref[144 + 4 * part : 148 + 4 * part, :] = jnp.where(core == 0, up[part], down[part])


def bins_of(depart_ref, depart_count_ref, depart_block_ref, direction):
    values = [depart_ref[c, 4 * direction : 4 * direction + 4, :] for c in range(16)]
    row = sub_iota((4, 128))
    for ref in (depart_count_ref, depart_block_ref):
        value = jnp.zeros((4, 128), jnp.int32)
        for member in range(4):
            value = jnp.where(row == member, ref[0, 0, 0, member, direction], value)
        values.append(value.astype(f32))
    return values


def put_pair(one_ref, two_ref, at, even, plus, minus):
    one_ref[at, :] = jnp.where(even, plus, minus)
    two_ref[at, :] = jnp.where(even, minus, plus)


def take_pair(one_ref, two_ref, at, even):
    one, two = one_ref[at, :], two_ref[at, :]
    return jnp.where(even, two, one), jnp.where(even, one, two)


def stage_kernel(window_in, bins_in, window_ref, bins_ref):
    window_ref[...] = window_in[...]
    bins_ref[...] = bins_in[...]


def second_kernel(window_in, from_one, from_two, bins_ref, window_ref, one_ref, two_ref):
    even = lax.axis_index("gx") % 2 == 0
    even_second = lax.axis_index("gy") % 2 == 0
    lanes = lane_iota((ZR, 128))
    lower = lanes % 8 < 4
    new = [[[None, None], [None, None]] for _ in range(8)]
    for c in range(8):
        for half in range(2):
            columns = slice(128 * half, 128 * half + 128)
            if c < 4:
                at = (2 * c + half) * ZR
                near, far = take_pair(from_one, from_two, slice(at, at + ZR), even)
                if half == 1:
                    near = jnp.where(lanes < 96, near, 0.0)
                    far = jnp.where(lanes < 96, far, 0.0)
            else:
                pair = (c - 4) // 2
                at = 192 + pair * ZR
                near, far = take_pair(from_one, from_two, slice(at, at + ZR), even)
                if half == 0:
                    near = jnp.where(lanes >= 48, near, 0.0)
                    far = jnp.where(lanes >= 48, far, 0.0)
                else:
                    at = (2 * pair + 1) * ZR
                    rest = take_pair(from_one, from_two, slice(at, at + ZR), even)
                    rest = [jnp.where(lanes < 56, roll_lanes(value, -48), 0.0) for value in rest]
                    near = jnp.where(lanes < 48, near, rest[0])
                    far = jnp.where(lanes < 48, far, rest[1])
            if c >= 4 and c % 2 == 0:
                near = jnp.where(lower, near, 0.0)
                far = jnp.where(lower, 0.0, roll_lanes(far, 4))
            elif c >= 4:
                near = jnp.where(lower, roll_lanes(near, -4), 0.0)
                far = jnp.where(lower, 0.0, far)
            new[c][0][half] = window_in[0, c, :, columns] + near
            new[c][1][half] = window_in[1, c, :, columns] + far
            for window in range(2):
                window_ref[window, c, :, columns] = new[c][window][half]
    for c in range(4):
        near, far = new[c]
        plus = jnp.where(lanes < 64, roll_lanes(near[1], -32), roll_lanes(far[1], 32))
        minus = jnp.where(lanes < 64, near[0], roll_lanes(far[0], 64))
        put_pair(one_ref, two_ref, slice(c * ZR, (c + 1) * ZR), even_second, plus, minus)
    for pair in range(2):
        at = slice(96 + pair * ZR, 96 + (pair + 1) * ZR)
        even_c, odd_c = new[4 + 2 * pair], new[5 + 2 * pair]
        sides = []
        for half in (1, 0):
            sides.append(
                jnp.where(
                    lanes < 64,
                    jnp.where(lanes < 32, roll_lanes(even_c[0][half], -32), even_c[1][half]),
                    jnp.where(
                        lanes < 96, roll_lanes(odd_c[0][half], 32), roll_lanes(odd_c[1][half], 64)
                    ),
                )
            )
        put_pair(one_ref, two_ref, at, even_second, sides[0], sides[1])
    put_pair(
        one_ref, two_ref, slice(144, 216), even_second, bins_ref[0:72, :], bins_ref[72:144, :]
    )


def third_kernel(window_in, from_one, from_two, bins_ref, window_ref, message_ref):
    even = lax.axis_index("gy") % 2 == 0
    core = lax.axis_index("gz")
    lanes = lane_iota((ZR, 128))
    for window in range(2):
        for c in range(8):
            if c < 4:
                near, far = take_pair(from_one, from_two, slice(c * ZR, (c + 1) * ZR), even)
                near = jnp.where(
                    (lanes >= 32) & (lanes < 96),
                    roll_lanes(near, 32 if window == 0 else -32),
                    0.0,
                )
                far = jnp.where(lanes < 64, far if window == 0 else roll_lanes(far, 64), 0.0)
            else:
                at = slice(96 + (c - 4) // 2 * ZR, 96 + ((c - 4) // 2 + 1) * ZR)
                shift = (32, 0, -32, -64)[2 * (c % 2) + window]
                inside = (lanes >= 32) & (lanes < 64)
                near, far = take_pair(from_one, from_two, at, even)
                near = jnp.where(inside, roll_lanes(near, shift), 0.0)
                far = jnp.where(inside, roll_lanes(far, shift), 0.0)
            for half, extra in ((0, near), (1, far)):
                columns = slice(128 * half, 128 * half + 128)
                value = window_in[window, c, :, columns] + extra
                window_ref[window, c, :, columns] = value
                at = ((window * 8 + c) * 2 + half) * 8
                message_ref[at : at + 8, :] = jnp.where(core == 0, value[16:24], value[0:8])
    message_ref[256:328, :] = bins_ref[144:216, :]


def advance(sums):
    mass = jnp.maximum(sums[0], mass_floor)
    previous = [sums[1 + axis] / mass for axis in range(3)]
    velocity = [previous[0], previous[1], previous[2] - time_step * gravity]
    normal = sums[4:7]
    scale = 1.0 + (normal[0] * normal[0] + normal[1] * normal[1] + normal[2] * normal[2])
    dot = velocity[0] * normal[0] + velocity[1] * normal[1] + velocity[2] * normal[2]
    inward = jnp.minimum(dot, 0.0) / scale
    velocity = [velocity[axis] - inward * normal[axis] for axis in range(3)]
    dot = velocity[0] * normal[0] + velocity[1] * normal[1] + velocity[2] * normal[2]
    along = dot / scale
    damp = 1.0 - jnp.exp(-sums[7])
    velocity = [
        velocity[axis] - damp * (velocity[axis] - along * normal[axis]) for axis in range(3)
    ]
    return velocity + previous


def collect_kernel(
    window_in,
    from_z,
    x_one,
    x_two,
    y_one,
    y_two,
    state_ref,
    bin_count_ref,
    moved_ref,
    arrived_ref,
    data,
    fields,
    turned,
    table,
    picked,
    live,
    target,
):
    core = lax.axis_index("gz")
    row = lax.axis_index("gy")
    lanes = lane_iota((8, 128))
    subs = sub_iota((8, 128))
    lower_rows = subs < 4
    lower_lanes = lanes % 8 < 4

    for g in range(4):
        for c in range(16):
            data[c, 8 * g : 8 * g + 8, :] = state_ref[c, 8 * g : 8 * g + 8, :]
    even_first = lax.axis_index("gx") % 2 == 0
    even_second = lax.axis_index("gy") % 2 == 0
    arrivals = []
    for one_ref, two_ref, begin, even in ((x_one, x_two, 240, even_first), (y_one, y_two, 144, even_second)):
        pairs = [
            take_pair(one_ref, two_ref, slice(begin + 4 * part, begin + 4 * part + 4), even)
            for part in range(18)
        ]
        arrivals += [[pair[0] for pair in pairs], [pair[1] for pair in pairs]]
    arrivals.append([from_z[256 + 4 * part : 260 + 4 * part, :] for part in range(18)])
    for g, values in enumerate(arrivals):
        for c in range(16):
            data[c, 32 + 4 * g : 36 + 4 * g, :] = values[c]
        slot = lane_iota((4, 128)).astype(f32)
        live[32 + 4 * g : 36 + 4 * g, :] = jnp.where(slot < values[16], 1.0, 0.0)
        block = values[17].astype(jnp.int32)
        for member in range(4):
            target[4 * g + member] = block[member, 0]

    below = core == 0
    above = core == 1
    taken = [
        jnp.logical_not(lower_rows) & above,
        (lower_rows & above) | (jnp.logical_not(lower_rows) & below),
        lower_rows & below,
    ]
    for third in range(3):
        rows = slice(8 * third, 8 * third + 8)
        for half in range(2):
            columns = slice(128 * half, 128 * half + 128)
            sums = [[], []]
            for c in range(8):
                values = [window_in[b, c, rows, columns] for b in range(2)]
                for b in range(2):
                    at = ((b * 8 + c) * 2 + half) * 8
                    edge = pltpu.roll(from_z[at : at + 8, :], 4, 0)
                    values[b] = values[b] + jnp.where(taken[third], edge, 0.0)
                sums[0].append(
                    values[0] + jnp.where(lower_lanes, 0.0, roll_lanes(values[1], 4))
                )
                sums[1].append(
                    values[1] + jnp.where(lower_lanes, roll_lanes(values[0], -4), 0.0)
                )
            node_second = row * 16 + (lanes + 128 * half) // 8 - 6
            node_third = core * 12 + subs + 8 * third - 2
            inside = (
                (node_second >= 0) & (node_second < 128) & (node_third >= 0) & (node_third < 32)
            )
            for b in range(2):
                for c, value in enumerate(advance(sums[b])):
                    fields[b, c, rows, columns] = jnp.where(inside, value, 0.0)

    wide = lane_iota((ZR, 128))
    local = wide % 64
    node_first = (local % 8).astype(f32) - 2.0 - center
    node_second = (local // 8).astype(f32) - 2.0 - center
    for b in range(2):
        for c in range(6):
            low = fields[b, c, :, 0:128]
            high = fields[b, c, :, 128:256]
            shown = [
                jnp.where(wide < 64, roll_lanes(low, -32), roll_lanes(low, 32)),
                jnp.where(wide < 64, roll_lanes(low, 64), low),
                jnp.where(
                    wide < 64,
                    jnp.where(wide < 32, roll_lanes(low, 32), roll_lanes(high, 32)),
                    jnp.where(wide < 96, roll_lanes(low, -32), roll_lanes(high, 96)),
                ),
                jnp.where(wide < 64, high, roll_lanes(high, 64)),
            ]
            for second in range(4):
                turned[second, :, c, :] = shown[second]
                if c < 3:
                    turned[second, :, 6 + c, :] = shown[second] * node_first
                    turned[second, :, 9 + c, :] = shown[second] * node_second
        for second in range(4):
            value = turned[second].reshape(ZR * 16, 128)
            high, low = parts(value)
            table[4 * b + second, :, 0:128] = high
            table[4 * b + second, :, 128:256] = low

    nodes = subs.astype(f32) - 2.0

    def one_bin(index, column, third):
        def row_of(channel):
            return data[channel, pl.ds(index, 1), :]

        place = row_of(2)
        wx = spline(row_of(0), nodes)
        wy = spline(row_of(1), nodes)
        wz = spline(place, nodes)
        lever = wz * (nodes - place)
        high, low = parts(plane_of(wx, wy))
        right = jnp.concatenate([high, low, high, low], axis=0)
        left = table[column, pl.ds(64 * third, 128), :]
        values = jnp.dot(left, right, preferred_element_type=f32)
        first = values[0:8] * wz[0:1]
        second = values[8:16] * wz[0:1]
        moment = values[0:8] * lever[0:1]
        for k in range(1, 8):
            first = first + values[16 * k : 16 * k + 8] * wz[k : k + 1]
            second = second + values[16 * k + 8 : 16 * k + 16] * wz[k : k + 1]
            moment = moment + values[16 * k : 16 * k + 8] * lever[k : k + 1]
        picked[0:8, index, :] = first
        picked[8:16, index, :] = second
        picked[16:24, index, :] = moment

    def residents(step, carry):
        first = step // 4
        second = step % 4
        for third in range(4):
            index = step * 4 + third
            one_bin(index, step, third + core)
            count = bin_count_ref[first, second, third]
            live[pl.ds(index, 1), :] = jnp.where(lane_iota((1, 128)) < count, 1.0, 0.0)
        return carry

    lax.fori_loop(0, 8, residents, 0)

    def movers(step, carry):
        for member in range(2):
            block = target[2 * step + member]
            one_bin(32 + 2 * step + member, block // 4, block % 4 + core)
        return carry

    lax.fori_loop(0, 10, movers, 0)

    def finish(begin, size):
        rows = slice(begin, begin + size)
        valid = live[rows, :]
        old = [data[c, rows, :] for c in range(16)]
        got = [picked[c, rows, :] for c in range(19)]
        result = []
        for axis in range(3):
            result.append(old[axis] + time_step * got[axis])
        for axis in range(3):
            result.append(
                flip_ratio * (old[3 + axis] + got[axis] - got[3 + axis])
                + (1.0 - flip_ratio) * got[axis]
            )
        affine = []
        for axis in range(3):
            affine.append(4.0 * (got[6 + axis] - (old[0] - center) * got[axis]))
            affine.append(4.0 * (got[9 + axis] - (old[1] - center) * got[axis]))
            affine.append(4.0 * got[16 + axis])
        result += affine
        result.append(old[15] * (1.0 + time_step * (affine[0] + affine[4] + affine[8])))
        return [value * valid for value in result]

    for g in range(4):
        for c, value in enumerate(finish(8 * g, 8)):
            moved_ref[c, 8 * g : 8 * g + 8, :] = value
    for g in range(2):
        for c, value in enumerate(finish(32 + 8 * g, 8)):
            arrived_ref[c, 8 * g : 8 * g + 8, :] = value
    for c, value in enumerate(finish(48, 4)):
        arrived_ref[c, 16:20, :] = jnp.where(core == 1, value, 0.0)
        arrived_ref[c, 20:24, :] = jnp.where(core == 0, value, 0.0)


def pairs_along(axis, first, closed):
    count = lax.axis_size(axis)
    route = [(i, (i + 1) % count) for i in range(first, count, 2) if closed or i + 1 < count]
    return route + [(j, i) for i, j in route]


vmem = pl.BlockSpec(memory_space=pltpu.VMEM)
smem = pl.BlockSpec(memory_space=pltpu.SMEM)
limits = pltpu.CompilerParams(vmem_limit_bytes=48 * 1024 * 1024)
ample = pltpu.CompilerParams(vmem_limit_bytes=60 * 1024 * 1024)


def shape_of(*dims):
    return jax.ShapeDtypeStruct(dims, f32)


def body(
    state,
    bin_count,
    departing,
    depart_count,
    depart_block,
    cut_cell,
    quad_count,
    wall_id,
    cut_level,
    wall_normal,
    wall_friction,
):
    state_rows = state.reshape(16, 32, 128)
    leaving = departing.reshape(16, 24, 128)
    cut = [value.reshape(4, 128) for value in (cut_cell, quad_count, wall_id, cut_level)]
    depart_count = jnp.swapaxes(depart_count, 3, 4)
    depart_block = jnp.swapaxes(depart_block, 3, 4)
    operands = (
        state_rows,
        bin_count,
        leaving,
        depart_count,
        depart_block,
        *cut,
        wall_normal,
        wall_friction,
    )
    scalars = (1, 3, 4, 9, 10)
    window, one, two, bins = pl.pallas_call(
        deposit_kernel,
        out_shape=[
            shape_of(2, 8, ZR, LN),
            shape_of(XROWS, 128),
            shape_of(XROWS, 128),
            shape_of(3 * BINROWS, 128),
        ],
        in_specs=[pl.BlockSpec(memory_space=pltpu.HBM)] * 11,
        out_specs=[vmem] * 4,
        scratch_shapes=[
            (pltpu.SMEM if place in scalars else pltpu.VMEM)(value.shape, value.dtype)
            for place, value in enumerate(operands)
        ]
        + [
            pltpu.VMEM((16, 56, 128), f32),
            pltpu.VMEM((4, 5, 32, LN), f32),
            pltpu.SemaphoreType.DMA((11,)),
        ],
        compiler_params=ample,
        name="deposit",
    )(*operands)
    x_one = lax.ppermute(one, "gx", pairs_along("gx", 0, True))
    x_two = lax.ppermute(two, "gx", pairs_along("gx", 1, True))
    window, bins = pl.pallas_call(
        stage_kernel,
        out_shape=[shape_of(2, 8, ZR, LN), shape_of(3 * BINROWS, 128)],
        in_specs=[vmem] * 2,
        out_specs=[vmem] * 2,
        cost_estimate=pl.CostEstimate(flops=10**9, bytes_accessed=2**20, transcendentals=0),
        compiler_params=limits,
        name="stage",
    )(window, bins)
    window, one, two = pl.pallas_call(
        second_kernel,
        out_shape=[shape_of(2, 8, ZR, LN), shape_of(YROWS, 128), shape_of(YROWS, 128)],
        in_specs=[vmem] * 4,
        out_specs=[vmem] * 3,
        compiler_params=limits,
        name="take_x",
    )(window, x_one, x_two, bins)
    y_one = lax.ppermute(one, "gy", pairs_along("gy", 0, False))
    y_two = lax.ppermute(two, "gy", pairs_along("gy", 1, False))
    window, message = pl.pallas_call(
        third_kernel,
        out_shape=[shape_of(2, 8, ZR, LN), shape_of(ZROWS, 128)],
        in_specs=[vmem] * 4,
        out_specs=[vmem] * 2,
        compiler_params=limits,
        name="take_y",
    )(window, y_one, y_two, bins)
    from_z = lax.ppermute(message, "gz", [(0, 1), (1, 0)])
    moved, arrived = pl.pallas_call(
        collect_kernel,
        out_shape=[shape_of(16, 32, 128), shape_of(16, 24, 128)],
        in_specs=[vmem] * 7 + [smem],
        out_specs=[vmem] * 2,
        scratch_shapes=[
            pltpu.VMEM((16, 56, 128), f32),
            pltpu.VMEM((2, 6, ZR, LN), f32),
            pltpu.VMEM((4, ZR, 16, 128), f32),
            pltpu.VMEM((8, ZR * 16, 256), bf16),
            pltpu.VMEM((24, 56, 128), f32),
            pltpu.VMEM((56, 128), f32),
            pltpu.SMEM((20,), jnp.int32),
        ],
        compiler_params=limits,
        name="collect",
    )(
        window,
        from_z,
        x_one,
        x_two,
        y_one,
        y_two,
        state_rows,
        bin_count,
    )
    return moved.reshape(state.shape), arrived.reshape(departing.shape)


def solution(mesh):
    placed = (
        P(None, "gx", "gy", "gz", None),
        P("gx", "gy", "gz"),
        P(None, "gx", "gy", "gz", None, None, None),
        P("gx", "gy", "gz", None, None),
        P("gx", "gy", "gz", None, None),
        P("gx", "gy", "gz", None),
        P("gx", "gy", "gz", None),
        P("gx", "gy", "gz", None),
        P("gx", "gy", "gz", None),
        P(),
        P(),
    )
    return jax.shard_map(
        body,
        mesh=mesh,
        in_specs=placed,
        out_specs=(P(None, "gx", "gy", "gz", None), P(None, "gx", "gy", "gz", None, None, None)),
        check_vma=False,
    )
```

```python
import jax
import jax.numpy as jnp
import numpy as np
from jax import lax
from jax.experimental import pallas as pl
from jax.experimental.pallas import tpu as pltpu
from jax.sharding import PartitionSpec as P

time_step = 0.1
stiffness = 4.0
gravity = 2.0
flip_ratio = 0.95
mass_floor = 0.25
center = 1.5
quad_points = [
    [0.5, 0.5, 0.5],
    [0.2, 0.7, 0.35],
    [0.8, 0.3, 0.65],
    [0.35, 0.15, 0.85],
    [0.65, 0.85, 0.15],
    [0.1, 0.45, 0.55],
    [0.9, 0.55, 0.45],
    [0.45, 0.9, 0.75],
]
f32 = jnp.float32
bf16 = jnp.bfloat16

ZR = 24
LN = 256
BINROWS = 72
XROWS = 192 + 48 + BINROWS
YROWS = 96 + 48 + BINROWS
ZROWS = 256 + BINROWS


def lane_iota(shape):
    return lax.broadcasted_iota(jnp.int32, shape, len(shape) - 1)


def sub_iota(shape):
    return lax.broadcasted_iota(jnp.int32, shape, len(shape) - 2)


def spline(coord, nodes):
    distance = jnp.abs(coord - nodes)
    inner = 0.75 - distance * distance
    reach = jnp.maximum(1.5 - distance, 0.0)
    return jnp.where(distance < 0.5, inner, 0.5 * reach * reach)


def parts(value):
    high = value.astype(bf16)
    low = (value - high.astype(f32)).astype(bf16)
    return high, low


def plane_of(wx, wy):
    return jnp.concatenate([wy[y : y + 1] * wx for y in range(8)], axis=0)


def roll_lanes(value, shift):
    return pltpu.roll(value, shift % 128, 1)


def contact_terms(cell_ref, quad_ref, wall_ref, level_ref, normal_ref, friction_ref):
    cells = cell_ref[...]
    counts = quad_ref[...]
    walls = wall_ref[...]
    level = level_ref[...]
    normal = []
    for axis in range(3):
        part = jnp.zeros_like(level)
        for wall in range(4):
            part = jnp.where(walls == wall, normal_ref[wall, axis], part)
        normal.append(part)
    friction = jnp.zeros_like(level)
    for wall in range(4):
        friction = jnp.where(walls == wall, friction_ref[wall], friction)
    inverse = 1.0 / jnp.maximum(counts, 1).astype(f32)
    weights = [None] * 8
    for q, point in enumerate(quad_points):
        level_set = level + (normal[0] * point[0] + normal[1] * point[1] + normal[2] * point[2])
        cover = jnp.clip(0.5 - level_set, 0.0, 1.0)
        share = jnp.where(counts > q, cover * inverse, 0.0)
        for corner in range(8):
            factor = 1.0
            for axis in range(3):
                bit = (corner >> (2 - axis)) & 1
                factor *= point[axis] if bit else 1.0 - point[axis]
            term = share * factor
            weights[corner] = term if weights[corner] is None else weights[corner] + term
    return cells, weights, normal + [friction]


def contact_windows(cell_ref, quad_ref, wall_ref, level_ref, normal_ref, friction_ref):
    cells, weights, factors = contact_terms(
        cell_ref, quad_ref, wall_ref, level_ref, normal_ref, friction_ref
    )
    place_third = cells % 16 + 2 + 4 * lax.axis_index("gz")
    column = (cells // 16) % 16 * 8 + cells // 256
    rows = sub_iota((ZR, 128))
    bit_rows = sub_iota((128, 128))
    lefts_high = []
    lefts_low = []
    rights = []
    for tile in range(4):
        third = place_third[tile : tile + 1]
        first_row = rows == third
        second_row = rows == third + 1
        pieces_high = []
        pieces_low = []
        for pair in range(4):
            lower = weights[2 * pair][tile : tile + 1]
            upper = weights[2 * pair + 1][tile : tile + 1]
            for channel in range(4):
                factor = factors[channel][tile : tile + 1]
                value = jnp.where(
                    first_row, lower * factor, jnp.where(second_row, upper * factor, 0.0)
                )
                high, low = parts(value)
                pieces_high.append(high.astype(f32))
                pieces_low.append(low.astype(f32))
        lefts_high.append(jnp.concatenate(pieces_high, axis=0).astype(bf16))
        lefts_low.append(jnp.concatenate(pieces_low, axis=0).astype(bf16))
        rights.append(
            jnp.where(bit_rows == column[tile : tile + 1], 1.0, 0.0).astype(bf16)
        )
    left = jnp.concatenate(lefts_high + lefts_low, axis=1)
    right = jnp.concatenate(rights + rights, axis=1)
    touched = lax.dot_general(
        left, right, (((1,), (1,)), ((), ())), preferred_element_type=f32
    )
    lanes = lane_iota((4 * ZR, 128))
    first = lanes % 8
    result = [[None, None], [None, None]]
    for pair in range(4):
        dx, dy = pair >> 1, pair & 1
        block = touched[pair * 4 * ZR : (pair + 1) * 4 * ZR]
        near = jnp.where(first <= 5 - dx, block, 0.0)
        far = jnp.where(first >= 6 - dx, block, 0.0)
        for window, (value, shift) in enumerate(
            ((near, 50 + 8 * dy + dx), (far, 46 + 8 * dy + dx))
        ):
            turned = roll_lanes(value, shift)
            for half, piece in enumerate(
                (jnp.where(lanes >= shift, turned, 0.0), jnp.where(lanes < shift, turned, 0.0))
            ):
                known = result[window][half]
                result[window][half] = piece if known is None else known + piece
    return result


def deposit_kernel(*refs):
    inputs, (window_ref, one_ref, two_ref, bins_ref) = refs[:11], refs[11:15]
    even = lax.axis_index("gx") % 2 == 0
    copies, (data, total, semaphores) = refs[15:26], refs[26:]
    started = []
    for place in (5, 6, 7, 8, 9, 10, 0, 2, 1, 3, 4):
        started.append(
            pltpu.make_async_copy(inputs[place], copies[place], semaphores.at[place])
        )
        started[-1].start()
    state_ref, bin_count_ref, depart_ref, depart_count_ref, depart_block_ref = copies[:5]
    for window in (0, 3):
        total[window] = jnp.zeros((6, 32, LN), f32)
    for window in (1, 2):
        for third in (0, 5):
            total[window, third] = jnp.zeros((32, LN), f32)
    for copy in started[:6]:
        copy.wait()
    contact = contact_windows(*copies[5:])
    for copy in started[6:]:
        copy.wait()

    core = lax.axis_index("gz")
    size = 8
    groups = [(state_ref, 8 * g, 8 * g) for g in range(4)]
    groups += [(depart_ref, 8 * g, 32 + 8 * g) for g in range(3)]
    for ref, begin, place in groups:
        channel = [ref[c, begin : begin + size, :] for c in range(16)]
        pressure = time_step * 4.0 * stiffness * jnp.maximum(1.0 - channel[15], 0.0)
        spread = [channel[6 + e] + (pressure if e % 4 == 0 else 0.0) for e in range(9)]
        offset = [channel[axis] - center for axis in range(3)]
        for axis in range(3):
            data[axis, place : place + size, :] = channel[axis]
            data[3 + axis, place : place + size, :] = (
                channel[3 + axis]
                - spread[3 * axis] * offset[0]
                - spread[3 * axis + 1] * offset[1]
                - spread[3 * axis + 2] * offset[2]
            )
        for entry in range(9):
            data[6 + entry, place : place + size, :] = spread[entry]

    nodes = sub_iota((8, 128)).astype(f32) - 2.0
    slots = lane_iota((8, 128))
    lanes = lane_iota((32, 128))
    local = lane_iota((8, 128)) % 64
    node_first = (local % 8).astype(f32) - 2.0 - center
    node_second = (local // 8).astype(f32) - 2.0 - center
    node_third = nodes - center
    blank = jnp.zeros((64, 3 * 128), bf16)

    def one_bin(index, begin, count):
        def row(channel):
            return data[channel, pl.ds(index, 1), :]

        wx = spline(row(0), nodes)
        wy = spline(row(1), nodes)
        wz = jnp.where(slots < count, spline(row(2), nodes), 0.0)
        lifted = jnp.concatenate([wz] + [row(3 + c) * wz for c in range(12)], axis=0)
        lift_high, lift_low = parts(lifted)
        plane_high, plane_low = parts(plane_of(wx, wy))
        left = jnp.concatenate([lift_high, lift_high, lift_low], axis=1)
        right = jnp.concatenate([plane_high, plane_low, plane_high], axis=1)
        right = jnp.concatenate([right, blank], axis=0)
        moments = lax.dot_general(
            left, right, (((1,), (1,)), ((), ())), preferred_element_type=f32
        )
        sums = [moments[0:8]]
        for axis in range(3):
            at = 32 + 24 * axis
            sums.append(
                moments[8 + 8 * axis : 16 + 8 * axis]
                + moments[at : at + 8] * node_first
                + moments[at + 8 : at + 16] * node_second
                + moments[at + 16 : at + 24] * node_third
            )
        turned = pltpu.roll(jnp.concatenate(sums, axis=0), begin % 128, 1)
        inside = (lanes >= begin) & (lanes < begin + 64)
        beyond = (lanes >= begin - 128) & (lanes < begin - 64)
        return jnp.where(inside, turned, 0.0), jnp.where(beyond, turned, 0.0)

    def residents(step, carry):
        first = step // 4
        third = step % 4
        low, high = None, None
        for second in range(4):
            one, two = one_bin(
                first * 16 + second * 4 + third,
                32 * (second + 1),
                bin_count_ref[first, second, third],
            )
            low = one if low is None else low + one
            high = two if high is None else high + two
        total[first + 1, third + 1, :, 0:128] = low
        total[first + 1, third + 1, :, 128:256] = high
        return carry

    lax.fori_loop(0, 8, residents, 0, unroll=4)

    def leavers(member, carry):
        for direction in range(5):
            block = depart_block_ref[0, 0, 0, member, direction]
            count = depart_count_ref[0, 0, 0, member, direction]
            index = 32 + direction * 4 + member
            window = block // 16 + 1
            begin = 32 * (block // 4 % 4 + 1)
            third = block % 4 + 1
            if direction < 2:
                window = 3 if direction == 0 else 0
            elif direction < 4:
                begin = 160 if direction == 2 else 0
            else:
                block = depart_block_ref[0, 0, 0, member, 4 + core]
                count = depart_count_ref[0, 0, 0, member, 4 + core]
                index = 48 + 4 * core + member
                window = block // 16 + 1
                begin = 32 * (block // 4 % 4 + 1)
                third = 5 - 5 * core
            one, two = one_bin(index, begin, count)
            total[window, third, :, 0:128] += one
            total[window, third, :, 128:256] += two
        return carry

    lax.fori_loop(0, 4, leavers, 0, unroll=4)

    lower_rows = sub_iota((8, 128)) < 4
    lower_lanes = lane_iota((8, 128)) % 8 < 4
    lower_tall = lane_iota((ZR, 128)) % 8 < 4
    pieces = {}
    for half in range(2):
        columns = slice(128 * half, 128 * half + 128)
        for c in range(4):
            folded = []
            for window in range(4):
                piece = [
                    total[window, third + 1 - core, 8 * c : 8 * c + 8, columns]
                    for third in range(5)
                ]
                one = pltpu.roll(piece[1], 4, 0)
                three = pltpu.roll(piece[3], 4, 0)
                folded.append(
                    jnp.concatenate(
                        [
                            piece[0] + jnp.where(lower_rows, 0.0, one),
                            piece[2] + jnp.where(lower_rows, one, three),
                            piece[4] + jnp.where(lower_rows, three, 0.0),
                        ],
                        axis=0,
                    )
                )
            window_ref[0, c, :, columns] = folded[1] + jnp.where(
                lower_tall, roll_lanes(folded[0], -4), 0.0
            )
            window_ref[1, c, :, columns] = folded[2] + jnp.where(
                lower_tall, 0.0, roll_lanes(folded[3], 4)
            )
            at = (2 * c + half) * ZR
            pieces[at] = [
                folded[3] + jnp.where(lower_tall, roll_lanes(folded[2], -4), 0.0),
                folded[0] + jnp.where(lower_tall, 0.0, roll_lanes(folded[1], 4)),
            ]
            near = contact[0][half][ZR * c : ZR * c + ZR]
            far = contact[1][half][ZR * c : ZR * c + ZR]
            window_ref[0, 4 + c, :, columns] = near
            window_ref[1, 4 + c, :, columns] = far
    tall = lane_iota((ZR, 128))
    for pair in range(2):
        first_c = slice(2 * pair * ZR, (2 * pair + 1) * ZR)
        second_c = slice((2 * pair + 1) * ZR, (2 * pair + 2) * ZR)
        near = [
            jnp.where(lower_tall, contact[0][half][first_c], roll_lanes(contact[0][half][second_c], 4))
            for half in range(2)
        ]
        far = [
            jnp.where(lower_tall, roll_lanes(contact[1][half][first_c], -4), contact[1][half][second_c])
            for half in range(2)
        ]
        main = 192 + pair * ZR
        rest = (2 * pair + 1) * ZR
        pieces[main] = []
        for side, packed in enumerate((far, near)):
            pieces[main].append(jnp.where(tall >= 48, packed[0], packed[1]))
            pieces[rest][side] = jnp.where(
                (tall >= 96) & (tall < 104), roll_lanes(packed[1], 48), pieces[rest][side]
            )
    for at, (plus, minus) in pieces.items():
        put_pair(one_ref, two_ref, slice(at, at + ZR), even, plus, minus)
    plus = bins_of(depart_ref, depart_count_ref, depart_block_ref, 0)
    minus = bins_of(depart_ref, depart_count_ref, depart_block_ref, 1)
    for part in range(18):
        at = 240 + 4 * part
        put_pair(one_ref, two_ref, slice(at, at + 4), even, plus[part], minus[part])
    south = bins_of(depart_ref, depart_count_ref, depart_block_ref, 2)
    north = bins_of(depart_ref, depart_count_ref, depart_block_ref, 3)
    up = bins_of(depart_ref, depart_count_ref, depart_block_ref, 4)
    down = bins_of(depart_ref, depart_count_ref, depart_block_ref, 5)
    for part in range(18):
        bins_ref[4 * part : 4 * part + 4, :] = south[part]
        bins_ref[72 + 4 * part : 76 + 4 * part, :] = north[part]
        bins_ref[144 + 4 * part : 148 + 4 * part, :] = jnp.where(core == 0, up[part], down[part])


def bins_of(depart_ref, depart_count_ref, depart_block_ref, direction):
    values = [depart_ref[c, 4 * direction : 4 * direction + 4, :] for c in range(16)]
    row = sub_iota((4, 128))
    for ref in (depart_count_ref, depart_block_ref):
        value = jnp.zeros((4, 128), jnp.int32)
        for member in range(4):
            value = jnp.where(row == member, ref[0, 0, 0, member, direction], value)
        values.append(value.astype(f32))
    return values


def put_pair(one_ref, two_ref, at, even, plus, minus):
    one_ref[at, :] = jnp.where(even, plus, minus)
    two_ref[at, :] = jnp.where(even, minus, plus)


def take_pair(one_ref, two_ref, at, even):
    one, two = one_ref[at, :], two_ref[at, :]
    return jnp.where(even, two, one), jnp.where(even, one, two)


def stage_kernel(window_in, bins_in, window_ref, bins_ref):
    window_ref[...] = window_in[...]
    bins_ref[...] = bins_in[...]


def second_kernel(window_in, from_one, from_two, bins_ref, window_ref, one_ref, two_ref):
    even = lax.axis_index("gx") % 2 == 0
    even_second = lax.axis_index("gy") % 2 == 0
    lanes = lane_iota((ZR, 128))
    lower = lanes % 8 < 4
    new = [[[None, None], [None, None]] for _ in range(8)]
    for c in range(8):
        for half in range(2):
            columns = slice(128 * half, 128 * half + 128)
            if c < 4:
                at = (2 * c + half) * ZR
                near, far = take_pair(from_one, from_two, slice(at, at + ZR), even)
                if half == 1:
                    near = jnp.where(lanes < 96, near, 0.0)
                    far = jnp.where(lanes < 96, far, 0.0)
            else:
                pair = (c - 4) // 2
                at = 192 + pair * ZR
                near, far = take_pair(from_one, from_two, slice(at, at + ZR), even)
                if half == 0:
                    near = jnp.where(lanes >= 48, near, 0.0)
                    far = jnp.where(lanes >= 48, far, 0.0)
                else:
                    at = (2 * pair + 1) * ZR
                    rest = take_pair(from_one, from_two, slice(at, at + ZR), even)
                    rest = [jnp.where(lanes < 56, roll_lanes(value, -48), 0.0) for value in rest]
                    near = jnp.where(lanes < 48, near, rest[0])
                    far = jnp.where(lanes < 48, far, rest[1])
            if c >= 4 and c % 2 == 0:
                near = jnp.where(lower, near, 0.0)
                far = jnp.where(lower, 0.0, roll_lanes(far, 4))
            elif c >= 4:
                near = jnp.where(lower, roll_lanes(near, -4), 0.0)
                far = jnp.where(lower, 0.0, far)
            new[c][0][half] = window_in[0, c, :, columns] + near
            new[c][1][half] = window_in[1, c, :, columns] + far
            for window in range(2):
                window_ref[window, c, :, columns] = new[c][window][half]
    for c in range(4):
        near, far = new[c]
        plus = jnp.where(lanes < 64, roll_lanes(near[1], -32), roll_lanes(far[1], 32))
        minus = jnp.where(lanes < 64, near[0], roll_lanes(far[0], 64))
        put_pair(one_ref, two_ref, slice(c * ZR, (c + 1) * ZR), even_second, plus, minus)
    for pair in range(2):
        at = slice(96 + pair * ZR, 96 + (pair + 1) * ZR)
        even_c, odd_c = new[4 + 2 * pair], new[5 + 2 * pair]
        sides = []
        for half in (1, 0):
            sides.append(
                jnp.where(
                    lanes < 64,
                    jnp.where(lanes < 32, roll_lanes(even_c[0][half], -32), even_c[1][half]),
                    jnp.where(
                        lanes < 96, roll_lanes(odd_c[0][half], 32), roll_lanes(odd_c[1][half], 64)
                    ),
                )
            )
        put_pair(one_ref, two_ref, at, even_second, sides[0], sides[1])
    put_pair(
        one_ref, two_ref, slice(144, 216), even_second, bins_ref[0:72, :], bins_ref[72:144, :]
    )


def third_kernel(window_in, from_one, from_two, bins_ref, window_ref, message_ref):
    even = lax.axis_index("gy") % 2 == 0
    core = lax.axis_index("gz")
    lanes = lane_iota((ZR, 128))
    for window in range(2):
        for c in range(8):
            if c < 4:
                near, far = take_pair(from_one, from_two, slice(c * ZR, (c + 1) * ZR), even)
                near = jnp.where(
                    (lanes >= 32) & (lanes < 96),
                    roll_lanes(near, 32 if window == 0 else -32),
                    0.0,
                )
                far = jnp.where(lanes < 64, far if window == 0 else roll_lanes(far, 64), 0.0)
            else:
                at = slice(96 + (c - 4) // 2 * ZR, 96 + ((c - 4) // 2 + 1) * ZR)
                shift = (32, 0, -32, -64)[2 * (c % 2) + window]
                inside = (lanes >= 32) & (lanes < 64)
                near, far = take_pair(from_one, from_two, at, even)
                near = jnp.where(inside, roll_lanes(near, shift), 0.0)
                far = jnp.where(inside, roll_lanes(far, shift), 0.0)
            for half, extra in ((0, near), (1, far)):
                columns = slice(128 * half, 128 * half + 128)
                value = window_in[window, c, :, columns] + extra
                window_ref[window, c, :, columns] = value
                at = ((window * 8 + c) * 2 + half) * 8
                message_ref[at : at + 8, :] = jnp.where(core == 0, value[16:24], value[0:8])
    message_ref[256:328, :] = bins_ref[144:216, :]


def advance(sums):
    mass = jnp.maximum(sums[0], mass_floor)
    previous = [sums[1 + axis] / mass for axis in range(3)]
    velocity = [previous[0], previous[1], previous[2] - time_step * gravity]
    normal = sums[4:7]
    scale = 1.0 + (normal[0] * normal[0] + normal[1] * normal[1] + normal[2] * normal[2])
    dot = velocity[0] * normal[0] + velocity[1] * normal[1] + velocity[2] * normal[2]
    inward = jnp.minimum(dot, 0.0) / scale
    velocity = [velocity[axis] - inward * normal[axis] for axis in range(3)]
    dot = velocity[0] * normal[0] + velocity[1] * normal[1] + velocity[2] * normal[2]
    along = dot / scale
    damp = 1.0 - jnp.exp(-sums[7])
    velocity = [
        velocity[axis] - damp * (velocity[axis] - along * normal[axis]) for axis in range(3)
    ]
    return velocity + previous


def collect_kernel(
    window_in,
    from_z,
    x_one,
    x_two,
    y_one,
    y_two,
    state_ref,
    bin_count_ref,
    moved_ref,
    arrived_ref,
    data,
    fields,
    turned,
    table,
    picked,
    live,
    target,
):
    core = lax.axis_index("gz")
    row = lax.axis_index("gy")
    lanes = lane_iota((8, 128))
    subs = sub_iota((8, 128))
    lower_rows = subs < 4
    lower_lanes = lanes % 8 < 4

    for g in range(4):
        for c in range(16):
            data[c, 8 * g : 8 * g + 8, :] = state_ref[c, 8 * g : 8 * g + 8, :]
    even_first = lax.axis_index("gx") % 2 == 0
    even_second = lax.axis_index("gy") % 2 == 0
    arrivals = []
    for one_ref, two_ref, begin, even in ((x_one, x_two, 240, even_first), (y_one, y_two, 144, even_second)):
        pairs = [
            take_pair(one_ref, two_ref, slice(begin + 4 * part, begin + 4 * part + 4), even)
            for part in range(18)
        ]
        arrivals += [[pair[0] for pair in pairs], [pair[1] for pair in pairs]]
    arrivals.append([from_z[256 + 4 * part : 260 + 4 * part, :] for part in range(18)])
    for g, values in enumerate(arrivals):
        for c in range(16):
            data[c, 32 + 4 * g : 36 + 4 * g, :] = values[c]
        slot = lane_iota((4, 128)).astype(f32)
        live[32 + 4 * g : 36 + 4 * g, :] = jnp.where(slot < values[16], 1.0, 0.0)
        block = values[17].astype(jnp.int32)
        for member in range(4):
            target[4 * g + member] = block[member, 0]

    below = core == 0
    above = core == 1
    taken = [
        jnp.logical_not(lower_rows) & above,
        (lower_rows & above) | (jnp.logical_not(lower_rows) & below),
        lower_rows & below,
    ]
    for third in range(3):
        rows = slice(8 * third, 8 * third + 8)
        for half in range(2):
            columns = slice(128 * half, 128 * half + 128)
            sums = [[], []]
            for c in range(8):
                values = [window_in[b, c, rows, columns] for b in range(2)]
                for b in range(2):
                    at = ((b * 8 + c) * 2 + half) * 8
                    edge = pltpu.roll(from_z[at : at + 8, :], 4, 0)
                    values[b] = values[b] + jnp.where(taken[third], edge, 0.0)
                sums[0].append(
                    values[0] + jnp.where(lower_lanes, 0.0, roll_lanes(values[1], 4))
                )
                sums[1].append(
                    values[1] + jnp.where(lower_lanes, roll_lanes(values[0], -4), 0.0)
                )
            node_second = row * 16 + (lanes + 128 * half) // 8 - 6
            node_third = core * 12 + subs + 8 * third - 2
            inside = (
                (node_second >= 0) & (node_second < 128) & (node_third >= 0) & (node_third < 32)
            )
            for b in range(2):
                for c, value in enumerate(advance(sums[b])):
                    fields[b, c, rows, columns] = jnp.where(inside, value, 0.0)

    wide = lane_iota((ZR, 128))
    local = wide % 64
    node_first = (local % 8).astype(f32) - 2.0 - center
    node_second = (local // 8).astype(f32) - 2.0 - center
    for b in range(2):
        for c in range(6):
            low = fields[b, c, :, 0:128]
            high = fields[b, c, :, 128:256]
            shown = [
                jnp.where(wide < 64, roll_lanes(low, -32), roll_lanes(low, 32)),
                jnp.where(wide < 64, roll_lanes(low, 64), low),
                jnp.where(
                    wide < 64,
                    jnp.where(wide < 32, roll_lanes(low, 32), roll_lanes(high, 32)),
                    jnp.where(wide < 96, roll_lanes(low, -32), roll_lanes(high, 96)),
                ),
                jnp.where(wide < 64, high, roll_lanes(high, 64)),
            ]
            for second in range(4):
                turned[second, :, c, :] = shown[second]
                if c < 3:
                    turned[second, :, 6 + c, :] = shown[second] * node_first
                    turned[second, :, 9 + c, :] = shown[second] * node_second
        for second in range(4):
            value = turned[second].reshape(ZR * 16, 128)
            high, low = parts(value)
            table[4 * b + second, :, 0:128] = high
            table[4 * b + second, :, 128:256] = low

    nodes = subs.astype(f32) - 2.0

    def one_bin(index, column, third):
        def row_of(channel):
            return data[channel, pl.ds(index, 1), :]

        place = row_of(2)
        wx = spline(row_of(0), nodes)
        wy = spline(row_of(1), nodes)
        wz = spline(place, nodes)
        lever = wz * (nodes - place)
        high, low = parts(plane_of(wx, wy))
        right = jnp.concatenate([high, low, high, low], axis=0)
        left = table[column, pl.ds(64 * third, 128), :]
        values = jnp.dot(left, right, preferred_element_type=f32)
        first = values[0:8] * wz[0:1]
        second = values[8:16] * wz[0:1]
        moment = values[0:8] * lever[0:1]
        for k in range(1, 8):
            first = first + values[16 * k : 16 * k + 8] * wz[k : k + 1]
            second = second + values[16 * k + 8 : 16 * k + 16] * wz[k : k + 1]
            moment = moment + values[16 * k : 16 * k + 8] * lever[k : k + 1]
        picked[0:8, index, :] = first
        picked[8:16, index, :] = second
        picked[16:24, index, :] = moment

    def residents(step, carry):
        first = step // 4
        second = step % 4
        for third in range(4):
            index = step * 4 + third
            one_bin(index, step, third + core)
            count = bin_count_ref[first, second, third]
            live[pl.ds(index, 1), :] = jnp.where(lane_iota((1, 128)) < count, 1.0, 0.0)
        return carry

    lax.fori_loop(0, 8, residents, 0, unroll=4)

    def movers(step, carry):
        for member in range(4):
            block = target[4 * step + member]
            one_bin(32 + 4 * step + member, block // 4, block % 4 + core)
        return carry

    lax.fori_loop(0, 5, movers, 0, unroll=5)

    def finish(begin, size):
        rows = slice(begin, begin + size)
        valid = live[rows, :]
        old = [data[c, rows, :] for c in range(16)]
        got = [picked[c, rows, :] for c in range(19)]
        result = []
        for axis in range(3):
            result.append(old[axis] + time_step * got[axis])
        for axis in range(3):
            result.append(
                flip_ratio * (old[3 + axis] + got[axis] - got[3 + axis])
                + (1.0 - flip_ratio) * got[axis]
            )
        affine = []
        for axis in range(3):
            affine.append(4.0 * (got[6 + axis] - (old[0] - center) * got[axis]))
            affine.append(4.0 * (got[9 + axis] - (old[1] - center) * got[axis]))
            affine.append(4.0 * got[16 + axis])
        result += affine
        result.append(old[15] * (1.0 + time_step * (affine[0] + affine[4] + affine[8])))
        return [value * valid for value in result]

    for g in range(4):
        for c, value in enumerate(finish(8 * g, 8)):
            moved_ref[c, 8 * g : 8 * g + 8, :] = value
    for g in range(2):
        for c, value in enumerate(finish(32 + 8 * g, 8)):
            arrived_ref[c, 8 * g : 8 * g + 8, :] = value
    for c, value in enumerate(finish(48, 4)):
        arrived_ref[c, 16:20, :] = jnp.where(core == 1, value, 0.0)
        arrived_ref[c, 20:24, :] = jnp.where(core == 0, value, 0.0)


def pairs_along(axis, first, closed):
    count = lax.axis_size(axis)
    route = [(i, (i + 1) % count) for i in range(first, count, 2) if closed or i + 1 < count]
    return route + [(j, i) for i, j in route]


vmem = pl.BlockSpec(memory_space=pltpu.VMEM)
smem = pl.BlockSpec(memory_space=pltpu.SMEM)
limits = pltpu.CompilerParams(vmem_limit_bytes=48 * 1024 * 1024)
ample = pltpu.CompilerParams(vmem_limit_bytes=60 * 1024 * 1024)


def shape_of(*dims):
    return jax.ShapeDtypeStruct(dims, f32)


def body(
    state,
    bin_count,
    departing,
    depart_count,
    depart_block,
    cut_cell,
    quad_count,
    wall_id,
    cut_level,
    wall_normal,
    wall_friction,
):
    state_rows = state.reshape(16, 32, 128)
    leaving = departing.reshape(16, 24, 128)
    cut = [value.reshape(4, 128) for value in (cut_cell, quad_count, wall_id, cut_level)]
    depart_count = jnp.swapaxes(depart_count, 3, 4)
    depart_block = jnp.swapaxes(depart_block, 3, 4)
    operands = (
        state_rows,
        bin_count,
        leaving,
        depart_count,
        depart_block,
        *cut,
        wall_normal,
        wall_friction,
    )
    scalars = (1, 3, 4, 9, 10)
    window, one, two, bins = pl.pallas_call(
        deposit_kernel,
        out_shape=[
            shape_of(2, 8, ZR, LN),
            shape_of(XROWS, 128),
            shape_of(XROWS, 128),
            shape_of(3 * BINROWS, 128),
        ],
        in_specs=[pl.BlockSpec(memory_space=pltpu.HBM)] * 11,
        out_specs=[vmem] * 4,
        scratch_shapes=[
            (pltpu.SMEM if place in scalars else pltpu.VMEM)(value.shape, value.dtype)
            for place, value in enumerate(operands)
        ]
        + [
            pltpu.VMEM((16, 56, 128), f32),
            pltpu.VMEM((4, 6, 32, LN), f32),
            pltpu.SemaphoreType.DMA((11,)),
        ],
        compiler_params=ample,
        name="deposit",
    )(*operands)
    x_one = lax.ppermute(one, "gx", pairs_along("gx", 0, True))
    x_two = lax.ppermute(two, "gx", pairs_along("gx", 1, True))
    window, bins = pl.pallas_call(
        stage_kernel,
        out_shape=[shape_of(2, 8, ZR, LN), shape_of(3 * BINROWS, 128)],
        in_specs=[vmem] * 2,
        out_specs=[vmem] * 2,
        cost_estimate=pl.CostEstimate(flops=10**9, bytes_accessed=2**20, transcendentals=0),
        compiler_params=limits,
        name="stage",
    )(window, bins)
    window, one, two = pl.pallas_call(
        second_kernel,
        out_shape=[shape_of(2, 8, ZR, LN), shape_of(YROWS, 128), shape_of(YROWS, 128)],
        in_specs=[vmem] * 4,
        out_specs=[vmem] * 3,
        compiler_params=limits,
        name="take_x",
    )(window, x_one, x_two, bins)
    y_one = lax.ppermute(one, "gy", pairs_along("gy", 0, False))
    y_two = lax.ppermute(two, "gy", pairs_along("gy", 1, False))
    window, message = pl.pallas_call(
        third_kernel,
        out_shape=[shape_of(2, 8, ZR, LN), shape_of(ZROWS, 128)],
        in_specs=[vmem] * 4,
        out_specs=[vmem] * 2,
        compiler_params=limits,
        name="take_y",
    )(window, y_one, y_two, bins)
    from_z = lax.ppermute(message, "gz", [(0, 1), (1, 0)])
    moved, arrived = pl.pallas_call(
        collect_kernel,
        out_shape=[shape_of(16, 32, 128), shape_of(16, 24, 128)],
        in_specs=[vmem] * 7 + [smem],
        out_specs=[vmem] * 2,
        scratch_shapes=[
            pltpu.VMEM((16, 56, 128), f32),
            pltpu.VMEM((2, 6, ZR, LN), f32),
            pltpu.VMEM((4, ZR, 16, 128), f32),
            pltpu.VMEM((8, ZR * 16, 256), bf16),
            pltpu.VMEM((24, 56, 128), f32),
            pltpu.VMEM((56, 128), f32),
            pltpu.SMEM((20,), jnp.int32),
        ],
        compiler_params=limits,
        name="collect",
    )(
        window,
        from_z,
        x_one,
        x_two,
        y_one,
        y_two,
        state_rows,
        bin_count,
    )
    return moved.reshape(state.shape), arrived.reshape(departing.shape)


def solution(mesh):
    placed = (
        P(None, "gx", "gy", "gz", None),
        P("gx", "gy", "gz"),
        P(None, "gx", "gy", "gz", None, None, None),
        P("gx", "gy", "gz", None, None),
        P("gx", "gy", "gz", None, None),
        P("gx", "gy", "gz", None),
        P("gx", "gy", "gz", None),
        P("gx", "gy", "gz", None),
        P("gx", "gy", "gz", None),
        P(),
        P(),
    )
    return jax.shard_map(
        body,
        mesh=mesh,
        in_specs=placed,
        out_specs=(P(None, "gx", "gy", "gz", None), P(None, "gx", "gy", "gz", None, None, None)),
        check_vma=False,
    )
```

```python
import jax
import jax.numpy as jnp
import numpy as np
from jax import lax
from jax.experimental import pallas as pl
from jax.experimental.pallas import tpu as pltpu
from jax.sharding import PartitionSpec as P

time_step = 0.1
stiffness = 4.0
gravity = 2.0
flip_ratio = 0.95
mass_floor = 0.25
center = 1.5
quad_points = [
    [0.5, 0.5, 0.5],
    [0.2, 0.7, 0.35],
    [0.8, 0.3, 0.65],
    [0.35, 0.15, 0.85],
    [0.65, 0.85, 0.15],
    [0.1, 0.45, 0.55],
    [0.9, 0.55, 0.45],
    [0.45, 0.9, 0.75],
]
f32 = jnp.float32
bf16 = jnp.bfloat16

ZR = 24
LN = 256
CARRIED = (0, 1, 2, 3, 4, 5, 15)
PARTS = 9
BINROWS = 40
XROWS = 192 + 48 + BINROWS
YROWS = 96 + 48 + BINROWS
ZROWS = 256 + BINROWS


def lane_iota(shape):
    return lax.broadcasted_iota(jnp.int32, shape, len(shape) - 1)


def sub_iota(shape):
    return lax.broadcasted_iota(jnp.int32, shape, len(shape) - 2)


def spline(coord, nodes):
    distance = jnp.abs(coord - nodes)
    inner = 0.75 - distance * distance
    reach = jnp.maximum(1.5 - distance, 0.0)
    return jnp.where(distance < 0.5, inner, 0.5 * reach * reach)


def parts(value):
    high = value.astype(bf16)
    low = (value - high.astype(f32)).astype(bf16)
    return high, low


def plane_of(wx, wy):
    return jnp.concatenate([wy[y : y + 1] * wx for y in range(8)], axis=0)


def roll_lanes(value, shift):
    return pltpu.roll(value, shift % 128, 1)


def contact_terms(cell_ref, quad_ref, wall_ref, level_ref, normal_ref, friction_ref):
    cells = cell_ref[...]
    counts = quad_ref[...]
    walls = wall_ref[...]
    level = level_ref[...]
    normal = []
    for axis in range(3):
        part = jnp.zeros_like(level)
        for wall in range(4):
            part = jnp.where(walls == wall, normal_ref[wall, axis], part)
        normal.append(part)
    friction = jnp.zeros_like(level)
    for wall in range(4):
        friction = jnp.where(walls == wall, friction_ref[wall], friction)
    inverse = 1.0 / jnp.maximum(counts, 1).astype(f32)
    weights = [None] * 8
    for q, point in enumerate(quad_points):
        level_set = level + (normal[0] * point[0] + normal[1] * point[1] + normal[2] * point[2])
        cover = jnp.clip(0.5 - level_set, 0.0, 1.0)
        share = jnp.where(counts > q, cover * inverse, 0.0)
        for corner in range(8):
            factor = 1.0
            for axis in range(3):
                bit = (corner >> (2 - axis)) & 1
                factor *= point[axis] if bit else 1.0 - point[axis]
            term = share * factor
            weights[corner] = term if weights[corner] is None else weights[corner] + term
    return cells, weights, normal + [friction]


def contact_windows(cell_ref, quad_ref, wall_ref, level_ref, normal_ref, friction_ref):
    cells, weights, factors = contact_terms(
        cell_ref, quad_ref, wall_ref, level_ref, normal_ref, friction_ref
    )
    place_third = cells % 16 + 2 + 4 * lax.axis_index("gz")
    column = (cells // 16) % 16 * 8 + cells // 256
    rows = sub_iota((ZR, 128))
    bit_rows = sub_iota((128, 128))
    lefts_high = []
    lefts_low = []
    rights = []
    for tile in range(4):
        third = place_third[tile : tile + 1]
        first_row = rows == third
        second_row = rows == third + 1
        pieces_high = []
        pieces_low = []
        for pair in range(4):
            lower = weights[2 * pair][tile : tile + 1]
            upper = weights[2 * pair + 1][tile : tile + 1]
            for channel in range(4):
                factor = factors[channel][tile : tile + 1]
                value = jnp.where(
                    first_row, lower * factor, jnp.where(second_row, upper * factor, 0.0)
                )
                high, low = parts(value)
                pieces_high.append(high.astype(f32))
                pieces_low.append(low.astype(f32))
        lefts_high.append(jnp.concatenate(pieces_high, axis=0).astype(bf16))
        lefts_low.append(jnp.concatenate(pieces_low, axis=0).astype(bf16))
        rights.append(
            jnp.where(bit_rows == column[tile : tile + 1], 1.0, 0.0).astype(bf16)
        )
    left = jnp.concatenate(lefts_high + lefts_low, axis=1)
    right = jnp.concatenate(rights + rights, axis=1)
    touched = lax.dot_general(
        left, right, (((1,), (1,)), ((), ())), preferred_element_type=f32
    )
    lanes = lane_iota((4 * ZR, 128))
    first = lanes % 8
    result = [[None, None], [None, None]]
    for pair in range(4):
        dx, dy = pair >> 1, pair & 1
        block = touched[pair * 4 * ZR : (pair + 1) * 4 * ZR]
        near = jnp.where(first <= 5 - dx, block, 0.0)
        far = jnp.where(first >= 6 - dx, block, 0.0)
        for window, (value, shift) in enumerate(
            ((near, 50 + 8 * dy + dx), (far, 46 + 8 * dy + dx))
        ):
            turned = roll_lanes(value, shift)
            for half, piece in enumerate(
                (jnp.where(lanes >= shift, turned, 0.0), jnp.where(lanes < shift, turned, 0.0))
            ):
                known = result[window][half]
                result[window][half] = piece if known is None else known + piece
    return result


def deposit_kernel(*refs):
    inputs, (window_ref, one_ref, two_ref, bins_ref) = refs[:11], refs[11:15]
    even = lax.axis_index("gx") % 2 == 0
    copies, (data, total, semaphores) = refs[15:26], refs[26:]
    started = []
    for place in (5, 6, 7, 8, 9, 10, 0, 2, 1, 3, 4):
        started.append(
            pltpu.make_async_copy(inputs[place], copies[place], semaphores.at[place])
        )
        started[-1].start()
    state_ref, bin_count_ref, depart_ref, depart_count_ref, depart_block_ref = copies[:5]
    for window in (0, 3):
        total[window] = jnp.zeros((6, 32, LN), f32)
    for window in (1, 2):
        for third in (0, 5):
            total[window, third] = jnp.zeros((32, LN), f32)
    for copy in started[:6]:
        copy.wait()
    contact = contact_windows(*copies[5:])
    for copy in started[6:]:
        copy.wait()

    core = lax.axis_index("gz")
    size = 8
    groups = [(state_ref, 8 * g, 8 * g) for g in range(4)]
    groups += [(depart_ref, 8 * g, 32 + 8 * g) for g in range(3)]
    for ref, begin, place in groups:
        channel = [ref[c, begin : begin + size, :] for c in range(16)]
        pressure = time_step * 4.0 * stiffness * jnp.maximum(1.0 - channel[15], 0.0)
        spread = [channel[6 + e] + (pressure if e % 4 == 0 else 0.0) for e in range(9)]
        offset = [channel[axis] - center for axis in range(3)]
        for axis in range(3):
            data[axis, place : place + size, :] = channel[axis]
            data[3 + axis, place : place + size, :] = (
                channel[3 + axis]
                - spread[3 * axis] * offset[0]
                - spread[3 * axis + 1] * offset[1]
                - spread[3 * axis + 2] * offset[2]
            )
        for entry in range(9):
            data[6 + entry, place : place + size, :] = spread[entry]

    nodes = sub_iota((8, 128)).astype(f32) - 2.0
    slots = lane_iota((8, 128))
    lanes = lane_iota((32, 128))
    local = lane_iota((8, 128)) % 64
    node_first = (local % 8).astype(f32) - 2.0 - center
    node_second = (local // 8).astype(f32) - 2.0 - center
    node_third = nodes - center
    blank = jnp.zeros((64, 3 * 128), bf16)

    def one_bin(index, begin, count):
        def row(channel):
            return data[channel, pl.ds(index, 1), :]

        wx = spline(row(0), nodes)
        wy = spline(row(1), nodes)
        wz = jnp.where(slots < count, spline(row(2), nodes), 0.0)
        lifted = jnp.concatenate([wz] + [row(3 + c) * wz for c in range(12)], axis=0)
        lift_high, lift_low = parts(lifted)
        plane_high, plane_low = parts(plane_of(wx, wy))
        left = jnp.concatenate([lift_high, lift_high, lift_low], axis=1)
        right = jnp.concatenate([plane_high, plane_low, plane_high], axis=1)
        right = jnp.concatenate([right, blank], axis=0)
        moments = lax.dot_general(
            left, right, (((1,), (1,)), ((), ())), preferred_element_type=f32
        )
        sums = [moments[0:8]]
        for axis in range(3):
            at = 32 + 24 * axis
            sums.append(
                moments[8 + 8 * axis : 16 + 8 * axis]
                + moments[at : at + 8] * node_first
                + moments[at + 8 : at + 16] * node_second
                + moments[at + 16 : at + 24] * node_third
            )
        turned = pltpu.roll(jnp.concatenate(sums, axis=0), begin % 128, 1)
        inside = (lanes >= begin) & (lanes < begin + 64)
        beyond = (lanes >= begin - 128) & (lanes < begin - 64)
        return jnp.where(inside, turned, 0.0), jnp.where(beyond, turned, 0.0)

    def residents(step, carry):
        first = step // 4
        third = step % 4
        low, high = None, None
        for second in range(4):
            one, two = one_bin(
                first * 16 + second * 4 + third,
                32 * (second + 1),
                bin_count_ref[first, second, third],
            )
            low = one if low is None else low + one
            high = two if high is None else high + two
        total[first + 1, third + 1, :, 0:128] = low
        total[first + 1, third + 1, :, 128:256] = high
        return carry

    lax.fori_loop(0, 8, residents, 0, unroll=4)

    def leavers(member, carry):
        for direction in range(5):
            block = depart_block_ref[0, 0, 0, member, direction]
            count = depart_count_ref[0, 0, 0, member, direction]
            index = 32 + direction * 4 + member
            window = block // 16 + 1
            begin = 32 * (block // 4 % 4 + 1)
            third = block % 4 + 1
            if direction < 2:
                window = 3 if direction == 0 else 0
            elif direction < 4:
                begin = 160 if direction == 2 else 0
            else:
                block = depart_block_ref[0, 0, 0, member, 4 + core]
                count = depart_count_ref[0, 0, 0, member, 4 + core]
                index = 48 + 4 * core + member
                window = block // 16 + 1
                begin = 32 * (block // 4 % 4 + 1)
                third = 5 - 5 * core
            one, two = one_bin(index, begin, count)
            total[window, third, :, 0:128] += one
            total[window, third, :, 128:256] += two
        return carry

    lax.fori_loop(0, 4, leavers, 0, unroll=4)

    lower_rows = sub_iota((8, 128)) < 4
    lower_lanes = lane_iota((8, 128)) % 8 < 4
    lower_tall = lane_iota((ZR, 128)) % 8 < 4
    pieces = {}
    for half in range(2):
        columns = slice(128 * half, 128 * half + 128)
        for c in range(4):
            folded = []
            for window in range(4):
                piece = [
                    total[window, third + 1 - core, 8 * c : 8 * c + 8, columns]
                    for third in range(5)
                ]
                one = pltpu.roll(piece[1], 4, 0)
                three = pltpu.roll(piece[3], 4, 0)
                folded.append(
                    jnp.concatenate(
                        [
                            piece[0] + jnp.where(lower_rows, 0.0, one),
                            piece[2] + jnp.where(lower_rows, one, three),
                            piece[4] + jnp.where(lower_rows, three, 0.0),
                        ],
                        axis=0,
                    )
                )
            window_ref[0, c, :, columns] = folded[1] + jnp.where(
                lower_tall, roll_lanes(folded[0], -4), 0.0
            )
            window_ref[1, c, :, columns] = folded[2] + jnp.where(
                lower_tall, 0.0, roll_lanes(folded[3], 4)
            )
            at = (2 * c + half) * ZR
            pieces[at] = [
                folded[3] + jnp.where(lower_tall, roll_lanes(folded[2], -4), 0.0),
                folded[0] + jnp.where(lower_tall, 0.0, roll_lanes(folded[1], 4)),
            ]
            near = contact[0][half][ZR * c : ZR * c + ZR]
            far = contact[1][half][ZR * c : ZR * c + ZR]
            window_ref[0, 4 + c, :, columns] = near
            window_ref[1, 4 + c, :, columns] = far
    tall = lane_iota((ZR, 128))
    for pair in range(2):
        first_c = slice(2 * pair * ZR, (2 * pair + 1) * ZR)
        second_c = slice((2 * pair + 1) * ZR, (2 * pair + 2) * ZR)
        near = [
            jnp.where(lower_tall, contact[0][half][first_c], roll_lanes(contact[0][half][second_c], 4))
            for half in range(2)
        ]
        far = [
            jnp.where(lower_tall, roll_lanes(contact[1][half][first_c], -4), contact[1][half][second_c])
            for half in range(2)
        ]
        main = 192 + pair * ZR
        rest = (2 * pair + 1) * ZR
        pieces[main] = []
        for side, packed in enumerate((far, near)):
            pieces[main].append(jnp.where(tall >= 48, packed[0], packed[1]))
            pieces[rest][side] = jnp.where(
                (tall >= 96) & (tall < 104), roll_lanes(packed[1], 48), pieces[rest][side]
            )
    for at, (plus, minus) in pieces.items():
        put_pair(one_ref, two_ref, slice(at, at + ZR), even, plus, minus)
    plus = bins_of(depart_ref, depart_count_ref, depart_block_ref, 0)
    minus = bins_of(depart_ref, depart_count_ref, depart_block_ref, 1)
    for part in range(PARTS):
        at = 240 + 4 * part
        put_pair(one_ref, two_ref, slice(at, at + 4), even, plus[part], minus[part])
    south = bins_of(depart_ref, depart_count_ref, depart_block_ref, 2)
    north = bins_of(depart_ref, depart_count_ref, depart_block_ref, 3)
    up = bins_of(depart_ref, depart_count_ref, depart_block_ref, 4)
    down = bins_of(depart_ref, depart_count_ref, depart_block_ref, 5)
    for part in range(PARTS):
        bins_ref[4 * part : 4 * part + 4, :] = south[part]
        bins_ref[40 + 4 * part : 44 + 4 * part, :] = north[part]
        bins_ref[80 + 4 * part : 84 + 4 * part, :] = jnp.where(core == 0, up[part], down[part])


def bins_of(depart_ref, depart_count_ref, depart_block_ref, direction):
    values = [depart_ref[c, 4 * direction : 4 * direction + 4, :] for c in CARRIED]
    row = sub_iota((4, 128))
    for ref in (depart_count_ref, depart_block_ref):
        value = jnp.zeros((4, 128), jnp.int32)
        for member in range(4):
            value = jnp.where(row == member, ref[0, 0, 0, member, direction], value)
        values.append(value.astype(f32))
    return values


def put_pair(one_ref, two_ref, at, even, plus, minus):
    one_ref[at, :] = jnp.where(even, plus, minus)
    two_ref[at, :] = jnp.where(even, minus, plus)


def take_pair(one_ref, two_ref, at, even):
    one, two = one_ref[at, :], two_ref[at, :]
    return jnp.where(even, two, one), jnp.where(even, one, two)


def stage_kernel(window_in, bins_in, state_ref, window_ref, bins_ref, plane_ref, weight_ref):
    window_ref[...] = window_in[...]
    bins_ref[...] = bins_in[...]
    nodes = sub_iota((8, 128)).astype(f32) - 2.0

    def one_bin(index, carry):
        place = [state_ref[axis, pl.ds(index, 1), :] for axis in range(3)]
        high, low, wz, lever = collect_terms(place, nodes)
        plane_ref[index, 0:64, :] = high
        plane_ref[index, 64:128, :] = low
        weight_ref[index, 0:8, :] = wz
        weight_ref[index, 8:16, :] = lever
        return carry

    lax.fori_loop(0, 32, one_bin, 0, unroll=8)


def collect_terms(place, nodes):
    high, low = parts(plane_of(spline(place[0], nodes), spline(place[1], nodes)))
    wz = spline(place[2], nodes)
    return high, low, wz, wz * (nodes - place[2])


def second_kernel(window_in, from_one, from_two, bins_ref, window_ref, one_ref, two_ref):
    even = lax.axis_index("gx") % 2 == 0
    even_second = lax.axis_index("gy") % 2 == 0
    lanes = lane_iota((ZR, 128))
    lower = lanes % 8 < 4
    new = [[[None, None], [None, None]] for _ in range(8)]
    for c in range(8):
        for half in range(2):
            columns = slice(128 * half, 128 * half + 128)
            if c < 4:
                at = (2 * c + half) * ZR
                near, far = take_pair(from_one, from_two, slice(at, at + ZR), even)
                if half == 1:
                    near = jnp.where(lanes < 96, near, 0.0)
                    far = jnp.where(lanes < 96, far, 0.0)
            else:
                pair = (c - 4) // 2
                at = 192 + pair * ZR
                near, far = take_pair(from_one, from_two, slice(at, at + ZR), even)
                if half == 0:
                    near = jnp.where(lanes >= 48, near, 0.0)
                    far = jnp.where(lanes >= 48, far, 0.0)
                else:
                    at = (2 * pair + 1) * ZR
                    rest = take_pair(from_one, from_two, slice(at, at + ZR), even)
                    rest = [jnp.where(lanes < 56, roll_lanes(value, -48), 0.0) for value in rest]
                    near = jnp.where(lanes < 48, near, rest[0])
                    far = jnp.where(lanes < 48, far, rest[1])
            if c >= 4 and c % 2 == 0:
                near = jnp.where(lower, near, 0.0)
                far = jnp.where(lower, 0.0, roll_lanes(far, 4))
            elif c >= 4:
                near = jnp.where(lower, roll_lanes(near, -4), 0.0)
                far = jnp.where(lower, 0.0, far)
            new[c][0][half] = window_in[0, c, :, columns] + near
            new[c][1][half] = window_in[1, c, :, columns] + far
            for window in range(2):
                window_ref[window, c, :, columns] = new[c][window][half]
    for c in range(4):
        near, far = new[c]
        plus = jnp.where(lanes < 64, roll_lanes(near[1], -32), roll_lanes(far[1], 32))
        minus = jnp.where(lanes < 64, near[0], roll_lanes(far[0], 64))
        put_pair(one_ref, two_ref, slice(c * ZR, (c + 1) * ZR), even_second, plus, minus)
    for pair in range(2):
        at = slice(96 + pair * ZR, 96 + (pair + 1) * ZR)
        even_c, odd_c = new[4 + 2 * pair], new[5 + 2 * pair]
        sides = []
        for half in (1, 0):
            sides.append(
                jnp.where(
                    lanes < 64,
                    jnp.where(lanes < 32, roll_lanes(even_c[0][half], -32), even_c[1][half]),
                    jnp.where(
                        lanes < 96, roll_lanes(odd_c[0][half], 32), roll_lanes(odd_c[1][half], 64)
                    ),
                )
            )
        put_pair(one_ref, two_ref, at, even_second, sides[0], sides[1])
    put_pair(
        one_ref, two_ref, slice(144, 184), even_second, bins_ref[0:40, :], bins_ref[40:80, :]
    )


def third_kernel(window_in, from_one, from_two, bins_ref, window_ref, message_ref):
    even = lax.axis_index("gy") % 2 == 0
    core = lax.axis_index("gz")
    lanes = lane_iota((ZR, 128))
    for window in range(2):
        for c in range(8):
            if c < 4:
                near, far = take_pair(from_one, from_two, slice(c * ZR, (c + 1) * ZR), even)
                near = jnp.where(
                    (lanes >= 32) & (lanes < 96),
                    roll_lanes(near, 32 if window == 0 else -32),
                    0.0,
                )
                far = jnp.where(lanes < 64, far if window == 0 else roll_lanes(far, 64), 0.0)
            else:
                at = slice(96 + (c - 4) // 2 * ZR, 96 + ((c - 4) // 2 + 1) * ZR)
                shift = (32, 0, -32, -64)[2 * (c % 2) + window]
                inside = (lanes >= 32) & (lanes < 64)
                near, far = take_pair(from_one, from_two, at, even)
                near = jnp.where(inside, roll_lanes(near, shift), 0.0)
                far = jnp.where(inside, roll_lanes(far, shift), 0.0)
            for half, extra in ((0, near), (1, far)):
                columns = slice(128 * half, 128 * half + 128)
                value = window_in[window, c, :, columns] + extra
                window_ref[window, c, :, columns] = value
                at = ((window * 8 + c) * 2 + half) * 8
                message_ref[at : at + 8, :] = jnp.where(core == 0, value[16:24], value[0:8])
    message_ref[256:296, :] = bins_ref[80:120, :]


def advance(sums):
    mass = jnp.maximum(sums[0], mass_floor)
    previous = [sums[1 + axis] / mass for axis in range(3)]
    velocity = [previous[0], previous[1], previous[2] - time_step * gravity]
    normal = sums[4:7]
    scale = 1.0 + (normal[0] * normal[0] + normal[1] * normal[1] + normal[2] * normal[2])
    dot = velocity[0] * normal[0] + velocity[1] * normal[1] + velocity[2] * normal[2]
    inward = jnp.minimum(dot, 0.0) / scale
    velocity = [velocity[axis] - inward * normal[axis] for axis in range(3)]
    dot = velocity[0] * normal[0] + velocity[1] * normal[1] + velocity[2] * normal[2]
    along = dot / scale
    damp = 1.0 - jnp.exp(-sums[7])
    velocity = [
        velocity[axis] - damp * (velocity[axis] - along * normal[axis]) for axis in range(3)
    ]
    return velocity + previous


def collect_kernel(
    window_in,
    from_z,
    x_one,
    x_two,
    y_one,
    y_two,
    plane_ref,
    weight_ref,
    state_ref,
    bin_count_ref,
    moved_ref,
    arrived_ref,
    data,
    fields,
    turned,
    table,
    picked,
    live,
    target,
    moved,
    arrived,
    semaphores,
):
    core = lax.axis_index("gz")
    row = lax.axis_index("gy")
    lanes = lane_iota((8, 128))
    subs = sub_iota((8, 128))
    lower_rows = subs < 4
    lower_lanes = lanes % 8 < 4

    even_first = lax.axis_index("gx") % 2 == 0
    even_second = lax.axis_index("gy") % 2 == 0
    arrivals = []
    for one_ref, two_ref, begin, even in ((x_one, x_two, 240, even_first), (y_one, y_two, 144, even_second)):
        pairs = [
            take_pair(one_ref, two_ref, slice(begin + 4 * part, begin + 4 * part + 4), even)
            for part in range(PARTS)
        ]
        arrivals += [[pair[0] for pair in pairs], [pair[1] for pair in pairs]]
    arrivals.append([from_z[256 + 4 * part : 260 + 4 * part, :] for part in range(PARTS)])
    for g, values in enumerate(arrivals):
        for part in range(7):
            data[part, 4 * g : 4 * g + 4, :] = values[part]
        slot = lane_iota((4, 128)).astype(f32)
        live[32 + 4 * g : 36 + 4 * g, :] = jnp.where(slot < values[7], 1.0, 0.0)
        block = values[8].astype(jnp.int32)
        for member in range(4):
            target[4 * g + member] = block[member, 0]

    below = core == 0
    above = core == 1
    taken = [
        jnp.logical_not(lower_rows) & above,
        (lower_rows & above) | (jnp.logical_not(lower_rows) & below),
        lower_rows & below,
    ]
    for third in range(3):
        rows = slice(8 * third, 8 * third + 8)
        for half in range(2):
            columns = slice(128 * half, 128 * half + 128)
            sums = [[], []]
            for c in range(8):
                values = [window_in[b, c, rows, columns] for b in range(2)]
                for b in range(2):
                    at = ((b * 8 + c) * 2 + half) * 8
                    edge = pltpu.roll(from_z[at : at + 8, :], 4, 0)
                    values[b] = values[b] + jnp.where(taken[third], edge, 0.0)
                sums[0].append(
                    values[0] + jnp.where(lower_lanes, 0.0, roll_lanes(values[1], 4))
                )
                sums[1].append(
                    values[1] + jnp.where(lower_lanes, roll_lanes(values[0], -4), 0.0)
                )
            node_second = row * 16 + (lanes + 128 * half) // 8 - 6
            node_third = core * 12 + subs + 8 * third - 2
            inside = (
                (node_second >= 0) & (node_second < 128) & (node_third >= 0) & (node_third < 32)
            )
            for b in range(2):
                for c, value in enumerate(advance(sums[b])):
                    fields[b, c, rows, columns] = jnp.where(inside, value, 0.0)

    wide = lane_iota((ZR, 128))
    local = wide % 64
    node_first = (local % 8).astype(f32) - 2.0 - center
    node_second = (local // 8).astype(f32) - 2.0 - center
    for b in range(2):
        for c in range(6):
            low = fields[b, c, :, 0:128]
            high = fields[b, c, :, 128:256]
            shown = [
                jnp.where(wide < 64, roll_lanes(low, -32), roll_lanes(low, 32)),
                jnp.where(wide < 64, roll_lanes(low, 64), low),
                jnp.where(
                    wide < 64,
                    jnp.where(wide < 32, roll_lanes(low, 32), roll_lanes(high, 32)),
                    jnp.where(wide < 96, roll_lanes(low, -32), roll_lanes(high, 96)),
                ),
                jnp.where(wide < 64, high, roll_lanes(high, 64)),
            ]
            for second in range(4):
                turned[second, :, c, :] = shown[second]
                if c < 3:
                    turned[second, :, 6 + c, :] = shown[second] * node_first
                    turned[second, :, 9 + c, :] = shown[second] * node_second
        for second in range(4):
            value = turned[second].reshape(ZR * 16, 128)
            high, low = parts(value)
            table[4 * b + second, :, 0:128] = high
            table[4 * b + second, :, 128:256] = low

    nodes = subs.astype(f32) - 2.0

    def one_bin(index, column, third, high, low, wz, lever):
        right = jnp.concatenate([high, low, high, low], axis=0)
        left = table[column, pl.ds(64 * third, 128), :]
        values = jnp.dot(left, right, preferred_element_type=f32)
        first = values[0:8] * wz[0:1]
        second = values[8:16] * wz[0:1]
        moment = values[0:8] * lever[0:1]
        for k in range(1, 8):
            first = first + values[16 * k : 16 * k + 8] * wz[k : k + 1]
            second = second + values[16 * k + 8 : 16 * k + 16] * wz[k : k + 1]
            moment = moment + values[16 * k : 16 * k + 8] * lever[k : k + 1]
        picked[0:8, index, :] = first
        picked[8:16, index, :] = second
        picked[16:24, index, :] = moment

    def residents(step, carry):
        first = step // 4
        second = step % 4
        for third in range(4):
            index = step * 4 + third
            high, low = plane_ref[index, 0:64, :], plane_ref[index, 64:128, :]
            wz, lever = weight_ref[index, 0:8, :], weight_ref[index, 8:16, :]
            one_bin(index, step, third + core, high, low, wz, lever)
            count = bin_count_ref[first, second, third]
            live[pl.ds(index, 1), :] = jnp.where(lane_iota((1, 128)) < count, 1.0, 0.0)
        return carry

    def movers(step, carry):
        for member in range(4):
            index = 4 * step + member
            block = target[index]
            terms = collect_terms([data[axis, pl.ds(index, 1), :] for axis in range(3)], nodes)
            one_bin(32 + index, block // 4, block % 4 + core, *terms)
        return carry

    lax.fori_loop(0, 5, movers, 0, unroll=5)

    def finish(begin, size, old):
        rows = slice(begin, begin + size)
        valid = live[rows, :]
        got = [picked[c, rows, :] for c in range(19)]
        result = []
        for axis in range(3):
            result.append(old[axis] + time_step * got[axis])
        for axis in range(3):
            result.append(
                flip_ratio * (old[3 + axis] + got[axis] - got[3 + axis])
                + (1.0 - flip_ratio) * got[axis]
            )
        affine = []
        for axis in range(3):
            affine.append(4.0 * (got[6 + axis] - (old[0] - center) * got[axis]))
            affine.append(4.0 * (got[9 + axis] - (old[1] - center) * got[axis]))
            affine.append(4.0 * got[16 + axis])
        result += affine
        result.append(old[6] * (1.0 + time_step * (affine[0] + affine[4] + affine[8])))
        return [value * valid for value in result]

    for g in range(3):
        begin, size = 8 * g, 8 if g < 2 else 4
        rows = slice(begin, begin + size)
        for c, value in enumerate(finish(32 + begin, size, [data[p, rows, :] for p in range(7)])):
            if g < 2:
                arrived[c, rows, :] = value
            else:
                arrived[c, 16:20, :] = jnp.where(core == 1, value, 0.0)
                arrived[c, 20:24, :] = jnp.where(core == 0, value, 0.0)
    arrived_copy = pltpu.make_async_copy(arrived, arrived_ref, semaphores.at[0])
    arrived_copy.start()
    lax.fori_loop(0, 8, residents, 0, unroll=4)
    for g in range(4):
        rows = slice(8 * g, 8 * g + 8)
        for c, value in enumerate(finish(8 * g, 8, [state_ref[c, rows, :] for c in CARRIED])):
            moved[c, rows, :] = value
    moved_copy = pltpu.make_async_copy(moved, moved_ref, semaphores.at[1])
    moved_copy.start()
    arrived_copy.wait()
    moved_copy.wait()


def pairs_along(axis, first, closed):
    count = lax.axis_size(axis)
    route = [(i, (i + 1) % count) for i in range(first, count, 2) if closed or i + 1 < count]
    return route + [(j, i) for i, j in route]


vmem = pl.BlockSpec(memory_space=pltpu.VMEM)
smem = pl.BlockSpec(memory_space=pltpu.SMEM)
limits = pltpu.CompilerParams(vmem_limit_bytes=48 * 1024 * 1024)
ample = pltpu.CompilerParams(vmem_limit_bytes=60 * 1024 * 1024)


def shape_of(*dims):
    return jax.ShapeDtypeStruct(dims, f32)


def body(
    state,
    bin_count,
    departing,
    depart_count,
    depart_block,
    cut_cell,
    quad_count,
    wall_id,
    cut_level,
    wall_normal,
    wall_friction,
):
    state_rows = state.reshape(16, 32, 128)
    leaving = departing.reshape(16, 24, 128)
    cut = [value.reshape(4, 128) for value in (cut_cell, quad_count, wall_id, cut_level)]
    depart_count = jnp.swapaxes(depart_count, 3, 4)
    depart_block = jnp.swapaxes(depart_block, 3, 4)
    operands = (
        state_rows,
        bin_count,
        leaving,
        depart_count,
        depart_block,
        *cut,
        wall_normal,
        wall_friction,
    )
    scalars = (1, 3, 4, 9, 10)
    window, one, two, bins = pl.pallas_call(
        deposit_kernel,
        out_shape=[
            shape_of(2, 8, ZR, LN),
            shape_of(XROWS, 128),
            shape_of(XROWS, 128),
            shape_of(3 * BINROWS, 128),
        ],
        in_specs=[pl.BlockSpec(memory_space=pltpu.HBM)] * 11,
        out_specs=[vmem] * 4,
        scratch_shapes=[
            (pltpu.SMEM if place in scalars else pltpu.VMEM)(value.shape, value.dtype)
            for place, value in enumerate(operands)
        ]
        + [
            pltpu.VMEM((16, 56, 128), f32),
            pltpu.VMEM((4, 6, 32, LN), f32),
            pltpu.SemaphoreType.DMA((11,)),
        ],
        compiler_params=ample,
        name="deposit",
    )(*operands)
    x_one = lax.ppermute(one, "gx", pairs_along("gx", 0, True))
    x_two = lax.ppermute(two, "gx", pairs_along("gx", 1, True))
    window, bins, planes, weights = pl.pallas_call(
        stage_kernel,
        out_shape=[
            shape_of(2, 8, ZR, LN),
            shape_of(3 * BINROWS, 128),
            jax.ShapeDtypeStruct((32, 128, 128), bf16),
            shape_of(32, 16, 128),
        ],
        in_specs=[vmem] * 3,
        out_specs=[vmem] * 4,
        cost_estimate=pl.CostEstimate(flops=10**9, bytes_accessed=2**20, transcendentals=0),
        compiler_params=limits,
        name="stage",
    )(window, bins, state_rows)
    window, one, two = pl.pallas_call(
        second_kernel,
        out_shape=[shape_of(2, 8, ZR, LN), shape_of(YROWS, 128), shape_of(YROWS, 128)],
        in_specs=[vmem] * 4,
        out_specs=[vmem] * 3,
        compiler_params=limits,
        name="take_x",
    )(window, x_one, x_two, bins)
    y_one = lax.ppermute(one, "gy", pairs_along("gy", 0, False))
    y_two = lax.ppermute(two, "gy", pairs_along("gy", 1, False))
    window, message = pl.pallas_call(
        third_kernel,
        out_shape=[shape_of(2, 8, ZR, LN), shape_of(ZROWS, 128)],
        in_specs=[vmem] * 4,
        out_specs=[vmem] * 2,
        compiler_params=limits,
        name="take_y",
    )(window, y_one, y_two, bins)
    from_z = lax.ppermute(message, "gz", [(0, 1), (1, 0)])
    moved, arrived = pl.pallas_call(
        collect_kernel,
        out_shape=[shape_of(16, 32, 128), shape_of(16, 24, 128)],
        in_specs=[vmem] * 9 + [smem],
        out_specs=[pl.BlockSpec(memory_space=pltpu.HBM)] * 2,
        scratch_shapes=[
            pltpu.VMEM((7, 24, 128), f32),
            pltpu.VMEM((2, 6, ZR, LN), f32),
            pltpu.VMEM((4, ZR, 16, 128), f32),
            pltpu.VMEM((8, ZR * 16, 256), bf16),
            pltpu.VMEM((24, 56, 128), f32),
            pltpu.VMEM((56, 128), f32),
            pltpu.SMEM((20,), jnp.int32),
            pltpu.VMEM((16, 32, 128), f32),
            pltpu.VMEM((16, 24, 128), f32),
            pltpu.SemaphoreType.DMA((2,)),
        ],
        compiler_params=limits,
        name="collect",
    )(
        window,
        from_z,
        x_one,
        x_two,
        y_one,
        y_two,
        planes,
        weights,
        state_rows,
        bin_count,
    )
    return moved.reshape(state.shape), arrived.reshape(departing.shape)


def solution(mesh):
    placed = (
        P(None, "gx", "gy", "gz", None),
        P("gx", "gy", "gz"),
        P(None, "gx", "gy", "gz", None, None, None),
        P("gx", "gy", "gz", None, None),
        P("gx", "gy", "gz", None, None),
        P("gx", "gy", "gz", None),
        P("gx", "gy", "gz", None),
        P("gx", "gy", "gz", None),
        P("gx", "gy", "gz", None),
        P(),
        P(),
    )
    return jax.shard_map(
        body,
        mesh=mesh,
        in_specs=placed,
        out_specs=(P(None, "gx", "gy", "gz", None), P(None, "gx", "gy", "gz", None, None, None)),
        check_vma=False,
    )
```

```python
import jax
import jax.numpy as jnp
import numpy as np
from jax import lax
from jax.experimental import pallas as pl
from jax.experimental.pallas import tpu as pltpu
from jax.sharding import PartitionSpec as P

time_step = 0.1
stiffness = 4.0
gravity = 2.0
flip_ratio = 0.95
mass_floor = 0.25
center = 1.5
quad_points = [
    [0.5, 0.5, 0.5],
    [0.2, 0.7, 0.35],
    [0.8, 0.3, 0.65],
    [0.35, 0.15, 0.85],
    [0.65, 0.85, 0.15],
    [0.1, 0.45, 0.55],
    [0.9, 0.55, 0.45],
    [0.45, 0.9, 0.75],
]
f32 = jnp.float32
bf16 = jnp.bfloat16

ZR = 24
LN = 256
CARRIED = (0, 1, 2, 3, 4, 5, 15)
PARTS = 9
BINROWS = 40
XROWS = 96 + 48 + 48 + BINROWS
YROWS = 96 + 48 + BINROWS
ZROWS = 256 + BINROWS


def lane_iota(shape):
    return lax.broadcasted_iota(jnp.int32, shape, len(shape) - 1)


def sub_iota(shape):
    return lax.broadcasted_iota(jnp.int32, shape, len(shape) - 2)


def spline(coord, nodes):
    distance = jnp.abs(coord - nodes)
    inner = 0.75 - distance * distance
    reach = jnp.maximum(1.5 - distance, 0.0)
    return jnp.where(distance < 0.5, inner, 0.5 * reach * reach)


def parts(value):
    high = value.astype(bf16)
    low = (value - high.astype(f32)).astype(bf16)
    return high, low


def plane_of(wx, wy):
    return jnp.concatenate([wy[y : y + 1] * wx for y in range(8)], axis=0)


def roll_lanes(value, shift):
    return pltpu.roll(value, shift % 128, 1)


def contact_terms(cell_ref, quad_ref, wall_ref, level_ref, normal_ref, friction_ref):
    cells = cell_ref[...]
    counts = quad_ref[...]
    walls = wall_ref[...]
    level = level_ref[...]
    normal = []
    for axis in range(3):
        part = jnp.zeros_like(level)
        for wall in range(4):
            part = jnp.where(walls == wall, normal_ref[wall, axis], part)
        normal.append(part)
    friction = jnp.zeros_like(level)
    for wall in range(4):
        friction = jnp.where(walls == wall, friction_ref[wall], friction)
    inverse = 1.0 / jnp.maximum(counts, 1).astype(f32)
    weights = [None] * 8
    for q, point in enumerate(quad_points):
        level_set = level + (normal[0] * point[0] + normal[1] * point[1] + normal[2] * point[2])
        cover = jnp.clip(0.5 - level_set, 0.0, 1.0)
        share = jnp.where(counts > q, cover * inverse, 0.0)
        for corner in range(8):
            factor = 1.0
            for axis in range(3):
                bit = (corner >> (2 - axis)) & 1
                factor *= point[axis] if bit else 1.0 - point[axis]
            term = share * factor
            weights[corner] = term if weights[corner] is None else weights[corner] + term
    return cells, weights, normal + [friction]


def contact_windows(cell_ref, quad_ref, wall_ref, level_ref, normal_ref, friction_ref):
    cells, weights, factors = contact_terms(
        cell_ref, quad_ref, wall_ref, level_ref, normal_ref, friction_ref
    )
    place_third = cells % 16 + 2 + 4 * lax.axis_index("gz")
    column = (cells // 16) % 16 * 8 + cells // 256
    rows = sub_iota((ZR, 128))
    bit_rows = sub_iota((128, 128))
    lefts_high = []
    lefts_low = []
    rights = []
    for tile in range(4):
        third = place_third[tile : tile + 1]
        first_row = rows == third
        second_row = rows == third + 1
        pieces_high = []
        pieces_low = []
        for pair in range(4):
            lower = weights[2 * pair][tile : tile + 1]
            upper = weights[2 * pair + 1][tile : tile + 1]
            for channel in range(4):
                factor = factors[channel][tile : tile + 1]
                value = jnp.where(
                    first_row, lower * factor, jnp.where(second_row, upper * factor, 0.0)
                )
                high, low = parts(value)
                pieces_high.append(high.astype(f32))
                pieces_low.append(low.astype(f32))
        lefts_high.append(jnp.concatenate(pieces_high, axis=0).astype(bf16))
        lefts_low.append(jnp.concatenate(pieces_low, axis=0).astype(bf16))
        rights.append(
            jnp.where(bit_rows == column[tile : tile + 1], 1.0, 0.0).astype(bf16)
        )
    left = jnp.concatenate(lefts_high + lefts_low, axis=1)
    right = jnp.concatenate(rights + rights, axis=1)
    touched = lax.dot_general(
        left, right, (((1,), (1,)), ((), ())), preferred_element_type=f32
    )
    lanes = lane_iota((4 * ZR, 128))
    first = lanes % 8
    result = [[None, None], [None, None]]
    for pair in range(4):
        dx, dy = pair >> 1, pair & 1
        block = touched[pair * 4 * ZR : (pair + 1) * 4 * ZR]
        near = jnp.where(first <= 5 - dx, block, 0.0)
        far = jnp.where(first >= 6 - dx, block, 0.0)
        for window, (value, shift) in enumerate(
            ((near, 50 + 8 * dy + dx), (far, 46 + 8 * dy + dx))
        ):
            turned = roll_lanes(value, shift)
            for half, piece in enumerate(
                (jnp.where(lanes >= shift, turned, 0.0), jnp.where(lanes < shift, turned, 0.0))
            ):
                known = result[window][half]
                result[window][half] = piece if known is None else known + piece
    return result


def deposit_kernel(*refs):
    inputs, outputs = refs[:11], refs[11:15]
    even = lax.axis_index("gx") % 2 == 0
    copies, (data, total, semaphores) = refs[15:26], refs[26:29]
    window_ref, one_ref, two_ref, bins_ref = refs[29:33]
    sent = []

    def send(place, *where):
        source = refs[29 + place].at[where] if where else refs[29 + place]
        target = outputs[place].at[where] if where else outputs[place]
        sent.append(pltpu.make_async_copy(source, target, semaphores.at[11 + len(sent)]))
        sent[-1].start()

    started = []
    for place in (5, 6, 7, 8, 9, 10, 0, 2, 1, 3, 4):
        started.append(
            pltpu.make_async_copy(inputs[place], copies[place], semaphores.at[place])
        )
        started[-1].start()
    state_ref, bin_count_ref, depart_ref, depart_count_ref, depart_block_ref = copies[:5]
    for window in (0, 3):
        total[window] = jnp.zeros((6, 32, LN), f32)
    for window in (1, 2):
        for third in (0, 5):
            total[window, third] = jnp.zeros((32, LN), f32)
    for copy in started[:6]:
        copy.wait()
    contact = contact_windows(*copies[5:])
    for window in range(2):
        for half in range(2):
            for c in range(4):
                window_ref[window, 4 + c, :, 128 * half : 128 * half + 128] = contact[window][
                    half
                ][ZR * c : ZR * c + ZR]
        send(0, window, slice(4, 8))
    for copy in started[6:]:
        copy.wait()

    core = lax.axis_index("gz")
    plus = bins_of(depart_ref, depart_count_ref, depart_block_ref, 0)
    minus = bins_of(depart_ref, depart_count_ref, depart_block_ref, 1)
    for part in range(PARTS):
        at = 192 + 4 * part
        put_pair(one_ref, two_ref, slice(at, at + 4), even, plus[part], minus[part])
    south = bins_of(depart_ref, depart_count_ref, depart_block_ref, 2)
    north = bins_of(depart_ref, depart_count_ref, depart_block_ref, 3)
    up = bins_of(depart_ref, depart_count_ref, depart_block_ref, 4)
    down = bins_of(depart_ref, depart_count_ref, depart_block_ref, 5)
    for part in range(PARTS):
        bins_ref[4 * part : 4 * part + 4, :] = south[part]
        bins_ref[40 + 4 * part : 44 + 4 * part, :] = north[part]
        bins_ref[80 + 4 * part : 84 + 4 * part, :] = jnp.where(core == 0, up[part], down[part])
    send(1, slice(192, XROWS))
    send(2, slice(192, XROWS))
    send(3)

    size = 8
    groups = [(state_ref, 8 * g, 8 * g) for g in range(4)]
    groups += [(depart_ref, 8 * g, 32 + 8 * g) for g in range(3)]
    for ref, begin, place in groups:
        channel = [ref[c, begin : begin + size, :] for c in range(16)]
        pressure = time_step * 4.0 * stiffness * jnp.maximum(1.0 - channel[15], 0.0)
        spread = [channel[6 + e] + (pressure if e % 4 == 0 else 0.0) for e in range(9)]
        offset = [channel[axis] - center for axis in range(3)]
        for axis in range(3):
            data[axis, place : place + size, :] = channel[axis]
            data[3 + axis, place : place + size, :] = (
                channel[3 + axis]
                - spread[3 * axis] * offset[0]
                - spread[3 * axis + 1] * offset[1]
                - spread[3 * axis + 2] * offset[2]
            )
        for entry in range(9):
            data[6 + entry, place : place + size, :] = spread[entry]

    nodes = sub_iota((8, 128)).astype(f32) - 2.0
    slots = lane_iota((8, 128))
    lanes = lane_iota((32, 128))
    local = lane_iota((8, 128)) % 64
    node_first = (local % 8).astype(f32) - 2.0 - center
    node_second = (local // 8).astype(f32) - 2.0 - center
    node_third = nodes - center

    def one_bin(index, begin, count):
        def row(channel):
            return data[channel, pl.ds(index, 1), :]

        wx = spline(row(0), nodes)
        wy = spline(row(1), nodes)
        wz = jnp.where(slots < count, spline(row(2), nodes), 0.0)
        lifted = jnp.concatenate([wz] + [row(3 + c) * wz for c in range(12)], axis=0)
        lift_high, lift_low = parts(lifted)
        plane_high, plane_low = parts(plane_of(wx, wy))
        left = jnp.concatenate([lift_high, lift_low], axis=1)
        right = jnp.concatenate([plane_high, plane_low], axis=0)
        right = jnp.concatenate([right, right], axis=1)
        moments = lax.dot_general(
            left, right, (((1,), (1,)), ((), ())), preferred_element_type=f32
        )
        sums = [moments[0:8]]
        for axis in range(3):
            at = 32 + 24 * axis
            sums.append(
                moments[8 + 8 * axis : 16 + 8 * axis]
                + moments[at : at + 8] * node_first
                + moments[at + 8 : at + 16] * node_second
                + moments[at + 16 : at + 24] * node_third
            )
        both = jnp.concatenate(sums, axis=0)
        turned = pltpu.roll(both + roll_lanes(both, 64), begin % 128, 1)
        inside = (lanes >= begin) & (lanes < begin + 64)
        beyond = (lanes >= begin - 128) & (lanes < begin - 64)
        return jnp.where(inside, turned, 0.0), jnp.where(beyond, turned, 0.0)

    def residents(step, carry):
        first = step // 4
        third = step % 4
        low, high = None, None
        for second in range(4):
            one, two = one_bin(
                first * 16 + second * 4 + third,
                32 * (second + 1),
                bin_count_ref[first, second, third],
            )
            low = one if low is None else low + one
            high = two if high is None else high + two
        total[first + 1, third + 1, :, 0:128] = low
        total[first + 1, third + 1, :, 128:256] = high
        return carry

    lax.fori_loop(0, 8, residents, 0, unroll=4)

    def leavers(member, carry):
        for direction in range(5):
            block = depart_block_ref[0, 0, 0, member, direction]
            count = depart_count_ref[0, 0, 0, member, direction]
            index = 32 + direction * 4 + member
            window = block // 16 + 1
            begin = 32 * (block // 4 % 4 + 1)
            third = block % 4 + 1
            if direction < 2:
                window = 3 if direction == 0 else 0
            elif direction < 4:
                begin = 160 if direction == 2 else 0
            else:
                block = depart_block_ref[0, 0, 0, member, 4 + core]
                count = depart_count_ref[0, 0, 0, member, 4 + core]
                index = 48 + 4 * core + member
                window = block // 16 + 1
                begin = 32 * (block // 4 % 4 + 1)
                third = 5 - 5 * core
            one, two = one_bin(index, begin, count)
            total[window, third, :, 0:128] += one
            total[window, third, :, 128:256] += two
        return carry

    lax.fori_loop(0, 4, leavers, 0, unroll=4)

    lower_rows = sub_iota((8, 128)) < 4
    lower_lanes = lane_iota((8, 128)) % 8 < 4
    lower_tall = lane_iota((ZR, 128)) % 8 < 4
    leaving = {}
    for half in range(2):
        columns = slice(128 * half, 128 * half + 128)
        for c in range(4):
            folded = []
            for window in range(4):
                piece = [
                    total[window, third + 1 - core, 8 * c : 8 * c + 8, columns]
                    for third in range(5)
                ]
                one = pltpu.roll(piece[1], 4, 0)
                three = pltpu.roll(piece[3], 4, 0)
                folded.append(
                    jnp.concatenate(
                        [
                            piece[0] + jnp.where(lower_rows, 0.0, one),
                            piece[2] + jnp.where(lower_rows, one, three),
                            piece[4] + jnp.where(lower_rows, three, 0.0),
                        ],
                        axis=0,
                    )
                )
            window_ref[0, c, :, columns] = folded[1] + jnp.where(
                lower_tall, roll_lanes(folded[0], -4), 0.0
            )
            window_ref[1, c, :, columns] = folded[2] + jnp.where(
                lower_tall, 0.0, roll_lanes(folded[3], 4)
            )
            leaving[c, half] = (
                folded[3] + jnp.where(lower_tall, roll_lanes(folded[2], -4), 0.0),
                folded[0] + jnp.where(lower_tall, 0.0, roll_lanes(folded[1], 4)),
            )
    send(0, 0, slice(0, 4))
    send(0, 1, slice(0, 4))

    tall = lane_iota((ZR, 128))
    narrow = lane_iota((8, 128))
    for pair in range(2):
        sides = []
        for side, (heavy, light) in enumerate(((pack_lower, pack_upper), (pack_upper, pack_lower))):
            own = [
                heavy(leaving[2 * pair, h][side], leaving[2 * pair + 1, h][side], lower_tall)
                for h in range(2)
            ]
            other = [
                light(leaving[2 * pair, h][side], leaving[2 * pair + 1, h][side], lower_tall)
                for h in range(2)
            ]
            rows_even = slice(2 * pair * ZR, (2 * pair + 1) * ZR)
            rows_odd = slice((2 * pair + 1) * ZR, (2 * pair + 2) * ZR)
            touch = [
                light(contact[1 - side][h][rows_even], contact[1 - side][h][rows_odd], lower_tall)
                for h in range(2)
            ]
            own[1] = jnp.where(tall < 96, own[1], roll_lanes(other[1], 64))
            mixed = jnp.where(tall < 32, other[1], other[0])
            spare = jnp.zeros((8, 128), f32)
            for group in range(6):
                value = touch[1][group // 2 * 8 : group // 2 * 8 + 8]
                swapped = pltpu.roll(value, 4, 0)
                if group % 2 == 0:
                    value = jnp.where(lower_rows, value, swapped)
                else:
                    value = jnp.where(lower_rows, swapped, value)
                inside = (narrow >= 16 * group) & (narrow < 16 * group + 8)
                spare = jnp.where(inside, roll_lanes(value, 16 * group - 48), spare)
            mixed = jnp.concatenate(
                [
                    jnp.where(lower_rows & (core == 1), spare, mixed[0:8]),
                    mixed[8:16],
                    jnp.where(lower_rows | (core == 1), mixed[16:24], spare),
                ],
                axis=0,
            )
            sides.append(own + [mixed, jnp.where(tall >= 48, touch[0], touch[1])])
        places = (2 * pair * ZR, (2 * pair + 1) * ZR, 96 + pair * ZR, 144 + pair * ZR)
        for at, plus, minus in zip(places, *sides):
            put_pair(one_ref, two_ref, slice(at, at + ZR), even, plus, minus)
    send(1, slice(0, 192))
    send(2, slice(0, 192))
    for copy in sent:
        copy.wait()


def bins_of(depart_ref, depart_count_ref, depart_block_ref, direction):
    values = [depart_ref[c, 4 * direction : 4 * direction + 4, :] for c in CARRIED]
    row = sub_iota((4, 128))
    for ref in (depart_count_ref, depart_block_ref):
        value = jnp.zeros((4, 128), jnp.int32)
        for member in range(4):
            value = jnp.where(row == member, ref[0, 0, 0, member, direction], value)
        values.append(value.astype(f32))
    return values


def pack_lower(even_c, odd_c, lower):
    return jnp.where(lower, even_c, roll_lanes(odd_c, 4))


def pack_upper(even_c, odd_c, lower):
    return jnp.where(lower, roll_lanes(even_c, -4), odd_c)


def put_pair(one_ref, two_ref, at, even, plus, minus):
    one_ref[at, :] = jnp.where(even, plus, minus)
    two_ref[at, :] = jnp.where(even, minus, plus)


def take_pair(one_ref, two_ref, at, even):
    one, two = one_ref[at, :], two_ref[at, :]
    return jnp.where(even, two, one), jnp.where(even, one, two)


def stage_kernel(window_in, bins_in, state_ref, window_ref, bins_ref, plane_ref, weight_ref):
    window_ref[...] = window_in[...]
    bins_ref[...] = bins_in[...]
    nodes = sub_iota((8, 128)).astype(f32) - 2.0

    def one_bin(index, carry):
        place = [state_ref[axis, pl.ds(index, 1), :] for axis in range(3)]
        high, low, wz, lever = collect_terms(place, nodes)
        plane_ref[index, 0:64, :] = high
        plane_ref[index, 64:128, :] = low
        weight_ref[index, 0:8, :] = wz
        weight_ref[index, 8:16, :] = lever
        return carry

    lax.fori_loop(0, 32, one_bin, 0, unroll=8)


def collect_terms(place, nodes):
    high, low = parts(plane_of(spline(place[0], nodes), spline(place[1], nodes)))
    wz = spline(place[2], nodes)
    return high, low, wz, wz * (nodes - place[2])


def second_kernel(window_in, from_one, from_two, bins_ref, window_ref, one_ref, two_ref):
    even = lax.axis_index("gx") % 2 == 0
    even_second = lax.axis_index("gy") % 2 == 0
    lanes = lane_iota((ZR, 128))
    lower = lanes % 8 < 4
    core = lax.axis_index("gz")
    narrow = lane_iota((8, 128))
    lower_rows = sub_iota((8, 128)) < 4
    got = [[[None, None], [None, None]] for _ in range(8)]
    for pair in range(2):
        places = (2 * pair * ZR, (2 * pair + 1) * ZR, 96 + pair * ZR, 144 + pair * ZR)
        taken = [take_pair(from_one, from_two, slice(at, at + ZR), even) for at in places]
        for side in range(2):
            own = [taken[0][side], taken[1][side]]
            mixed, touch = taken[2][side], taken[3][side]
            spare = jnp.where(core == 0, mixed[16:24], mixed[0:8])
            swapped = pltpu.roll(spare, 4, 0)
            spare = jnp.where(lower_rows == (core == 1), spare, swapped)
            mixed = jnp.concatenate(
                [
                    jnp.where(lower_rows & (core == 1), 0.0, mixed[0:8]),
                    mixed[8:16],
                    jnp.where(lower_rows | (core == 1), mixed[16:24], 0.0),
                ],
                axis=0,
            )
            other = [
                jnp.where(lanes >= 32, mixed, 0.0),
                jnp.where(
                    lanes < 32, mixed, jnp.where(lanes < 64, roll_lanes(own[1], -64), 0.0)
                ),
            ]
            own[1] = jnp.where(lanes < 96, own[1], 0.0)
            rest = [
                jnp.where(
                    lower_rows,
                    roll_lanes(spare, 48 - 32 * tile),
                    roll_lanes(spare, 32 - 32 * tile),
                )
                for tile in range(3)
            ]
            rest = jnp.concatenate(rest, axis=0)
            touched = [
                jnp.where(lanes >= 48, touch, 0.0),
                jnp.where(lanes < 48, touch, jnp.where(lanes < 56, rest, 0.0)),
            ]
            for half in range(2):
                values = (own[half], other[half]) if side == 0 else (other[half], own[half])
                got[2 * pair][side][half] = jnp.where(lower, values[0], roll_lanes(values[1], 4))
                got[2 * pair + 1][side][half] = jnp.where(
                    lower, roll_lanes(values[0], -4), values[1]
                )
                value = touched[half]
                if side == 0:
                    got[4 + 2 * pair][side][half] = jnp.where(lower, value, 0.0)
                    got[5 + 2 * pair][side][half] = jnp.where(lower, roll_lanes(value, -4), 0.0)
                else:
                    got[4 + 2 * pair][side][half] = jnp.where(lower, 0.0, roll_lanes(value, 4))
                    got[5 + 2 * pair][side][half] = jnp.where(lower, 0.0, value)
    new = [[[None, None], [None, None]] for _ in range(8)]
    for c in range(8):
        for window in range(2):
            for half in range(2):
                columns = slice(128 * half, 128 * half + 128)
                value = window_in[window, c, :, columns] + got[c][window][half]
                new[c][window][half] = value
                window_ref[window, c, :, columns] = value
    for c in range(4):
        near, far = new[c]
        plus = jnp.where(lanes < 64, roll_lanes(near[1], -32), roll_lanes(far[1], 32))
        minus = jnp.where(lanes < 64, near[0], roll_lanes(far[0], 64))
        put_pair(one_ref, two_ref, slice(c * ZR, (c + 1) * ZR), even_second, plus, minus)
    for pair in range(2):
        at = slice(96 + pair * ZR, 96 + (pair + 1) * ZR)
        even_c, odd_c = new[4 + 2 * pair], new[5 + 2 * pair]
        sides = []
        for half in (1, 0):
            sides.append(
                jnp.where(
                    lanes < 64,
                    jnp.where(lanes < 32, roll_lanes(even_c[0][half], -32), even_c[1][half]),
                    jnp.where(
                        lanes < 96, roll_lanes(odd_c[0][half], 32), roll_lanes(odd_c[1][half], 64)
                    ),
                )
            )
        put_pair(one_ref, two_ref, at, even_second, sides[0], sides[1])
    put_pair(
        one_ref, two_ref, slice(144, 184), even_second, bins_ref[0:40, :], bins_ref[40:80, :]
    )


def third_kernel(window_in, from_one, from_two, bins_ref, window_ref, message_ref):
    even = lax.axis_index("gy") % 2 == 0
    core = lax.axis_index("gz")
    lanes = lane_iota((ZR, 128))
    for window in range(2):
        for c in range(8):
            if c < 4:
                near, far = take_pair(from_one, from_two, slice(c * ZR, (c + 1) * ZR), even)
                near = jnp.where(
                    (lanes >= 32) & (lanes < 96),
                    roll_lanes(near, 32 if window == 0 else -32),
                    0.0,
                )
                far = jnp.where(lanes < 64, far if window == 0 else roll_lanes(far, 64), 0.0)
            else:
                at = slice(96 + (c - 4) // 2 * ZR, 96 + ((c - 4) // 2 + 1) * ZR)
                shift = (32, 0, -32, -64)[2 * (c % 2) + window]
                inside = (lanes >= 32) & (lanes < 64)
                near, far = take_pair(from_one, from_two, at, even)
                near = jnp.where(inside, roll_lanes(near, shift), 0.0)
                far = jnp.where(inside, roll_lanes(far, shift), 0.0)
            for half, extra in ((0, near), (1, far)):
                columns = slice(128 * half, 128 * half + 128)
                value = window_in[window, c, :, columns] + extra
                window_ref[window, c, :, columns] = value
                at = ((window * 8 + c) * 2 + half) * 8
                message_ref[at : at + 8, :] = jnp.where(core == 0, value[16:24], value[0:8])
    message_ref[256:296, :] = bins_ref[80:120, :]


def advance(sums):
    mass = jnp.maximum(sums[0], mass_floor)
    previous = [sums[1 + axis] / mass for axis in range(3)]
    velocity = [previous[0], previous[1], previous[2] - time_step * gravity]
    normal = sums[4:7]
    scale = 1.0 + (normal[0] * normal[0] + normal[1] * normal[1] + normal[2] * normal[2])
    dot = velocity[0] * normal[0] + velocity[1] * normal[1] + velocity[2] * normal[2]
    inward = jnp.minimum(dot, 0.0) / scale
    velocity = [velocity[axis] - inward * normal[axis] for axis in range(3)]
    dot = velocity[0] * normal[0] + velocity[1] * normal[1] + velocity[2] * normal[2]
    along = dot / scale
    damp = 1.0 - jnp.exp(-sums[7])
    velocity = [
        velocity[axis] - damp * (velocity[axis] - along * normal[axis]) for axis in range(3)
    ]
    return velocity + previous


def collect_kernel(
    window_in,
    from_z,
    x_one,
    x_two,
    y_one,
    y_two,
    plane_ref,
    weight_ref,
    state_ref,
    bin_count_ref,
    moved_ref,
    arrived_ref,
    data,
    fields,
    turned,
    table,
    picked,
    live,
    target,
    moved,
    arrived,
    semaphores,
):
    core = lax.axis_index("gz")
    row = lax.axis_index("gy")
    lanes = lane_iota((8, 128))
    subs = sub_iota((8, 128))
    lower_rows = subs < 4
    lower_lanes = lanes % 8 < 4

    even_first = lax.axis_index("gx") % 2 == 0
    even_second = lax.axis_index("gy") % 2 == 0
    arrivals = []
    for one_ref, two_ref, begin, even in ((x_one, x_two, 192, even_first), (y_one, y_two, 144, even_second)):
        pairs = [
            take_pair(one_ref, two_ref, slice(begin + 4 * part, begin + 4 * part + 4), even)
            for part in range(PARTS)
        ]
        arrivals += [[pair[0] for pair in pairs], [pair[1] for pair in pairs]]
    arrivals.append([from_z[256 + 4 * part : 260 + 4 * part, :] for part in range(PARTS)])
    for g, values in enumerate(arrivals):
        for part in range(7):
            data[part, 4 * g : 4 * g + 4, :] = values[part]
        slot = lane_iota((4, 128)).astype(f32)
        live[32 + 4 * g : 36 + 4 * g, :] = jnp.where(slot < values[7], 1.0, 0.0)
        block = values[8].astype(jnp.int32)
        for member in range(4):
            target[4 * g + member] = block[member, 0]

    below = core == 0
    above = core == 1
    taken = [
        jnp.logical_not(lower_rows) & above,
        (lower_rows & above) | (jnp.logical_not(lower_rows) & below),
        lower_rows & below,
    ]
    for third in range(3):
        rows = slice(8 * third, 8 * third + 8)
        for half in range(2):
            columns = slice(128 * half, 128 * half + 128)
            sums = [[], []]
            for c in range(8):
                values = [window_in[b, c, rows, columns] for b in range(2)]
                for b in range(2):
                    at = ((b * 8 + c) * 2 + half) * 8
                    edge = pltpu.roll(from_z[at : at + 8, :], 4, 0)
                    values[b] = values[b] + jnp.where(taken[third], edge, 0.0)
                sums[0].append(
                    values[0] + jnp.where(lower_lanes, 0.0, roll_lanes(values[1], 4))
                )
                sums[1].append(
                    values[1] + jnp.where(lower_lanes, roll_lanes(values[0], -4), 0.0)
                )
            node_second = row * 16 + (lanes + 128 * half) // 8 - 6
            node_third = core * 12 + subs + 8 * third - 2
            inside = (
                (node_second >= 0) & (node_second < 128) & (node_third >= 0) & (node_third < 32)
            )
            for b in range(2):
                for c, value in enumerate(advance(sums[b])):
                    fields[b, c, rows, columns] = jnp.where(inside, value, 0.0)

    wide = lane_iota((ZR, 128))
    local = wide % 64
    node_first = (local % 8).astype(f32) - 2.0 - center
    node_second = (local // 8).astype(f32) - 2.0 - center
    for b in range(2):
        for c in range(6):
            low = fields[b, c, :, 0:128]
            high = fields[b, c, :, 128:256]
            shown = [
                jnp.where(wide < 64, roll_lanes(low, -32), roll_lanes(low, 32)),
                jnp.where(wide < 64, roll_lanes(low, 64), low),
                jnp.where(
                    wide < 64,
                    jnp.where(wide < 32, roll_lanes(low, 32), roll_lanes(high, 32)),
                    jnp.where(wide < 96, roll_lanes(low, -32), roll_lanes(high, 96)),
                ),
                jnp.where(wide < 64, high, roll_lanes(high, 64)),
            ]
            for second in range(4):
                turned[second, :, c, :] = shown[second]
                if c < 3:
                    turned[second, :, 6 + c, :] = shown[second] * node_first
                    turned[second, :, 9 + c, :] = shown[second] * node_second
        for second in range(4):
            value = turned[second].reshape(ZR * 16, 128)
            high, low = parts(value)
            table[4 * b + second, :, 0:128] = high
            table[4 * b + second, :, 128:256] = low

    nodes = subs.astype(f32) - 2.0

    def one_bin(index, column, third, high, low, wz, lever):
        right = jnp.concatenate([high, low, high, low], axis=0)
        left = table[column, pl.ds(64 * third, 128), :]
        values = jnp.dot(left, right, preferred_element_type=f32)
        first = values[0:8] * wz[0:1]
        second = values[8:16] * wz[0:1]
        moment = values[0:8] * lever[0:1]
        for k in range(1, 8):
            first = first + values[16 * k : 16 * k + 8] * wz[k : k + 1]
            second = second + values[16 * k + 8 : 16 * k + 16] * wz[k : k + 1]
            moment = moment + values[16 * k : 16 * k + 8] * lever[k : k + 1]
        picked[0:8, index, :] = first
        picked[8:16, index, :] = second
        picked[16:24, index, :] = moment

    def residents(step, carry):
        first = step // 4
        second = step % 4
        for third in range(4):
            index = step * 4 + third
            high, low = plane_ref[index, 0:64, :], plane_ref[index, 64:128, :]
            wz, lever = weight_ref[index, 0:8, :], weight_ref[index, 8:16, :]
            one_bin(index, step, third + core, high, low, wz, lever)
            count = bin_count_ref[first, second, third]
            live[pl.ds(index, 1), :] = jnp.where(lane_iota((1, 128)) < count, 1.0, 0.0)
        return carry

    def movers(step, carry):
        for member in range(4):
            index = 4 * step + member
            block = target[index]
            terms = collect_terms([data[axis, pl.ds(index, 1), :] for axis in range(3)], nodes)
            one_bin(32 + index, block // 4, block % 4 + core, *terms)
        return carry

    lax.fori_loop(0, 5, movers, 0, unroll=5)

    def finish(begin, size, old):
        rows = slice(begin, begin + size)
        valid = live[rows, :]
        got = [picked[c, rows, :] for c in range(19)]
        result = []
        for axis in range(3):
            result.append(old[axis] + time_step * got[axis])
        for axis in range(3):
            result.append(
                flip_ratio * (old[3 + axis] + got[axis] - got[3 + axis])
                + (1.0 - flip_ratio) * got[axis]
            )
        affine = []
        for axis in range(3):
            affine.append(4.0 * (got[6 + axis] - (old[0] - center) * got[axis]))
            affine.append(4.0 * (got[9 + axis] - (old[1] - center) * got[axis]))
            affine.append(4.0 * got[16 + axis])
        result += affine
        result.append(old[6] * (1.0 + time_step * (affine[0] + affine[4] + affine[8])))
        return [value * valid for value in result]

    for g in range(3):
        begin, size = 8 * g, 8 if g < 2 else 4
        rows = slice(begin, begin + size)
        for c, value in enumerate(finish(32 + begin, size, [data[p, rows, :] for p in range(7)])):
            if g < 2:
                arrived[c, rows, :] = value
            else:
                arrived[c, 16:20, :] = jnp.where(core == 1, value, 0.0)
                arrived[c, 20:24, :] = jnp.where(core == 0, value, 0.0)
    arrived_copy = pltpu.make_async_copy(arrived, arrived_ref, semaphores.at[0])
    arrived_copy.start()
    moved_copies = []
    for part in range(2):
        lax.fori_loop(4 * part, 4 * part + 4, residents, 0, unroll=4)
        for g in range(2 * part, 2 * part + 2):
            rows = slice(8 * g, 8 * g + 8)
            for c, value in enumerate(finish(8 * g, 8, [state_ref[c, rows, :] for c in CARRIED])):
                moved[c, rows, :] = value
        where = (slice(None), pl.ds(16 * part, 16))
        moved_copies.append(
            pltpu.make_async_copy(moved.at[where], moved_ref.at[where], semaphores.at[1 + part])
        )
        moved_copies[-1].start()
    arrived_copy.wait()
    for copy in moved_copies:
        copy.wait()


def pairs_along(axis, first, closed):
    count = lax.axis_size(axis)
    route = [(i, (i + 1) % count) for i in range(first, count, 2) if closed or i + 1 < count]
    return route + [(j, i) for i, j in route]


vmem = pl.BlockSpec(memory_space=pltpu.VMEM)
smem = pl.BlockSpec(memory_space=pltpu.SMEM)
limits = pltpu.CompilerParams(vmem_limit_bytes=48 * 1024 * 1024)
ample = pltpu.CompilerParams(vmem_limit_bytes=60 * 1024 * 1024)


def shape_of(*dims):
    return jax.ShapeDtypeStruct(dims, f32)


def body(
    state,
    bin_count,
    departing,
    depart_count,
    depart_block,
    cut_cell,
    quad_count,
    wall_id,
    cut_level,
    wall_normal,
    wall_friction,
):
    state_rows = state.reshape(16, 32, 128)
    leaving = departing.reshape(16, 24, 128)
    cut = [value.reshape(4, 128) for value in (cut_cell, quad_count, wall_id, cut_level)]
    depart_count = jnp.swapaxes(depart_count, 3, 4)
    depart_block = jnp.swapaxes(depart_block, 3, 4)
    operands = (
        state_rows,
        bin_count,
        leaving,
        depart_count,
        depart_block,
        *cut,
        wall_normal,
        wall_friction,
    )
    scalars = (1, 3, 4, 9, 10)
    window, one, two, bins = pl.pallas_call(
        deposit_kernel,
        out_shape=[
            shape_of(2, 8, ZR, LN),
            shape_of(XROWS, 128),
            shape_of(XROWS, 128),
            shape_of(3 * BINROWS, 128),
        ],
        in_specs=[pl.BlockSpec(memory_space=pltpu.HBM)] * 11,
        out_specs=[pl.BlockSpec(memory_space=pltpu.HBM)] * 4,
        scratch_shapes=[
            (pltpu.SMEM if place in scalars else pltpu.VMEM)(value.shape, value.dtype)
            for place, value in enumerate(operands)
        ]
        + [
            pltpu.VMEM((16, 56, 128), f32),
            pltpu.VMEM((4, 6, 32, LN), f32),
            pltpu.SemaphoreType.DMA((20,)),
            pltpu.VMEM((2, 8, ZR, LN), f32),
            pltpu.VMEM((XROWS, 128), f32),
            pltpu.VMEM((XROWS, 128), f32),
            pltpu.VMEM((3 * BINROWS, 128), f32),
        ],
        compiler_params=ample,
        name="deposit",
    )(*operands)
    x_one = lax.ppermute(one, "gx", pairs_along("gx", 0, True))
    x_two = lax.ppermute(two, "gx", pairs_along("gx", 1, True))
    window, bins, planes, weights = pl.pallas_call(
        stage_kernel,
        out_shape=[
            shape_of(2, 8, ZR, LN),
            shape_of(3 * BINROWS, 128),
            jax.ShapeDtypeStruct((32, 128, 128), bf16),
            shape_of(32, 16, 128),
        ],
        in_specs=[vmem] * 3,
        out_specs=[vmem] * 4,
        cost_estimate=pl.CostEstimate(flops=10**9, bytes_accessed=2**20, transcendentals=0),
        compiler_params=limits,
        name="stage",
    )(window, bins, state_rows)
    window, one, two = pl.pallas_call(
        second_kernel,
        out_shape=[shape_of(2, 8, ZR, LN), shape_of(YROWS, 128), shape_of(YROWS, 128)],
        in_specs=[vmem] * 4,
        out_specs=[vmem] * 3,
        compiler_params=limits,
        name="take_x",
    )(window, x_one, x_two, bins)
    y_one = lax.ppermute(one, "gy", pairs_along("gy", 0, False))
    y_two = lax.ppermute(two, "gy", pairs_along("gy", 1, False))
    window, message = pl.pallas_call(
        third_kernel,
        out_shape=[shape_of(2, 8, ZR, LN), shape_of(ZROWS, 128)],
        in_specs=[vmem] * 4,
        out_specs=[vmem] * 2,
        compiler_params=limits,
        name="take_y",
    )(window, y_one, y_two, bins)
    from_z = lax.ppermute(message, "gz", [(0, 1), (1, 0)])
    moved, arrived = pl.pallas_call(
        collect_kernel,
        out_shape=[shape_of(16, 32, 128), shape_of(16, 24, 128)],
        in_specs=[vmem] * 9 + [smem],
        out_specs=[pl.BlockSpec(memory_space=pltpu.HBM)] * 2,
        scratch_shapes=[
            pltpu.VMEM((7, 24, 128), f32),
            pltpu.VMEM((2, 6, ZR, LN), f32),
            pltpu.VMEM((4, ZR, 16, 128), f32),
            pltpu.VMEM((8, ZR * 16, 256), bf16),
            pltpu.VMEM((24, 56, 128), f32),
            pltpu.VMEM((56, 128), f32),
            pltpu.SMEM((20,), jnp.int32),
            pltpu.VMEM((16, 32, 128), f32),
            pltpu.VMEM((16, 24, 128), f32),
            pltpu.SemaphoreType.DMA((3,)),
        ],
        compiler_params=limits,
        name="collect",
    )(
        window,
        from_z,
        x_one,
        x_two,
        y_one,
        y_two,
        planes,
        weights,
        state_rows,
        bin_count,
    )
    return moved.reshape(state.shape), arrived.reshape(departing.shape)


def solution(mesh):
    placed = (
        P(None, "gx", "gy", "gz", None),
        P("gx", "gy", "gz"),
        P(None, "gx", "gy", "gz", None, None, None),
        P("gx", "gy", "gz", None, None),
        P("gx", "gy", "gz", None, None),
        P("gx", "gy", "gz", None),
        P("gx", "gy", "gz", None),
        P("gx", "gy", "gz", None),
        P("gx", "gy", "gz", None),
        P(),
        P(),
    )
    return jax.shard_map(
        body,
        mesh=mesh,
        in_specs=placed,
        out_specs=(P(None, "gx", "gy", "gz", None), P(None, "gx", "gy", "gz", None, None, None)),
        check_vma=False,
    )
```

```python
import jax
import jax.numpy as jnp
import numpy as np
from jax import lax
from jax.experimental import pallas as pl
from jax.experimental.pallas import tpu as pltpu
from jax.sharding import PartitionSpec as P

time_step = 0.1
stiffness = 4.0
gravity = 2.0
flip_ratio = 0.95
mass_floor = 0.25
center = 1.5
quad_points = [
    [0.5, 0.5, 0.5],
    [0.2, 0.7, 0.35],
    [0.8, 0.3, 0.65],
    [0.35, 0.15, 0.85],
    [0.65, 0.85, 0.15],
    [0.1, 0.45, 0.55],
    [0.9, 0.55, 0.45],
    [0.45, 0.9, 0.75],
]
f32 = jnp.float32
bf16 = jnp.bfloat16

ZR = 24
LN = 256
CARRIED = (0, 1, 2, 3, 4, 5, 15)
PARTS = 9
BINROWS = 40
XROWS = 96 + 48 + 48 + BINROWS
YROWS = 96 + 48 + BINROWS
ZROWS = 256 + BINROWS


def lane_iota(shape):
    return lax.broadcasted_iota(jnp.int32, shape, len(shape) - 1)


def sub_iota(shape):
    return lax.broadcasted_iota(jnp.int32, shape, len(shape) - 2)


def spline(coord, nodes):
    distance = jnp.abs(coord - nodes)
    inner = 0.75 - distance * distance
    reach = jnp.maximum(1.5 - distance, 0.0)
    return jnp.where(distance < 0.5, inner, 0.5 * reach * reach)


def parts(value):
    high = value.astype(bf16)
    low = (value - high.astype(f32)).astype(bf16)
    return high, low


def plane_of(wx, wy):
    return jnp.concatenate([wy[y : y + 1] * wx for y in range(8)], axis=0)


def roll_lanes(value, shift):
    return pltpu.roll(value, shift % 128, 1)


def contact_terms(cell_ref, quad_ref, wall_ref, level_ref, normal_ref, friction_ref):
    cells = cell_ref[...]
    counts = quad_ref[...]
    walls = wall_ref[...]
    level = level_ref[...]
    normal = []
    for axis in range(3):
        part = jnp.zeros_like(level)
        for wall in range(4):
            part = jnp.where(walls == wall, normal_ref[wall, axis], part)
        normal.append(part)
    friction = jnp.zeros_like(level)
    for wall in range(4):
        friction = jnp.where(walls == wall, friction_ref[wall], friction)
    inverse = 1.0 / jnp.maximum(counts, 1).astype(f32)
    weights = [None] * 8
    for q, point in enumerate(quad_points):
        level_set = level + (normal[0] * point[0] + normal[1] * point[1] + normal[2] * point[2])
        cover = jnp.clip(0.5 - level_set, 0.0, 1.0)
        share = jnp.where(counts > q, cover * inverse, 0.0)
        for corner in range(8):
            factor = 1.0
            for axis in range(3):
                bit = (corner >> (2 - axis)) & 1
                factor *= point[axis] if bit else 1.0 - point[axis]
            term = share * factor
            weights[corner] = term if weights[corner] is None else weights[corner] + term
    return cells, weights, normal + [friction]


def contact_windows(cell_ref, quad_ref, wall_ref, level_ref, normal_ref, friction_ref):
    cells, weights, factors = contact_terms(
        cell_ref, quad_ref, wall_ref, level_ref, normal_ref, friction_ref
    )
    place_third = cells % 16 + 2 + 4 * lax.axis_index("gz")
    column = (cells // 16) % 16 * 8 + cells // 256
    rows = sub_iota((ZR, 128))
    bit_rows = sub_iota((128, 128))
    lefts_high = []
    lefts_low = []
    rights = []
    for tile in range(4):
        third = place_third[tile : tile + 1]
        first_row = rows == third
        second_row = rows == third + 1
        pieces_high = []
        pieces_low = []
        for pair in range(4):
            lower = weights[2 * pair][tile : tile + 1]
            upper = weights[2 * pair + 1][tile : tile + 1]
            for channel in range(4):
                factor = factors[channel][tile : tile + 1]
                value = jnp.where(
                    first_row, lower * factor, jnp.where(second_row, upper * factor, 0.0)
                )
                high, low = parts(value)
                pieces_high.append(high.astype(f32))
                pieces_low.append(low.astype(f32))
        lefts_high.append(jnp.concatenate(pieces_high, axis=0).astype(bf16))
        lefts_low.append(jnp.concatenate(pieces_low, axis=0).astype(bf16))
        rights.append(
            jnp.where(bit_rows == column[tile : tile + 1], 1.0, 0.0).astype(bf16)
        )
    left = jnp.concatenate(lefts_high + lefts_low, axis=1)
    right = jnp.concatenate(rights + rights, axis=1)
    touched = lax.dot_general(
        left, right, (((1,), (1,)), ((), ())), preferred_element_type=f32
    )
    lanes = lane_iota((4 * ZR, 128))
    first = lanes % 8
    result = [[None, None], [None, None]]
    for pair in range(4):
        dx, dy = pair >> 1, pair & 1
        block = touched[pair * 4 * ZR : (pair + 1) * 4 * ZR]
        near = jnp.where(first <= 5 - dx, block, 0.0)
        far = jnp.where(first >= 6 - dx, block, 0.0)
        for window, (value, shift) in enumerate(
            ((near, 50 + 8 * dy + dx), (far, 46 + 8 * dy + dx))
        ):
            turned = roll_lanes(value, shift)
            for half, piece in enumerate(
                (jnp.where(lanes >= shift, turned, 0.0), jnp.where(lanes < shift, turned, 0.0))
            ):
                known = result[window][half]
                result[window][half] = piece if known is None else known + piece
    return result


def deposit_kernel(*refs):
    inputs, (window_ref, one_ref, two_ref, bins_ref) = refs[:11], refs[11:15]
    even = lax.axis_index("gx") % 2 == 0
    copies, (data, total, semaphores) = refs[15:26], refs[26:]

    started = []
    for place in (5, 6, 7, 8, 9, 10, 0, 2, 1, 3, 4):
        started.append(
            pltpu.make_async_copy(inputs[place], copies[place], semaphores.at[place])
        )
        started[-1].start()
    state_ref, bin_count_ref, depart_ref, depart_count_ref, depart_block_ref = copies[:5]
    for window in (0, 3):
        total[window] = jnp.zeros((6, 32, LN), f32)
    for window in (1, 2):
        for third in (0, 5):
            total[window, third] = jnp.zeros((32, LN), f32)
    for copy in started[:6]:
        copy.wait()
    contact = contact_windows(*copies[5:])
    for window in range(2):
        for half in range(2):
            for c in range(4):
                window_ref[window, 4 + c, :, 128 * half : 128 * half + 128] = contact[window][
                    half
                ][ZR * c : ZR * c + ZR]
    for copy in started[6:]:
        copy.wait()

    core = lax.axis_index("gz")
    plus = bins_of(depart_ref, depart_count_ref, depart_block_ref, 0)
    minus = bins_of(depart_ref, depart_count_ref, depart_block_ref, 1)
    for part in range(PARTS):
        at = 192 + 4 * part
        put_pair(one_ref, two_ref, slice(at, at + 4), even, plus[part], minus[part])
    south = bins_of(depart_ref, depart_count_ref, depart_block_ref, 2)
    north = bins_of(depart_ref, depart_count_ref, depart_block_ref, 3)
    up = bins_of(depart_ref, depart_count_ref, depart_block_ref, 4)
    down = bins_of(depart_ref, depart_count_ref, depart_block_ref, 5)
    for part in range(PARTS):
        bins_ref[4 * part : 4 * part + 4, :] = south[part]
        bins_ref[40 + 4 * part : 44 + 4 * part, :] = north[part]
        bins_ref[80 + 4 * part : 84 + 4 * part, :] = jnp.where(core == 0, up[part], down[part])

    size = 8
    groups = [(state_ref, 8 * g, 8 * g) for g in range(4)]
    groups += [(depart_ref, 8 * g, 32 + 8 * g) for g in range(3)]
    for ref, begin, place in groups:
        channel = [ref[c, begin : begin + size, :] for c in range(16)]
        pressure = time_step * 4.0 * stiffness * jnp.maximum(1.0 - channel[15], 0.0)
        spread = [channel[6 + e] + (pressure if e % 4 == 0 else 0.0) for e in range(9)]
        offset = [channel[axis] - center for axis in range(3)]
        for axis in range(3):
            data[axis, place : place + size, :] = channel[axis]
            data[3 + axis, place : place + size, :] = (
                channel[3 + axis]
                - spread[3 * axis] * offset[0]
                - spread[3 * axis + 1] * offset[1]
                - spread[3 * axis + 2] * offset[2]
            )
        for entry in range(9):
            data[6 + entry, place : place + size, :] = spread[entry]

    nodes = sub_iota((8, 128)).astype(f32) - 2.0
    slots = lane_iota((8, 128))
    lanes = lane_iota((32, 128))
    local = lane_iota((8, 128)) % 64
    node_first = (local % 8).astype(f32) - 2.0 - center
    node_second = (local // 8).astype(f32) - 2.0 - center
    node_third = nodes - center

    def one_bin(index, begin, count):
        def row(channel):
            return data[channel, pl.ds(index, 1), :]

        wx = spline(row(0), nodes)
        wy = spline(row(1), nodes)
        wz = jnp.where(slots < count, spline(row(2), nodes), 0.0)
        lifted = jnp.concatenate([wz] + [row(3 + c) * wz for c in range(12)], axis=0)
        lift_high, lift_low = parts(lifted)
        plane_high, plane_low = parts(plane_of(wx, wy))
        left = jnp.concatenate([lift_high, lift_low], axis=1)
        right = jnp.concatenate([plane_high, plane_low], axis=0)
        right = jnp.concatenate([right, right], axis=1)
        moments = lax.dot_general(
            left, right, (((1,), (1,)), ((), ())), preferred_element_type=f32
        )
        sums = [moments[0:8]]
        for axis in range(3):
            at = 32 + 24 * axis
            sums.append(
                moments[8 + 8 * axis : 16 + 8 * axis]
                + moments[at : at + 8] * node_first
                + moments[at + 8 : at + 16] * node_second
                + moments[at + 16 : at + 24] * node_third
            )
        both = jnp.concatenate(sums, axis=0)
        turned = pltpu.roll(both + roll_lanes(both, 64), begin % 128, 1)
        inside = (lanes >= begin) & (lanes < begin + 64)
        beyond = (lanes >= begin - 128) & (lanes < begin - 64)
        return jnp.where(inside, turned, 0.0), jnp.where(beyond, turned, 0.0)

    def residents(step, carry):
        first = step // 4
        third = step % 4
        low, high = None, None
        for second in range(4):
            one, two = one_bin(
                first * 16 + second * 4 + third,
                32 * (second + 1),
                bin_count_ref[first, second, third],
            )
            low = one if low is None else low + one
            high = two if high is None else high + two
        total[first + 1, third + 1, :, 0:128] = low
        total[first + 1, third + 1, :, 128:256] = high
        return carry

    lax.fori_loop(0, 8, residents, 0, unroll=4)

    def leavers(member, carry):
        for direction in range(5):
            block = depart_block_ref[0, 0, 0, member, direction]
            count = depart_count_ref[0, 0, 0, member, direction]
            index = 32 + direction * 4 + member
            window = block // 16 + 1
            begin = 32 * (block // 4 % 4 + 1)
            third = block % 4 + 1
            if direction < 2:
                window = 3 if direction == 0 else 0
            elif direction < 4:
                begin = 160 if direction == 2 else 0
            else:
                block = depart_block_ref[0, 0, 0, member, 4 + core]
                count = depart_count_ref[0, 0, 0, member, 4 + core]
                index = 48 + 4 * core + member
                window = block // 16 + 1
                begin = 32 * (block // 4 % 4 + 1)
                third = 5 - 5 * core
            one, two = one_bin(index, begin, count)
            total[window, third, :, 0:128] += one
            total[window, third, :, 128:256] += two
        return carry

    lax.fori_loop(0, 4, leavers, 0, unroll=4)

    lower_rows = sub_iota((8, 128)) < 4
    lower_lanes = lane_iota((8, 128)) % 8 < 4
    lower_tall = lane_iota((ZR, 128)) % 8 < 4
    leaving = {}
    for half in range(2):
        columns = slice(128 * half, 128 * half + 128)
        for c in range(4):
            folded = []
            for window in range(4):
                piece = [
                    total[window, third + 1 - core, 8 * c : 8 * c + 8, columns]
                    for third in range(5)
                ]
                one = pltpu.roll(piece[1], 4, 0)
                three = pltpu.roll(piece[3], 4, 0)
                folded.append(
                    jnp.concatenate(
                        [
                            piece[0] + jnp.where(lower_rows, 0.0, one),
                            piece[2] + jnp.where(lower_rows, one, three),
                            piece[4] + jnp.where(lower_rows, three, 0.0),
                        ],
                        axis=0,
                    )
                )
            window_ref[0, c, :, columns] = folded[1] + jnp.where(
                lower_tall, roll_lanes(folded[0], -4), 0.0
            )
            window_ref[1, c, :, columns] = folded[2] + jnp.where(
                lower_tall, 0.0, roll_lanes(folded[3], 4)
            )
            leaving[c, half] = (
                folded[3] + jnp.where(lower_tall, roll_lanes(folded[2], -4), 0.0),
                folded[0] + jnp.where(lower_tall, 0.0, roll_lanes(folded[1], 4)),
            )
    tall = lane_iota((ZR, 128))
    narrow = lane_iota((8, 128))
    for pair in range(2):
        sides = []
        for side, (heavy, light) in enumerate(((pack_lower, pack_upper), (pack_upper, pack_lower))):
            own = [
                heavy(leaving[2 * pair, h][side], leaving[2 * pair + 1, h][side], lower_tall)
                for h in range(2)
            ]
            other = [
                light(leaving[2 * pair, h][side], leaving[2 * pair + 1, h][side], lower_tall)
                for h in range(2)
            ]
            rows_even = slice(2 * pair * ZR, (2 * pair + 1) * ZR)
            rows_odd = slice((2 * pair + 1) * ZR, (2 * pair + 2) * ZR)
            touch = [
                light(contact[1 - side][h][rows_even], contact[1 - side][h][rows_odd], lower_tall)
                for h in range(2)
            ]
            own[1] = jnp.where(tall < 96, own[1], roll_lanes(other[1], 64))
            mixed = jnp.where(tall < 32, other[1], other[0])
            spare = jnp.zeros((8, 128), f32)
            for group in range(6):
                value = touch[1][group // 2 * 8 : group // 2 * 8 + 8]
                swapped = pltpu.roll(value, 4, 0)
                if group % 2 == 0:
                    value = jnp.where(lower_rows, value, swapped)
                else:
                    value = jnp.where(lower_rows, swapped, value)
                inside = (narrow >= 16 * group) & (narrow < 16 * group + 8)
                spare = jnp.where(inside, roll_lanes(value, 16 * group - 48), spare)
            mixed = jnp.concatenate(
                [
                    jnp.where(lower_rows & (core == 1), spare, mixed[0:8]),
                    mixed[8:16],
                    jnp.where(lower_rows | (core == 1), mixed[16:24], spare),
                ],
                axis=0,
            )
            sides.append(own + [mixed, jnp.where(tall >= 48, touch[0], touch[1])])
        places = (2 * pair * ZR, (2 * pair + 1) * ZR, 96 + pair * ZR, 144 + pair * ZR)
        for at, plus, minus in zip(places, *sides):
            put_pair(one_ref, two_ref, slice(at, at + ZR), even, plus, minus)


def bins_of(depart_ref, depart_count_ref, depart_block_ref, direction):
    values = [depart_ref[c, 4 * direction : 4 * direction + 4, :] for c in CARRIED]
    row = sub_iota((4, 128))
    for ref in (depart_count_ref, depart_block_ref):
        value = jnp.zeros((4, 128), jnp.int32)
        for member in range(4):
            value = jnp.where(row == member, ref[0, 0, 0, member, direction], value)
        values.append(value.astype(f32))
    return values


def pack_lower(even_c, odd_c, lower):
    return jnp.where(lower, even_c, roll_lanes(odd_c, 4))


def pack_upper(even_c, odd_c, lower):
    return jnp.where(lower, roll_lanes(even_c, -4), odd_c)


def put_pair(one_ref, two_ref, at, even, plus, minus):
    one_ref[at, :] = jnp.where(even, plus, minus)
    two_ref[at, :] = jnp.where(even, minus, plus)


def take_pair(one_ref, two_ref, at, even):
    one, two = one_ref[at, :], two_ref[at, :]
    return jnp.where(even, two, one), jnp.where(even, one, two)


def stage_kernel(window_in, bins_in, state_ref, window_ref, bins_ref, plane_ref, weight_ref):
    window_ref[...] = window_in[...]
    bins_ref[...] = bins_in[...]
    nodes = sub_iota((8, 128)).astype(f32) - 2.0

    def one_bin(index, carry):
        place = [state_ref[axis, pl.ds(index, 1), :] for axis in range(3)]
        high, low, wz, lever = collect_terms(place, nodes)
        plane_ref[index, 0:64, :] = high
        plane_ref[index, 64:128, :] = low
        weight_ref[index, 0:8, :] = wz
        weight_ref[index, 8:16, :] = lever
        return carry

    lax.fori_loop(0, 32, one_bin, 0, unroll=8)


def collect_terms(place, nodes):
    high, low = parts(plane_of(spline(place[0], nodes), spline(place[1], nodes)))
    wz = spline(place[2], nodes)
    return high, low, wz, wz * (nodes - place[2])


def second_kernel(window_in, from_one, from_two, bins_ref, window_ref, one_ref, two_ref):
    even = lax.axis_index("gx") % 2 == 0
    even_second = lax.axis_index("gy") % 2 == 0
    lanes = lane_iota((ZR, 128))
    lower = lanes % 8 < 4
    core = lax.axis_index("gz")
    narrow = lane_iota((8, 128))
    lower_rows = sub_iota((8, 128)) < 4
    got = [[[None, None], [None, None]] for _ in range(8)]
    for pair in range(2):
        places = (2 * pair * ZR, (2 * pair + 1) * ZR, 96 + pair * ZR, 144 + pair * ZR)
        taken = [take_pair(from_one, from_two, slice(at, at + ZR), even) for at in places]
        for side in range(2):
            own = [taken[0][side], taken[1][side]]
            mixed, touch = taken[2][side], taken[3][side]
            spare = jnp.where(core == 0, mixed[16:24], mixed[0:8])
            swapped = pltpu.roll(spare, 4, 0)
            spare = jnp.where(lower_rows == (core == 1), spare, swapped)
            mixed = jnp.concatenate(
                [
                    jnp.where(lower_rows & (core == 1), 0.0, mixed[0:8]),
                    mixed[8:16],
                    jnp.where(lower_rows | (core == 1), mixed[16:24], 0.0),
                ],
                axis=0,
            )
            other = [
                jnp.where(lanes >= 32, mixed, 0.0),
                jnp.where(
                    lanes < 32, mixed, jnp.where(lanes < 64, roll_lanes(own[1], -64), 0.0)
                ),
            ]
            own[1] = jnp.where(lanes < 96, own[1], 0.0)
            rest = [
                jnp.where(
                    lower_rows,
                    roll_lanes(spare, 48 - 32 * tile),
                    roll_lanes(spare, 32 - 32 * tile),
                )
                for tile in range(3)
            ]
            rest = jnp.concatenate(rest, axis=0)
            touched = [
                jnp.where(lanes >= 48, touch, 0.0),
                jnp.where(lanes < 48, touch, jnp.where(lanes < 56, rest, 0.0)),
            ]
            for half in range(2):
                values = (own[half], other[half]) if side == 0 else (other[half], own[half])
                got[2 * pair][side][half] = jnp.where(lower, values[0], roll_lanes(values[1], 4))
                got[2 * pair + 1][side][half] = jnp.where(
                    lower, roll_lanes(values[0], -4), values[1]
                )
                value = touched[half]
                if side == 0:
                    got[4 + 2 * pair][side][half] = jnp.where(lower, value, 0.0)
                    got[5 + 2 * pair][side][half] = jnp.where(lower, roll_lanes(value, -4), 0.0)
                else:
                    got[4 + 2 * pair][side][half] = jnp.where(lower, 0.0, roll_lanes(value, 4))
                    got[5 + 2 * pair][side][half] = jnp.where(lower, 0.0, value)
    new = [[[None, None], [None, None]] for _ in range(8)]
    for c in range(8):
        for window in range(2):
            for half in range(2):
                columns = slice(128 * half, 128 * half + 128)
                value = window_in[window, c, :, columns] + got[c][window][half]
                new[c][window][half] = value
                window_ref[window, c, :, columns] = value
    for c in range(4):
        near, far = new[c]
        plus = jnp.where(lanes < 64, roll_lanes(near[1], -32), roll_lanes(far[1], 32))
        minus = jnp.where(lanes < 64, near[0], roll_lanes(far[0], 64))
        put_pair(one_ref, two_ref, slice(c * ZR, (c + 1) * ZR), even_second, plus, minus)
    for pair in range(2):
        at = slice(96 + pair * ZR, 96 + (pair + 1) * ZR)
        even_c, odd_c = new[4 + 2 * pair], new[5 + 2 * pair]
        sides = []
        for half in (1, 0):
            sides.append(
                jnp.where(
                    lanes < 64,
                    jnp.where(lanes < 32, roll_lanes(even_c[0][half], -32), even_c[1][half]),
                    jnp.where(
                        lanes < 96, roll_lanes(odd_c[0][half], 32), roll_lanes(odd_c[1][half], 64)
                    ),
                )
            )
        put_pair(one_ref, two_ref, at, even_second, sides[0], sides[1])
    put_pair(
        one_ref, two_ref, slice(144, 184), even_second, bins_ref[0:40, :], bins_ref[40:80, :]
    )


def third_kernel(window_in, from_one, from_two, bins_ref, window_ref, message_ref):
    even = lax.axis_index("gy") % 2 == 0
    core = lax.axis_index("gz")
    lanes = lane_iota((ZR, 128))
    for window in range(2):
        for c in range(8):
            if c < 4:
                near, far = take_pair(from_one, from_two, slice(c * ZR, (c + 1) * ZR), even)
                near = jnp.where(
                    (lanes >= 32) & (lanes < 96),
                    roll_lanes(near, 32 if window == 0 else -32),
                    0.0,
                )
                far = jnp.where(lanes < 64, far if window == 0 else roll_lanes(far, 64), 0.0)
            else:
                at = slice(96 + (c - 4) // 2 * ZR, 96 + ((c - 4) // 2 + 1) * ZR)
                shift = (32, 0, -32, -64)[2 * (c % 2) + window]
                inside = (lanes >= 32) & (lanes < 64)
                near, far = take_pair(from_one, from_two, at, even)
                near = jnp.where(inside, roll_lanes(near, shift), 0.0)
                far = jnp.where(inside, roll_lanes(far, shift), 0.0)
            for half, extra in ((0, near), (1, far)):
                columns = slice(128 * half, 128 * half + 128)
                value = window_in[window, c, :, columns] + extra
                window_ref[window, c, :, columns] = value
                at = ((window * 8 + c) * 2 + half) * 8
                message_ref[at : at + 8, :] = jnp.where(core == 0, value[16:24], value[0:8])
    message_ref[256:296, :] = bins_ref[80:120, :]


def advance(sums):
    mass = jnp.maximum(sums[0], mass_floor)
    previous = [sums[1 + axis] / mass for axis in range(3)]
    velocity = [previous[0], previous[1], previous[2] - time_step * gravity]
    normal = sums[4:7]
    scale = 1.0 + (normal[0] * normal[0] + normal[1] * normal[1] + normal[2] * normal[2])
    dot = velocity[0] * normal[0] + velocity[1] * normal[1] + velocity[2] * normal[2]
    inward = jnp.minimum(dot, 0.0) / scale
    velocity = [velocity[axis] - inward * normal[axis] for axis in range(3)]
    dot = velocity[0] * normal[0] + velocity[1] * normal[1] + velocity[2] * normal[2]
    along = dot / scale
    damp = 1.0 - jnp.exp(-sums[7])
    velocity = [
        velocity[axis] - damp * (velocity[axis] - along * normal[axis]) for axis in range(3)
    ]
    return velocity + previous


def collect_kernel(
    window_in,
    from_z,
    x_one,
    x_two,
    y_one,
    y_two,
    plane_ref,
    weight_ref,
    state_ref,
    bin_count_ref,
    moved_ref,
    arrived_ref,
    data,
    fields,
    turned,
    table,
    picked,
    live,
    target,
    moved,
    arrived,
    semaphores,
):
    core = lax.axis_index("gz")
    row = lax.axis_index("gy")
    lanes = lane_iota((8, 128))
    subs = sub_iota((8, 128))
    lower_rows = subs < 4
    lower_lanes = lanes % 8 < 4

    even_first = lax.axis_index("gx") % 2 == 0
    even_second = lax.axis_index("gy") % 2 == 0
    arrivals = []
    for one_ref, two_ref, begin, even in ((x_one, x_two, 192, even_first), (y_one, y_two, 144, even_second)):
        pairs = [
            take_pair(one_ref, two_ref, slice(begin + 4 * part, begin + 4 * part + 4), even)
            for part in range(PARTS)
        ]
        arrivals += [[pair[0] for pair in pairs], [pair[1] for pair in pairs]]
    arrivals.append([from_z[256 + 4 * part : 260 + 4 * part, :] for part in range(PARTS)])
    for g, values in enumerate(arrivals):
        for part in range(7):
            data[part, 4 * g : 4 * g + 4, :] = values[part]
        slot = lane_iota((4, 128)).astype(f32)
        live[32 + 4 * g : 36 + 4 * g, :] = jnp.where(slot < values[7], 1.0, 0.0)
        block = values[8].astype(jnp.int32)
        for member in range(4):
            target[4 * g + member] = block[member, 0]

    below = core == 0
    above = core == 1
    taken = [
        jnp.logical_not(lower_rows) & above,
        (lower_rows & above) | (jnp.logical_not(lower_rows) & below),
        lower_rows & below,
    ]
    for third in range(3):
        rows = slice(8 * third, 8 * third + 8)
        for half in range(2):
            columns = slice(128 * half, 128 * half + 128)
            sums = [[], []]
            for c in range(8):
                values = [window_in[b, c, rows, columns] for b in range(2)]
                for b in range(2):
                    at = ((b * 8 + c) * 2 + half) * 8
                    edge = pltpu.roll(from_z[at : at + 8, :], 4, 0)
                    values[b] = values[b] + jnp.where(taken[third], edge, 0.0)
                sums[0].append(
                    values[0] + jnp.where(lower_lanes, 0.0, roll_lanes(values[1], 4))
                )
                sums[1].append(
                    values[1] + jnp.where(lower_lanes, roll_lanes(values[0], -4), 0.0)
                )
            node_second = row * 16 + (lanes + 128 * half) // 8 - 6
            node_third = core * 12 + subs + 8 * third - 2
            inside = (
                (node_second >= 0) & (node_second < 128) & (node_third >= 0) & (node_third < 32)
            )
            for b in range(2):
                for c, value in enumerate(advance(sums[b])):
                    fields[b, c, rows, columns] = jnp.where(inside, value, 0.0)

    wide = lane_iota((ZR, 128))
    local = wide % 64
    node_first = (local % 8).astype(f32) - 2.0 - center
    node_second = (local // 8).astype(f32) - 2.0 - center
    for b in range(2):
        for c in range(6):
            low = fields[b, c, :, 0:128]
            high = fields[b, c, :, 128:256]
            shown = [
                jnp.where(wide < 64, roll_lanes(low, -32), roll_lanes(low, 32)),
                jnp.where(wide < 64, roll_lanes(low, 64), low),
                jnp.where(
                    wide < 64,
                    jnp.where(wide < 32, roll_lanes(low, 32), roll_lanes(high, 32)),
                    jnp.where(wide < 96, roll_lanes(low, -32), roll_lanes(high, 96)),
                ),
                jnp.where(wide < 64, high, roll_lanes(high, 64)),
            ]
            for second in range(4):
                turned[second, :, c, :] = shown[second]
                if c < 3:
                    turned[second, :, 6 + c, :] = shown[second] * node_first
                    turned[second, :, 9 + c, :] = shown[second] * node_second
        for second in range(4):
            value = turned[second].reshape(ZR * 16, 128)
            high, low = parts(value)
            table[4 * b + second, :, 0:128] = high
            table[4 * b + second, :, 128:256] = low

    nodes = subs.astype(f32) - 2.0

    def one_bin(index, column, third, high, low, wz, lever):
        right = jnp.concatenate([high, low, high, low], axis=0)
        left = table[column, pl.ds(64 * third, 128), :]
        values = jnp.dot(left, right, preferred_element_type=f32)
        first = values[0:8] * wz[0:1]
        second = values[8:16] * wz[0:1]
        moment = values[0:8] * lever[0:1]
        for k in range(1, 8):
            first = first + values[16 * k : 16 * k + 8] * wz[k : k + 1]
            second = second + values[16 * k + 8 : 16 * k + 16] * wz[k : k + 1]
            moment = moment + values[16 * k : 16 * k + 8] * lever[k : k + 1]
        picked[0:8, index, :] = first
        picked[8:16, index, :] = second
        picked[16:24, index, :] = moment

    def residents(step, carry):
        first = step // 4
        second = step % 4
        for third in range(4):
            index = step * 4 + third
            high, low = plane_ref[index, 0:64, :], plane_ref[index, 64:128, :]
            wz, lever = weight_ref[index, 0:8, :], weight_ref[index, 8:16, :]
            one_bin(index, step, third + core, high, low, wz, lever)
            count = bin_count_ref[first, second, third]
            live[pl.ds(index, 1), :] = jnp.where(lane_iota((1, 128)) < count, 1.0, 0.0)
        return carry

    def movers(step, carry):
        for member in range(4):
            index = 4 * step + member
            block = target[index]
            terms = collect_terms([data[axis, pl.ds(index, 1), :] for axis in range(3)], nodes)
            one_bin(32 + index, block // 4, block % 4 + core, *terms)
        return carry

    lax.fori_loop(0, 5, movers, 0, unroll=5)

    def finish(begin, size, old):
        rows = slice(begin, begin + size)
        valid = live[rows, :]
        got = [picked[c, rows, :] for c in range(19)]
        result = []
        for axis in range(3):
            result.append(old[axis] + time_step * got[axis])
        for axis in range(3):
            result.append(
                flip_ratio * (old[3 + axis] + got[axis] - got[3 + axis])
                + (1.0 - flip_ratio) * got[axis]
            )
        affine = []
        for axis in range(3):
            affine.append(4.0 * (got[6 + axis] - (old[0] - center) * got[axis]))
            affine.append(4.0 * (got[9 + axis] - (old[1] - center) * got[axis]))
            affine.append(4.0 * got[16 + axis])
        result += affine
        result.append(old[6] * (1.0 + time_step * (affine[0] + affine[4] + affine[8])))
        return [value * valid for value in result]

    for g in range(3):
        begin, size = 8 * g, 8 if g < 2 else 4
        rows = slice(begin, begin + size)
        for c, value in enumerate(finish(32 + begin, size, [data[p, rows, :] for p in range(7)])):
            if g < 2:
                arrived[c, rows, :] = value
            else:
                arrived[c, 16:20, :] = jnp.where(core == 1, value, 0.0)
                arrived[c, 20:24, :] = jnp.where(core == 0, value, 0.0)
    arrived_copy = pltpu.make_async_copy(arrived, arrived_ref, semaphores.at[0])
    arrived_copy.start()
    moved_copies = []
    for part in range(2):
        lax.fori_loop(4 * part, 4 * part + 4, residents, 0, unroll=4)
        for g in range(2 * part, 2 * part + 2):
            rows = slice(8 * g, 8 * g + 8)
            for c, value in enumerate(finish(8 * g, 8, [state_ref[c, rows, :] for c in CARRIED])):
                moved[c, rows, :] = value
        where = (slice(None), pl.ds(16 * part, 16))
        moved_copies.append(
            pltpu.make_async_copy(moved.at[where], moved_ref.at[where], semaphores.at[1 + part])
        )
        moved_copies[-1].start()
    arrived_copy.wait()
    for copy in moved_copies:
        copy.wait()


def pairs_along(axis, first, closed):
    count = lax.axis_size(axis)
    route = [(i, (i + 1) % count) for i in range(first, count, 2) if closed or i + 1 < count]
    return route + [(j, i) for i, j in route]


vmem = pl.BlockSpec(memory_space=pltpu.VMEM)
smem = pl.BlockSpec(memory_space=pltpu.SMEM)
limits = pltpu.CompilerParams(vmem_limit_bytes=48 * 1024 * 1024)


def shape_of(*dims):
    return jax.ShapeDtypeStruct(dims, f32)


def body(
    state,
    bin_count,
    departing,
    depart_count,
    depart_block,
    cut_cell,
    quad_count,
    wall_id,
    cut_level,
    wall_normal,
    wall_friction,
):
    state_rows = state.reshape(16, 32, 128)
    leaving = departing.reshape(16, 24, 128)
    cut = [value.reshape(4, 128) for value in (cut_cell, quad_count, wall_id, cut_level)]
    depart_count = jnp.swapaxes(depart_count, 3, 4)
    depart_block = jnp.swapaxes(depart_block, 3, 4)
    operands = (
        state_rows,
        bin_count,
        leaving,
        depart_count,
        depart_block,
        *cut,
        wall_normal,
        wall_friction,
    )
    operands = tuple(pltpu.with_memory_space_constraint(value, pltpu.HBM) for value in operands)
    scalars = (1, 3, 4, 9, 10)
    window, one, two, bins = pl.pallas_call(
        deposit_kernel,
        out_shape=[
            shape_of(2, 8, ZR, LN),
            shape_of(XROWS, 128),
            shape_of(XROWS, 128),
            shape_of(3 * BINROWS, 128),
        ],
        in_specs=[pl.BlockSpec(memory_space=pltpu.HBM)] * 11,
        out_specs=[vmem] * 4,
        scratch_shapes=[
            (pltpu.SMEM if place in scalars else pltpu.VMEM)(value.shape, value.dtype)
            for place, value in enumerate(operands)
        ]
        + [
            pltpu.VMEM((16, 56, 128), f32),
            pltpu.VMEM((4, 6, 32, LN), f32),
            pltpu.SemaphoreType.DMA((11,)),
        ],
        compiler_params=limits,
        name="deposit",
    )(*operands)
    x_one = lax.ppermute(one, "gx", pairs_along("gx", 0, True))
    x_two = lax.ppermute(two, "gx", pairs_along("gx", 1, True))
    window, bins, planes, weights = pl.pallas_call(
        stage_kernel,
        out_shape=[
            shape_of(2, 8, ZR, LN),
            shape_of(3 * BINROWS, 128),
            jax.ShapeDtypeStruct((32, 128, 128), bf16),
            shape_of(32, 16, 128),
        ],
        in_specs=[vmem] * 3,
        out_specs=[vmem] * 4,
        cost_estimate=pl.CostEstimate(flops=10**9, bytes_accessed=2**20, transcendentals=0),
        compiler_params=limits,
        name="stage",
    )(window, bins, state_rows)
    window, one, two = pl.pallas_call(
        second_kernel,
        out_shape=[shape_of(2, 8, ZR, LN), shape_of(YROWS, 128), shape_of(YROWS, 128)],
        in_specs=[vmem] * 4,
        out_specs=[vmem] * 3,
        compiler_params=limits,
        name="take_x",
    )(window, x_one, x_two, bins)
    y_one = lax.ppermute(one, "gy", pairs_along("gy", 0, False))
    y_two = lax.ppermute(two, "gy", pairs_along("gy", 1, False))
    window, message = pl.pallas_call(
        third_kernel,
        out_shape=[shape_of(2, 8, ZR, LN), shape_of(ZROWS, 128)],
        in_specs=[vmem] * 4,
        out_specs=[vmem] * 2,
        compiler_params=limits,
        name="take_y",
    )(window, y_one, y_two, bins)
    from_z = lax.ppermute(message, "gz", [(0, 1), (1, 0)])
    moved, arrived = pl.pallas_call(
        collect_kernel,
        out_shape=[shape_of(16, 32, 128), shape_of(16, 24, 128)],
        in_specs=[vmem] * 9 + [smem],
        out_specs=[pl.BlockSpec(memory_space=pltpu.HBM)] * 2,
        scratch_shapes=[
            pltpu.VMEM((7, 24, 128), f32),
            pltpu.VMEM((2, 6, ZR, LN), f32),
            pltpu.VMEM((4, ZR, 16, 128), f32),
            pltpu.VMEM((8, ZR * 16, 256), bf16),
            pltpu.VMEM((24, 56, 128), f32),
            pltpu.VMEM((56, 128), f32),
            pltpu.SMEM((20,), jnp.int32),
            pltpu.VMEM((16, 32, 128), f32),
            pltpu.VMEM((16, 24, 128), f32),
            pltpu.SemaphoreType.DMA((3,)),
        ],
        compiler_params=limits,
        name="collect",
    )(
        window,
        from_z,
        x_one,
        x_two,
        y_one,
        y_two,
        planes,
        weights,
        state_rows,
        bin_count,
    )
    return moved.reshape(state.shape), arrived.reshape(departing.shape)


def solution(mesh):
    placed = (
        P(None, "gx", "gy", "gz", None),
        P("gx", "gy", "gz"),
        P(None, "gx", "gy", "gz", None, None, None),
        P("gx", "gy", "gz", None, None),
        P("gx", "gy", "gz", None, None),
        P("gx", "gy", "gz", None),
        P("gx", "gy", "gz", None),
        P("gx", "gy", "gz", None),
        P("gx", "gy", "gz", None),
        P(),
        P(),
    )
    return jax.shard_map(
        body,
        mesh=mesh,
        in_specs=placed,
        out_specs=(P(None, "gx", "gy", "gz", None), P(None, "gx", "gy", "gz", None, None, None)),
        check_vma=False,
    )
```

```python
import jax
import jax.numpy as jnp
import numpy as np
from jax import lax
from jax.experimental import pallas as pl
from jax.experimental.pallas import tpu as pltpu
from jax.sharding import PartitionSpec as P

time_step = 0.1
stiffness = 4.0
gravity = 2.0
flip_ratio = 0.95
mass_floor = 0.25
center = 1.5
quad_points = [
    [0.5, 0.5, 0.5],
    [0.2, 0.7, 0.35],
    [0.8, 0.3, 0.65],
    [0.35, 0.15, 0.85],
    [0.65, 0.85, 0.15],
    [0.1, 0.45, 0.55],
    [0.9, 0.55, 0.45],
    [0.45, 0.9, 0.75],
]
f32 = jnp.float32
bf16 = jnp.bfloat16

ZR = 24
LN = 256
CARRIED = (0, 1, 2, 3, 4, 5, 15)
PARTS = 9
BINROWS = 40
XROWS = 96 + 48 + 48 + BINROWS
YROWS = 96 + 48 + BINROWS
ZROWS = 256 + BINROWS


def lane_iota(shape):
    return lax.broadcasted_iota(jnp.int32, shape, len(shape) - 1)


def sub_iota(shape):
    return lax.broadcasted_iota(jnp.int32, shape, len(shape) - 2)


def spline(coord, nodes):
    distance = jnp.abs(coord - nodes)
    inner = 0.75 - distance * distance
    reach = jnp.maximum(1.5 - distance, 0.0)
    return jnp.where(distance < 0.5, inner, 0.5 * reach * reach)


def parts(value):
    high = value.astype(bf16)
    low = (value - high.astype(f32)).astype(bf16)
    return high, low


def plane_of(wx, wy):
    return jnp.concatenate([wy[y : y + 1] * wx for y in range(8)], axis=0)


def roll_lanes(value, shift):
    return pltpu.roll(value, shift % 128, 1)


def contact_terms(cell_ref, quad_ref, wall_ref, level_ref, normal_ref, friction_ref):
    cells = cell_ref[...]
    counts = quad_ref[...]
    walls = wall_ref[...]
    level = level_ref[...]
    normal = []
    for axis in range(3):
        part = jnp.zeros_like(level)
        for wall in range(4):
            part = jnp.where(walls == wall, normal_ref[wall, axis], part)
        normal.append(part)
    friction = jnp.zeros_like(level)
    for wall in range(4):
        friction = jnp.where(walls == wall, friction_ref[wall], friction)
    inverse = 1.0 / jnp.maximum(counts, 1).astype(f32)
    weights = [None] * 8
    for q, point in enumerate(quad_points):
        level_set = level + (normal[0] * point[0] + normal[1] * point[1] + normal[2] * point[2])
        cover = jnp.clip(0.5 - level_set, 0.0, 1.0)
        share = jnp.where(counts > q, cover * inverse, 0.0)
        for corner in range(8):
            factor = 1.0
            for axis in range(3):
                bit = (corner >> (2 - axis)) & 1
                factor *= point[axis] if bit else 1.0 - point[axis]
            term = share * factor
            weights[corner] = term if weights[corner] is None else weights[corner] + term
    return cells, weights, normal + [friction]


def contact_windows(cell_ref, quad_ref, wall_ref, level_ref, normal_ref, friction_ref):
    cells, weights, factors = contact_terms(
        cell_ref, quad_ref, wall_ref, level_ref, normal_ref, friction_ref
    )
    place_third = cells % 16 + 2 + 4 * lax.axis_index("gz")
    column = (cells // 16) % 16 * 8 + cells // 256
    rows = sub_iota((ZR, 128))
    bit_rows = sub_iota((128, 128))
    lefts_high = []
    lefts_low = []
    rights = []
    for tile in range(4):
        third = place_third[tile : tile + 1]
        first_row = rows == third
        second_row = rows == third + 1
        pieces_high = []
        pieces_low = []
        for pair in range(4):
            lower = weights[2 * pair][tile : tile + 1]
            upper = weights[2 * pair + 1][tile : tile + 1]
            for channel in range(4):
                factor = factors[channel][tile : tile + 1]
                value = jnp.where(
                    first_row, lower * factor, jnp.where(second_row, upper * factor, 0.0)
                )
                high, low = parts(value)
                pieces_high.append(high.astype(f32))
                pieces_low.append(low.astype(f32))
        lefts_high.append(jnp.concatenate(pieces_high, axis=0).astype(bf16))
        lefts_low.append(jnp.concatenate(pieces_low, axis=0).astype(bf16))
        rights.append(
            jnp.where(bit_rows == column[tile : tile + 1], 1.0, 0.0).astype(bf16)
        )
    left = jnp.concatenate(lefts_high + lefts_low, axis=1)
    right = jnp.concatenate(rights + rights, axis=1)
    touched = lax.dot_general(
        left, right, (((1,), (1,)), ((), ())), preferred_element_type=f32
    )
    lanes = lane_iota((4 * ZR, 128))
    first = lanes % 8
    result = [[None, None], [None, None]]
    for pair in range(4):
        dx, dy = pair >> 1, pair & 1
        block = touched[pair * 4 * ZR : (pair + 1) * 4 * ZR]
        near = jnp.where(first <= 5 - dx, block, 0.0)
        far = jnp.where(first >= 6 - dx, block, 0.0)
        for window, (value, shift) in enumerate(
            ((near, 50 + 8 * dy + dx), (far, 46 + 8 * dy + dx))
        ):
            turned = roll_lanes(value, shift)
            for half, piece in enumerate(
                (jnp.where(lanes >= shift, turned, 0.0), jnp.where(lanes < shift, turned, 0.0))
            ):
                known = result[window][half]
                result[window][half] = piece if known is None else known + piece
    return result


def deposit_kernel(*refs):
    inputs, (window_ref, one_ref, two_ref, bins_ref) = refs[:11], refs[11:15]
    even = lax.axis_index("gx") % 2 == 0
    copies, (data, total, semaphores) = refs[15:26], refs[26:]

    started = []
    for place in (5, 6, 7, 8, 9, 10, 0, 2, 1, 3, 4):
        started.append(
            pltpu.make_async_copy(inputs[place], copies[place], semaphores.at[place])
        )
        started[-1].start()
    state_ref, bin_count_ref, depart_ref, depart_count_ref, depart_block_ref = copies[:5]
    for window in (0, 3):
        total[window] = jnp.zeros((6, 32, LN), f32)
    for window in (1, 2):
        for third in (0, 5):
            total[window, third] = jnp.zeros((32, LN), f32)
    for copy in started[:6]:
        copy.wait()
    contact = contact_windows(*copies[5:])
    for window in range(2):
        for half in range(2):
            for c in range(4):
                window_ref[window, 4 + c, :, 128 * half : 128 * half + 128] = contact[window][
                    half
                ][ZR * c : ZR * c + ZR]
    for copy in started[6:]:
        copy.wait()

    core = lax.axis_index("gz")
    plus = bins_of(depart_ref, depart_count_ref, depart_block_ref, 0)
    minus = bins_of(depart_ref, depart_count_ref, depart_block_ref, 1)
    for part in range(PARTS):
        at = 192 + 4 * part
        put_pair(one_ref, two_ref, slice(at, at + 4), even, plus[part], minus[part])
    south = bins_of(depart_ref, depart_count_ref, depart_block_ref, 2)
    north = bins_of(depart_ref, depart_count_ref, depart_block_ref, 3)
    up = bins_of(depart_ref, depart_count_ref, depart_block_ref, 4)
    down = bins_of(depart_ref, depart_count_ref, depart_block_ref, 5)
    for part in range(PARTS):
        bins_ref[4 * part : 4 * part + 4, :] = south[part]
        bins_ref[40 + 4 * part : 44 + 4 * part, :] = north[part]
        bins_ref[80 + 4 * part : 84 + 4 * part, :] = jnp.where(core == 0, up[part], down[part])

    size = 8
    groups = [(state_ref, 8 * g, 8 * g) for g in range(4)]
    groups += [(depart_ref, 8 * g, 32 + 8 * g) for g in range(3)]
    for ref, begin, place in groups:
        channel = [ref[c, begin : begin + size, :] for c in range(16)]
        pressure = time_step * 4.0 * stiffness * jnp.maximum(1.0 - channel[15], 0.0)
        spread = [channel[6 + e] + (pressure if e % 4 == 0 else 0.0) for e in range(9)]
        offset = [channel[axis] - center for axis in range(3)]
        for axis in range(3):
            data[axis, place : place + size, :] = channel[axis]
            data[3 + axis, place : place + size, :] = (
                channel[3 + axis]
                - spread[3 * axis] * offset[0]
                - spread[3 * axis + 1] * offset[1]
                - spread[3 * axis + 2] * offset[2]
            )
        for entry in range(9):
            data[6 + entry, place : place + size, :] = spread[entry]

    nodes = sub_iota((8, 128)).astype(f32) - 2.0
    slots = lane_iota((8, 128))
    lanes = lane_iota((32, 128))
    local = lane_iota((8, 128)) % 64
    node_first = (local % 8).astype(f32) - 2.0 - center
    node_second = (local // 8).astype(f32) - 2.0 - center
    node_third = nodes - center

    def one_bin(index, begin, count):
        def row(channel):
            return data[channel, pl.ds(index, 1), :]

        wx = spline(row(0), nodes)
        wy = spline(row(1), nodes)
        wz = jnp.where(slots < count, spline(row(2), nodes), 0.0)
        lifted = jnp.concatenate([wz] + [row(3 + c) * wz for c in range(12)], axis=0)
        lift_high, lift_low = parts(lifted)
        plane_high, plane_low = parts(plane_of(wx, wy))
        left = jnp.concatenate([lift_high, lift_low], axis=1)
        right = jnp.concatenate([plane_high, plane_low], axis=0)
        right = jnp.concatenate([right, right], axis=1)
        moments = lax.dot_general(
            left, right, (((1,), (1,)), ((), ())), preferred_element_type=f32
        )
        sums = [moments[0:8]]
        for axis in range(3):
            at = 32 + 24 * axis
            sums.append(
                moments[8 + 8 * axis : 16 + 8 * axis]
                + moments[at : at + 8] * node_first
                + moments[at + 8 : at + 16] * node_second
                + moments[at + 16 : at + 24] * node_third
            )
        both = jnp.concatenate(sums, axis=0)
        turned = pltpu.roll(both + roll_lanes(both, 64), begin % 128, 1)
        inside = (lanes >= begin) & (lanes < begin + 64)
        beyond = (lanes >= begin - 128) & (lanes < begin - 64)
        return jnp.where(inside, turned, 0.0), jnp.where(beyond, turned, 0.0)

    def residents(step, carry):
        first = step // 4
        third = step % 4
        low, high = None, None
        for second in range(4):
            one, two = one_bin(
                first * 16 + second * 4 + third,
                32 * (second + 1),
                bin_count_ref[first, second, third],
            )
            low = one if low is None else low + one
            high = two if high is None else high + two
        total[first + 1, third + 1, :, 0:128] = low
        total[first + 1, third + 1, :, 128:256] = high
        return carry

    lax.fori_loop(0, 8, residents, 0, unroll=4)

    def leavers(member, carry):
        for direction in range(5):
            block = depart_block_ref[0, 0, 0, member, direction]
            count = depart_count_ref[0, 0, 0, member, direction]
            index = 32 + direction * 4 + member
            window = block // 16 + 1
            begin = 32 * (block // 4 % 4 + 1)
            third = block % 4 + 1
            if direction < 2:
                window = 3 if direction == 0 else 0
            elif direction < 4:
                begin = 160 if direction == 2 else 0
            else:
                block = depart_block_ref[0, 0, 0, member, 4 + core]
                count = depart_count_ref[0, 0, 0, member, 4 + core]
                index = 48 + 4 * core + member
                window = block // 16 + 1
                begin = 32 * (block // 4 % 4 + 1)
                third = 5 - 5 * core
            one, two = one_bin(index, begin, count)
            total[window, third, :, 0:128] += one
            total[window, third, :, 128:256] += two
        return carry

    lax.fori_loop(0, 4, leavers, 0, unroll=4)

    lower_rows = sub_iota((8, 128)) < 4
    lower_lanes = lane_iota((8, 128)) % 8 < 4
    lower_tall = lane_iota((ZR, 128)) % 8 < 4
    leaving = {}
    for half in range(2):
        columns = slice(128 * half, 128 * half + 128)
        for c in range(4):
            folded = []
            for window in range(4):
                piece = [
                    total[window, third + 1 - core, 8 * c : 8 * c + 8, columns]
                    for third in range(5)
                ]
                one = pltpu.roll(piece[1], 4, 0)
                three = pltpu.roll(piece[3], 4, 0)
                folded.append(
                    jnp.concatenate(
                        [
                            piece[0] + jnp.where(lower_rows, 0.0, one),
                            piece[2] + jnp.where(lower_rows, one, three),
                            piece[4] + jnp.where(lower_rows, three, 0.0),
                        ],
                        axis=0,
                    )
                )
            window_ref[0, c, :, columns] = folded[1] + jnp.where(
                lower_tall, roll_lanes(folded[0], -4), 0.0
            )
            window_ref[1, c, :, columns] = folded[2] + jnp.where(
                lower_tall, 0.0, roll_lanes(folded[3], 4)
            )
            leaving[c, half] = (
                folded[3] + jnp.where(lower_tall, roll_lanes(folded[2], -4), 0.0),
                folded[0] + jnp.where(lower_tall, 0.0, roll_lanes(folded[1], 4)),
            )
    tall = lane_iota((ZR, 128))
    narrow = lane_iota((8, 128))
    for pair in range(2):
        sides = []
        for side, (heavy, light) in enumerate(((pack_lower, pack_upper), (pack_upper, pack_lower))):
            own = [
                heavy(leaving[2 * pair, h][side], leaving[2 * pair + 1, h][side], lower_tall)
                for h in range(2)
            ]
            other = [
                light(leaving[2 * pair, h][side], leaving[2 * pair + 1, h][side], lower_tall)
                for h in range(2)
            ]
            rows_even = slice(2 * pair * ZR, (2 * pair + 1) * ZR)
            rows_odd = slice((2 * pair + 1) * ZR, (2 * pair + 2) * ZR)
            touch = [
                light(contact[1 - side][h][rows_even], contact[1 - side][h][rows_odd], lower_tall)
                for h in range(2)
            ]
            own[1] = jnp.where(tall < 96, own[1], roll_lanes(other[1], 64))
            mixed = jnp.where(tall < 32, other[1], other[0])
            spare = jnp.zeros((8, 128), f32)
            for group in range(6):
                value = touch[1][group // 2 * 8 : group // 2 * 8 + 8]
                swapped = pltpu.roll(value, 4, 0)
                if group % 2 == 0:
                    value = jnp.where(lower_rows, value, swapped)
                else:
                    value = jnp.where(lower_rows, swapped, value)
                inside = (narrow >= 16 * group) & (narrow < 16 * group + 8)
                spare = jnp.where(inside, roll_lanes(value, 16 * group - 48), spare)
            mixed = jnp.concatenate(
                [
                    jnp.where(lower_rows & (core == 1), spare, mixed[0:8]),
                    mixed[8:16],
                    jnp.where(lower_rows | (core == 1), mixed[16:24], spare),
                ],
                axis=0,
            )
            sides.append(own + [mixed, jnp.where(tall >= 48, touch[0], touch[1])])
        places = (2 * pair * ZR, (2 * pair + 1) * ZR, 96 + pair * ZR, 144 + pair * ZR)
        for at, plus, minus in zip(places, *sides):
            put_pair(one_ref, two_ref, slice(at, at + ZR), even, plus, minus)


def bins_of(depart_ref, depart_count_ref, depart_block_ref, direction):
    values = [depart_ref[c, 4 * direction : 4 * direction + 4, :] for c in CARRIED]
    row = sub_iota((4, 128))
    for ref in (depart_count_ref, depart_block_ref):
        value = jnp.zeros((4, 128), jnp.int32)
        for member in range(4):
            value = jnp.where(row == member, ref[0, 0, 0, member, direction], value)
        values.append(value.astype(f32))
    return values


def pack_lower(even_c, odd_c, lower):
    return jnp.where(lower, even_c, roll_lanes(odd_c, 4))


def pack_upper(even_c, odd_c, lower):
    return jnp.where(lower, roll_lanes(even_c, -4), odd_c)


def put_pair(one_ref, two_ref, at, even, plus, minus):
    one_ref[at, :] = jnp.where(even, plus, minus)
    two_ref[at, :] = jnp.where(even, minus, plus)


def take_pair(one_ref, two_ref, at, even):
    one, two = one_ref[at, :], two_ref[at, :]
    return jnp.where(even, two, one), jnp.where(even, one, two)


def stage_kernel(window_in, bins_in, state_ref, window_ref, bins_ref, plane_ref, weight_ref):
    window_ref[...] = window_in[...]
    bins_ref[...] = bins_in[...]
    nodes = sub_iota((8, 128)).astype(f32) - 2.0

    def one_bin(index, carry):
        place = [state_ref[axis, pl.ds(index, 1), :] for axis in range(3)]
        high, low, wz, lever = collect_terms(place, nodes)
        plane_ref[index, 0:64, :] = high
        plane_ref[index, 64:128, :] = low
        weight_ref[index, 0:8, :] = wz
        weight_ref[index, 8:16, :] = lever
        return carry

    lax.fori_loop(0, 32, one_bin, 0, unroll=8)


def collect_terms(place, nodes):
    high, low = parts(plane_of(spline(place[0], nodes), spline(place[1], nodes)))
    wz = spline(place[2], nodes)
    return high, low, wz, wz * (nodes - place[2])


def second_kernel(window_in, from_one, from_two, bins_ref, window_ref, one_ref, two_ref):
    even = lax.axis_index("gx") % 2 == 0
    even_second = lax.axis_index("gy") % 2 == 1
    lanes = lane_iota((ZR, 128))
    lower = lanes % 8 < 4
    core = lax.axis_index("gz")
    narrow = lane_iota((8, 128))
    lower_rows = sub_iota((8, 128)) < 4
    got = [[[None, None], [None, None]] for _ in range(8)]
    for pair in range(2):
        places = (2 * pair * ZR, (2 * pair + 1) * ZR, 96 + pair * ZR, 144 + pair * ZR)
        taken = [take_pair(from_one, from_two, slice(at, at + ZR), even) for at in places]
        for side in range(2):
            own = [taken[0][side], taken[1][side]]
            mixed, touch = taken[2][side], taken[3][side]
            spare = jnp.where(core == 0, mixed[16:24], mixed[0:8])
            swapped = pltpu.roll(spare, 4, 0)
            spare = jnp.where(lower_rows == (core == 1), spare, swapped)
            mixed = jnp.concatenate(
                [
                    jnp.where(lower_rows & (core == 1), 0.0, mixed[0:8]),
                    mixed[8:16],
                    jnp.where(lower_rows | (core == 1), mixed[16:24], 0.0),
                ],
                axis=0,
            )
            other = [
                jnp.where(lanes >= 32, mixed, 0.0),
                jnp.where(
                    lanes < 32, mixed, jnp.where(lanes < 64, roll_lanes(own[1], -64), 0.0)
                ),
            ]
            own[1] = jnp.where(lanes < 96, own[1], 0.0)
            rest = [
                jnp.where(
                    lower_rows,
                    roll_lanes(spare, 48 - 32 * tile),
                    roll_lanes(spare, 32 - 32 * tile),
                )
                for tile in range(3)
            ]
            rest = jnp.concatenate(rest, axis=0)
            touched = [
                jnp.where(lanes >= 48, touch, 0.0),
                jnp.where(lanes < 48, touch, jnp.where(lanes < 56, rest, 0.0)),
            ]
            for half in range(2):
                values = (own[half], other[half]) if side == 0 else (other[half], own[half])
                got[2 * pair][side][half] = jnp.where(lower, values[0], roll_lanes(values[1], 4))
                got[2 * pair + 1][side][half] = jnp.where(
                    lower, roll_lanes(values[0], -4), values[1]
                )
                value = touched[half]
                if side == 0:
                    got[4 + 2 * pair][side][half] = jnp.where(lower, value, 0.0)
                    got[5 + 2 * pair][side][half] = jnp.where(lower, roll_lanes(value, -4), 0.0)
                else:
                    got[4 + 2 * pair][side][half] = jnp.where(lower, 0.0, roll_lanes(value, 4))
                    got[5 + 2 * pair][side][half] = jnp.where(lower, 0.0, value)
    new = [[[None, None], [None, None]] for _ in range(8)]
    for c in range(8):
        for window in range(2):
            for half in range(2):
                columns = slice(128 * half, 128 * half + 128)
                value = window_in[window, c, :, columns] + got[c][window][half]
                new[c][window][half] = value
                window_ref[window, c, :, columns] = value
    for c in range(4):
        near, far = new[c]
        plus = jnp.where(lanes < 64, roll_lanes(near[1], -32), roll_lanes(far[1], 32))
        minus = jnp.where(lanes < 64, near[0], roll_lanes(far[0], 64))
        put_pair(one_ref, two_ref, slice(c * ZR, (c + 1) * ZR), even_second, plus, minus)
    for pair in range(2):
        at = slice(96 + pair * ZR, 96 + (pair + 1) * ZR)
        even_c, odd_c = new[4 + 2 * pair], new[5 + 2 * pair]
        sides = []
        for half in (1, 0):
            sides.append(
                jnp.where(
                    lanes < 64,
                    jnp.where(lanes < 32, roll_lanes(even_c[0][half], -32), even_c[1][half]),
                    jnp.where(
                        lanes < 96, roll_lanes(odd_c[0][half], 32), roll_lanes(odd_c[1][half], 64)
                    ),
                )
            )
        put_pair(one_ref, two_ref, at, even_second, sides[0], sides[1])
    put_pair(
        one_ref, two_ref, slice(144, 184), even_second, bins_ref[0:40, :], bins_ref[40:80, :]
    )


def third_kernel(window_in, from_one, from_two, bins_ref, window_ref, message_ref):
    even = lax.axis_index("gy") % 2 == 1
    core = lax.axis_index("gz")
    lanes = lane_iota((ZR, 128))
    for window in range(2):
        for c in range(8):
            if c < 4:
                near, far = take_pair(from_one, from_two, slice(c * ZR, (c + 1) * ZR), even)
                near = jnp.where(
                    (lanes >= 32) & (lanes < 96),
                    roll_lanes(near, 32 if window == 0 else -32),
                    0.0,
                )
                far = jnp.where(lanes < 64, far if window == 0 else roll_lanes(far, 64), 0.0)
            else:
                at = slice(96 + (c - 4) // 2 * ZR, 96 + ((c - 4) // 2 + 1) * ZR)
                shift = (32, 0, -32, -64)[2 * (c % 2) + window]
                inside = (lanes >= 32) & (lanes < 64)
                near, far = take_pair(from_one, from_two, at, even)
                near = jnp.where(inside, roll_lanes(near, shift), 0.0)
                far = jnp.where(inside, roll_lanes(far, shift), 0.0)
            for half, extra in ((0, near), (1, far)):
                columns = slice(128 * half, 128 * half + 128)
                value = window_in[window, c, :, columns] + extra
                window_ref[window, c, :, columns] = value
                at = ((window * 8 + c) * 2 + half) * 8
                message_ref[at : at + 8, :] = jnp.where(core == 0, value[16:24], value[0:8])
    message_ref[256:296, :] = bins_ref[80:120, :]


def advance(sums):
    mass = jnp.maximum(sums[0], mass_floor)
    previous = [sums[1 + axis] / mass for axis in range(3)]
    velocity = [previous[0], previous[1], previous[2] - time_step * gravity]
    normal = sums[4:7]
    scale = 1.0 + (normal[0] * normal[0] + normal[1] * normal[1] + normal[2] * normal[2])
    dot = velocity[0] * normal[0] + velocity[1] * normal[1] + velocity[2] * normal[2]
    inward = jnp.minimum(dot, 0.0) / scale
    velocity = [velocity[axis] - inward * normal[axis] for axis in range(3)]
    dot = velocity[0] * normal[0] + velocity[1] * normal[1] + velocity[2] * normal[2]
    along = dot / scale
    damp = 1.0 - jnp.exp(-sums[7])
    velocity = [
        velocity[axis] - damp * (velocity[axis] - along * normal[axis]) for axis in range(3)
    ]
    return velocity + previous


def collect_kernel(
    window_in,
    from_z,
    x_one,
    x_two,
    y_one,
    y_two,
    plane_ref,
    weight_ref,
    state_ref,
    bin_count_ref,
    moved_ref,
    arrived_ref,
    data,
    fields,
    turned,
    table,
    picked,
    live,
    target,
    moved,
    arrived,
    semaphores,
):
    core = lax.axis_index("gz")
    row = lax.axis_index("gy")
    lanes = lane_iota((8, 128))
    subs = sub_iota((8, 128))
    lower_rows = subs < 4
    lower_lanes = lanes % 8 < 4

    even_first = lax.axis_index("gx") % 2 == 0
    even_second = lax.axis_index("gy") % 2 == 1
    arrivals = []
    for one_ref, two_ref, begin, even in ((x_one, x_two, 192, even_first), (y_one, y_two, 144, even_second)):
        pairs = [
            take_pair(one_ref, two_ref, slice(begin + 4 * part, begin + 4 * part + 4), even)
            for part in range(PARTS)
        ]
        arrivals += [[pair[0] for pair in pairs], [pair[1] for pair in pairs]]
    arrivals.append([from_z[256 + 4 * part : 260 + 4 * part, :] for part in range(PARTS)])
    for g, values in enumerate(arrivals):
        for part in range(7):
            data[part, 4 * g : 4 * g + 4, :] = values[part]
        slot = lane_iota((4, 128)).astype(f32)
        live[32 + 4 * g : 36 + 4 * g, :] = jnp.where(slot < values[7], 1.0, 0.0)
        block = values[8].astype(jnp.int32)
        for member in range(4):
            target[4 * g + member] = block[member, 0]

    below = core == 0
    above = core == 1
    taken = [
        jnp.logical_not(lower_rows) & above,
        (lower_rows & above) | (jnp.logical_not(lower_rows) & below),
        lower_rows & below,
    ]
    for third in range(3):
        rows = slice(8 * third, 8 * third + 8)
        for half in range(2):
            columns = slice(128 * half, 128 * half + 128)
            sums = [[], []]
            for c in range(8):
                values = [window_in[b, c, rows, columns] for b in range(2)]
                for b in range(2):
                    at = ((b * 8 + c) * 2 + half) * 8
                    edge = pltpu.roll(from_z[at : at + 8, :], 4, 0)
                    values[b] = values[b] + jnp.where(taken[third], edge, 0.0)
                sums[0].append(
                    values[0] + jnp.where(lower_lanes, 0.0, roll_lanes(values[1], 4))
                )
                sums[1].append(
                    values[1] + jnp.where(lower_lanes, roll_lanes(values[0], -4), 0.0)
                )
            node_second = row * 16 + (lanes + 128 * half) // 8 - 6
            node_third = core * 12 + subs + 8 * third - 2
            inside = (
                (node_second >= 0) & (node_second < 128) & (node_third >= 0) & (node_third < 32)
            )
            for b in range(2):
                for c, value in enumerate(advance(sums[b])):
                    fields[b, c, rows, columns] = jnp.where(inside, value, 0.0)

    wide = lane_iota((ZR, 128))
    local = wide % 64
    node_first = (local % 8).astype(f32) - 2.0 - center
    node_second = (local // 8).astype(f32) - 2.0 - center
    for b in range(2):
        for c in range(6):
            low = fields[b, c, :, 0:128]
            high = fields[b, c, :, 128:256]
            shown = [
                jnp.where(wide < 64, roll_lanes(low, -32), roll_lanes(low, 32)),
                jnp.where(wide < 64, roll_lanes(low, 64), low),
                jnp.where(
                    wide < 64,
                    jnp.where(wide < 32, roll_lanes(low, 32), roll_lanes(high, 32)),
                    jnp.where(wide < 96, roll_lanes(low, -32), roll_lanes(high, 96)),
                ),
                jnp.where(wide < 64, high, roll_lanes(high, 64)),
            ]
            for second in range(4):
                turned[second, :, c, :] = shown[second]
                if c < 3:
                    turned[second, :, 6 + c, :] = shown[second] * node_first
                    turned[second, :, 9 + c, :] = shown[second] * node_second
        for second in range(4):
            value = turned[second].reshape(ZR * 16, 128)
            high, low = parts(value)
            table[4 * b + second, :, 0:128] = high
            table[4 * b + second, :, 128:256] = low

    nodes = subs.astype(f32) - 2.0

    def one_bin(index, column, third, high, low, wz, lever):
        right = jnp.concatenate([high, low, high, low], axis=0)
        left = table[column, pl.ds(64 * third, 128), :]
        values = jnp.dot(left, right, preferred_element_type=f32)
        first = values[0:8] * wz[0:1]
        second = values[8:16] * wz[0:1]
        moment = values[0:8] * lever[0:1]
        for k in range(1, 8):
            first = first + values[16 * k : 16 * k + 8] * wz[k : k + 1]
            second = second + values[16 * k + 8 : 16 * k + 16] * wz[k : k + 1]
            moment = moment + values[16 * k : 16 * k + 8] * lever[k : k + 1]
        picked[0:8, index, :] = first
        picked[8:16, index, :] = second
        picked[16:24, index, :] = moment

    def residents(step, carry):
        first = step // 4
        second = step % 4
        for third in range(4):
            index = step * 4 + third
            high, low = plane_ref[index, 0:64, :], plane_ref[index, 64:128, :]
            wz, lever = weight_ref[index, 0:8, :], weight_ref[index, 8:16, :]
            one_bin(index, step, third + core, high, low, wz, lever)
            count = bin_count_ref[first, second, third]
            live[pl.ds(index, 1), :] = jnp.where(lane_iota((1, 128)) < count, 1.0, 0.0)
        return carry

    def movers(step, carry):
        for member in range(4):
            index = 4 * step + member
            block = target[index]
            terms = collect_terms([data[axis, pl.ds(index, 1), :] for axis in range(3)], nodes)
            one_bin(32 + index, block // 4, block % 4 + core, *terms)
        return carry

    lax.fori_loop(0, 5, movers, 0, unroll=5)

    def finish(begin, size, old):
        rows = slice(begin, begin + size)
        valid = live[rows, :]
        got = [picked[c, rows, :] for c in range(19)]
        result = []
        for axis in range(3):
            result.append(old[axis] + time_step * got[axis])
        for axis in range(3):
            result.append(
                flip_ratio * (old[3 + axis] + got[axis] - got[3 + axis])
                + (1.0 - flip_ratio) * got[axis]
            )
        affine = []
        for axis in range(3):
            affine.append(4.0 * (got[6 + axis] - (old[0] - center) * got[axis]))
            affine.append(4.0 * (got[9 + axis] - (old[1] - center) * got[axis]))
            affine.append(4.0 * got[16 + axis])
        result += affine
        result.append(old[6] * (1.0 + time_step * (affine[0] + affine[4] + affine[8])))
        return [value * valid for value in result]

    for g in range(3):
        begin, size = 8 * g, 8 if g < 2 else 4
        rows = slice(begin, begin + size)
        for c, value in enumerate(finish(32 + begin, size, [data[p, rows, :] for p in range(7)])):
            if g < 2:
                arrived[c, rows, :] = value
            else:
                arrived[c, 16:20, :] = jnp.where(core == 1, value, 0.0)
                arrived[c, 20:24, :] = jnp.where(core == 0, value, 0.0)
    arrived_copy = pltpu.make_async_copy(arrived, arrived_ref, semaphores.at[0])
    arrived_copy.start()
    moved_copies = []
    for part in range(2):
        lax.fori_loop(4 * part, 4 * part + 4, residents, 0, unroll=4)
        for g in range(2 * part, 2 * part + 2):
            rows = slice(8 * g, 8 * g + 8)
            for c, value in enumerate(finish(8 * g, 8, [state_ref[c, rows, :] for c in CARRIED])):
                moved[c, rows, :] = value
        where = (slice(None), pl.ds(16 * part, 16))
        moved_copies.append(
            pltpu.make_async_copy(moved.at[where], moved_ref.at[where], semaphores.at[1 + part])
        )
        moved_copies[-1].start()
    arrived_copy.wait()
    for copy in moved_copies:
        copy.wait()


def pairs_along(axis, first, closed):
    count = lax.axis_size(axis)
    route = [(i, (i + 1) % count) for i in range(first, count, 2) if closed or i + 1 < count]
    return route + [(j, i) for i, j in route]


vmem = pl.BlockSpec(memory_space=pltpu.VMEM)
smem = pl.BlockSpec(memory_space=pltpu.SMEM)
limits = pltpu.CompilerParams(vmem_limit_bytes=48 * 1024 * 1024)


def shape_of(*dims):
    return jax.ShapeDtypeStruct(dims, f32)


def body(
    state,
    bin_count,
    departing,
    depart_count,
    depart_block,
    cut_cell,
    quad_count,
    wall_id,
    cut_level,
    wall_normal,
    wall_friction,
):
    state_rows = state.reshape(16, 32, 128)
    leaving = departing.reshape(16, 24, 128)
    cut = [value.reshape(4, 128) for value in (cut_cell, quad_count, wall_id, cut_level)]
    depart_count = jnp.swapaxes(depart_count, 3, 4)
    depart_block = jnp.swapaxes(depart_block, 3, 4)
    operands = (
        state_rows,
        bin_count,
        leaving,
        depart_count,
        depart_block,
        *cut,
        wall_normal,
        wall_friction,
    )
    operands = tuple(pltpu.with_memory_space_constraint(value, pltpu.HBM) for value in operands)
    scalars = (1, 3, 4, 9, 10)
    window, one, two, bins = pl.pallas_call(
        deposit_kernel,
        out_shape=[
            shape_of(2, 8, ZR, LN),
            shape_of(XROWS, 128),
            shape_of(XROWS, 128),
            shape_of(3 * BINROWS, 128),
        ],
        in_specs=[pl.BlockSpec(memory_space=pltpu.HBM)] * 11,
        out_specs=[vmem] * 4,
        scratch_shapes=[
            (pltpu.SMEM if place in scalars else pltpu.VMEM)(value.shape, value.dtype)
            for place, value in enumerate(operands)
        ]
        + [
            pltpu.VMEM((16, 56, 128), f32),
            pltpu.VMEM((4, 6, 32, LN), f32),
            pltpu.SemaphoreType.DMA((11,)),
        ],
        compiler_params=limits,
        name="deposit",
    )(*operands)
    x_one = lax.ppermute(one, "gx", pairs_along("gx", 0, True))
    x_two = lax.ppermute(two, "gx", pairs_along("gx", 1, True))
    window, bins, planes, weights = pl.pallas_call(
        stage_kernel,
        out_shape=[
            shape_of(2, 8, ZR, LN),
            shape_of(3 * BINROWS, 128),
            jax.ShapeDtypeStruct((32, 128, 128), bf16),
            shape_of(32, 16, 128),
        ],
        in_specs=[vmem] * 3,
        out_specs=[vmem] * 4,
        cost_estimate=pl.CostEstimate(flops=10**9, bytes_accessed=2**20, transcendentals=0),
        compiler_params=limits,
        name="stage",
    )(window, bins, state_rows)
    window, one, two = pl.pallas_call(
        second_kernel,
        out_shape=[shape_of(2, 8, ZR, LN), shape_of(YROWS, 128), shape_of(YROWS, 128)],
        in_specs=[vmem] * 4,
        out_specs=[vmem] * 3,
        compiler_params=limits,
        name="take_x",
    )(window, x_one, x_two, bins)
    y_one = lax.ppermute(one, "gy", pairs_along("gy", 1, False))
    y_two = lax.ppermute(two, "gy", pairs_along("gy", 0, False))
    window, message = pl.pallas_call(
        third_kernel,
        out_shape=[shape_of(2, 8, ZR, LN), shape_of(ZROWS, 128)],
        in_specs=[vmem] * 4,
        out_specs=[vmem] * 2,
        compiler_params=limits,
        name="take_y",
    )(window, y_one, y_two, bins)
    from_z = lax.ppermute(message, "gz", [(0, 1), (1, 0)])
    moved, arrived = pl.pallas_call(
        collect_kernel,
        out_shape=[shape_of(16, 32, 128), shape_of(16, 24, 128)],
        in_specs=[vmem] * 9 + [smem],
        out_specs=[pl.BlockSpec(memory_space=pltpu.HBM)] * 2,
        scratch_shapes=[
            pltpu.VMEM((7, 24, 128), f32),
            pltpu.VMEM((2, 6, ZR, LN), f32),
            pltpu.VMEM((4, ZR, 16, 128), f32),
            pltpu.VMEM((8, ZR * 16, 256), bf16),
            pltpu.VMEM((24, 56, 128), f32),
            pltpu.VMEM((56, 128), f32),
            pltpu.SMEM((20,), jnp.int32),
            pltpu.VMEM((16, 32, 128), f32),
            pltpu.VMEM((16, 24, 128), f32),
            pltpu.SemaphoreType.DMA((3,)),
        ],
        compiler_params=limits,
        name="collect",
    )(
        window,
        from_z,
        x_one,
        x_two,
        y_one,
        y_two,
        planes,
        weights,
        state_rows,
        bin_count,
    )
    return moved.reshape(state.shape), arrived.reshape(departing.shape)


def solution(mesh):
    placed = (
        P(None, "gx", "gy", "gz", None),
        P("gx", "gy", "gz"),
        P(None, "gx", "gy", "gz", None, None, None),
        P("gx", "gy", "gz", None, None),
        P("gx", "gy", "gz", None, None),
        P("gx", "gy", "gz", None),
        P("gx", "gy", "gz", None),
        P("gx", "gy", "gz", None),
        P("gx", "gy", "gz", None),
        P(),
        P(),
    )
    return jax.shard_map(
        body,
        mesh=mesh,
        in_specs=placed,
        out_specs=(P(None, "gx", "gy", "gz", None), P(None, "gx", "gy", "gz", None, None, None)),
        check_vma=False,
    )
```
